32 devices in a mesh: gx: 4 (over z), gy: 8 (over y, x, core).
Axes of the slice: x: 2, y: 2, z: 4, core: 2. Of those that a mesh axis runs over, the one named last changes fastest.
Arguments:
- observed: bfloat16 [1024, 1024, 128], P('gx', 'gy'), may hold values from -6 to 6
- confidence: bfloat16 [1024, 1024, 128], P('gx', 'gy'), may hold values from 0.1 to 13
- iterate: float32 [1024, 1024, 128], P('gx', 'gy'), may hold values from -24 to 24
- kernel_bank: float32 [3, 64], replicated, may hold values from 0.02 to 1
- tap_index: int32 [3, 33], replicated, may hold values from 0 to 63
- offsets: int32 [3], replicated, may hold values from -4 to 4
- basis_x: bfloat16 [1024, 1024], P('gx'), may hold values from -0.1875 to 0.1875
- basis_y: bfloat16 [1024, 1024], P('gy'), may hold values from -0.1875 to 0.1875
- basis_z: bfloat16 [128, 128], replicated, may hold values from -0.5 to 0.5
- eigen_x: float32 [1024], P('gx'), may hold values from 0.1 to 1
- eigen_y: float32 [1024], replicated, may hold values from 0.1 to 1
- eigen_z: float32 [128], replicated, may hold values from 0.1 to 1
Outputs:
- updated: float32 [1024, 1024, 128], P('gx', 'gy')
- residual: float32 [1024, 1024, 128], P('gx', 'gy')
The draws below stay inside these ranges and needn't reach their ends.
All inputs are finite; a program needn't handle non-finite values.
Results may differ from the reference program's by a relative error of at most 0.0028.
Values may be sent and summed in bfloat16 or wider, within the bound.
A program may use at most 256 MiB of HBM per device.

```python
import math
import jax
import jax.numpy as jnp
from jax import lax

NX = 1024
NY = 1024
NZ = 128
HALF = 16
SHIFT = 4
BANK = 64
TAPS = 33


def draw_confidence(key, part):
    sub_key = jax.random.fold_in(key, 11)
    x_frac = (jnp.arange(NX, dtype=jnp.float32) / NX)[:, None, None]
    y_frac = (jnp.arange(NY, dtype=jnp.float32) / NY)[None, :, None]
    baseline = jnp.exp(jax.random.uniform(sub_key, (NX, NY, NZ), jnp.float32, jnp.log(0.1), 0.0))
    slope = 2.0
    growth = (1.0 + slope * x_frac) * (1.0 + slope * y_frac)
    return (baseline * growth).astype(jnp.bfloat16)


def draw_offsets(key, part):
    shuffle = jax.random.permutation(jax.random.fold_in(key, 5), 3)
    baseline = jax.random.randint(jax.random.fold_in(key, 7), (3,), -SHIFT, SHIFT + 1)
    axis_ids = jnp.arange(3, dtype=jnp.int32)
    chosen = jnp.where(axis_ids == shuffle[1], -SHIFT, baseline)
    return jnp.where(axis_ids == shuffle[0], SHIFT, chosen).astype(jnp.int32)


def place_ends(drawn, stream_key, least, top_value):
    extent = drawn.shape
    spot = [jax.random.randint(jax.random.fold_in(stream_key, axis), (), 0, extent[axis]) for axis in range(len(extent))]
    drawn = drawn.at[tuple(spot)].set(least)
    longest = extent.index(max(extent))
    spot[longest] = (spot[longest] + 1) % extent[longest]
    return drawn.at[tuple(spot)].set(top_value)


def levels(stream_key, dims, split, low, largest):
    loudness = 1.0
    for position, blocks in split:
        steps = jax.random.uniform(jax.random.fold_in(jax.random.fold_in(stream_key, 6), position), (blocks,), jnp.float32, low / len(split), largest / len(split))
        loudness = loudness * jnp.repeat(jnp.exp(steps), dims[position] // blocks).reshape((-1,) + (1,) * (len(dims) - 1 - position))
    return loudness


def normal_values(rng, dims, width, reach, pieces=(), held_as=jnp.bfloat16):
    result = width * jax.random.normal(rng, dims, jnp.float32)
    if pieces:
        result = result * levels(rng, dims, pieces, -0.22, 0.18)
    return jnp.clip(result, -reach, reach).astype(held_as)


def setup_inputs(seed: int = 0) -> dict:
    splits = jax.random.split(jax.random.key(seed), 13)
    observed = normal_values(splits[0], (NX, NY, NZ), 1.0, 6.0, ((0, 4), (1, 8)))
    confidence = draw_confidence(jax.random.fold_in(splits[12], 71), 0)
    iterate = normal_values(splits[2], (NX, NY, NZ), 4.0, 24.0, ((0, 4), (1, 8)), jnp.float32)
    kernel_bank = jnp.clip(jnp.exp(jax.random.uniform(splits[3], (3, BANK), jnp.float32, math.log(0.02), math.log(1.0))), 0.02, 1.0)
    tap_index = place_ends(jax.random.randint(splits[4], (3, TAPS), 0, BANK), jax.random.fold_in(splits[4], 1), 0, BANK - 1).astype(jnp.int32)
    offsets = draw_offsets(jax.random.fold_in(splits[12], 71), 0)
    basis_x = normal_values(splits[6], (NX, NX), NX ** -0.5, 0.1875, ((0, 4),))
    basis_y = normal_values(splits[7], (NY, NY), NY ** -0.5, 0.1875, ((0, 8),))
    basis_z = normal_values(splits[8], (NZ, NZ), NZ ** -0.5, 0.5)
    eigen_x = jnp.clip(jnp.exp(math.log(1.0) - 2.3025851 * jax.random.uniform(splits[9], (NX,), jnp.float32) ** levels(splits[9], (NX,), ((0, 4),), -0.2, 0.2)), 0.1, 1.0)
    eigen_y = jnp.clip(jnp.exp(jax.random.uniform(splits[10], (NY,), jnp.float32, math.log(0.1), math.log(1.0))), 0.1, 1.0)
    eigen_z = jnp.clip(jnp.exp(jax.random.uniform(splits[11], (NZ,), jnp.float32, math.log(0.1), math.log(1.0))), 0.1, 1.0)
    return {"observed": observed, "confidence": confidence, "iterate": iterate, "kernel_bank": kernel_bank, "tap_index": tap_index, "offsets": offsets, "basis_x": basis_x, "basis_y": basis_y, "basis_z": basis_z, "eigen_x": eigen_x, "eigen_y": eigen_y, "eigen_z": eigen_z}


highest = lax.Precision.HIGHEST
tikhonov = 0.002


def kernels_of(kernel_bank, tap_index):
    raw_taps = jnp.take_along_axis(kernel_bank, tap_index, axis=1)
    return raw_taps / jnp.sum(raw_taps, axis=1, keepdims=True)


def shift_blur(source, kernel, offset, axis_pos):
    rim_width = HALF + SHIFT
    pad_spec = [(0, 0), (0, 0), (0, 0)]
    pad_spec[axis_pos] = (rim_width, rim_width)
    padded = jnp.pad(source, pad_spec)
    length = source.shape[axis_pos]
    accum = jnp.zeros_like(source)
    for tap_pos in range(2 * HALF + 1):
        begin_at = (offset + (rim_width + tap_pos - HALF)).astype(jnp.int32)
        accum = accum + kernel[tap_pos] * lax.dynamic_slice_in_dim(padded, begin_at, length, axis_pos)
    return accum


def blur_all(source, kernels, offsets):
    along_z = shift_blur(source, kernels[2], offsets[2], 2)
    along_x = shift_blur(along_z, kernels[0], offsets[0], 0)
    return shift_blur(along_x, kernels[1], offsets[1], 1)


def precondition(gradient, basis_x, basis_y, basis_z, eigen_x, eigen_y, eigen_z):
    basis_xf = basis_x.astype(jnp.float32)
    basis_yf = basis_y.astype(jnp.float32)
    basis_zf = basis_z.astype(jnp.float32)
    gradient_b = gradient.astype(jnp.bfloat16).astype(jnp.float32)
    section_one = jnp.einsum('xyz,zk->xyk', gradient_b, basis_zf, precision=highest).astype(jnp.bfloat16)
    section_two = jnp.einsum('xyz,xk->kyz', section_one.astype(jnp.float32), basis_xf, precision=highest).astype(jnp.bfloat16)
    section_three = jnp.einsum('xyz,yk->xkz', section_two.astype(jnp.float32), basis_yf, precision=highest)
    inverse = 1.0 / (eigen_x[:, None, None] * eigen_y[None, :, None] * eigen_z[None, None, :] + tikhonov)
    section_four = (section_three * inverse).astype(jnp.bfloat16)
    section_five = jnp.einsum('xkz,jk->xjz', section_four.astype(jnp.float32), basis_yf, precision=highest).astype(jnp.bfloat16)
    section_six = jnp.einsum('kyz,jk->jyz', section_five.astype(jnp.float32), basis_xf, precision=highest).astype(jnp.bfloat16)
    return jnp.einsum('xyk,zk->xyz', section_six.astype(jnp.float32), basis_zf, precision=highest)


def reference(observed, confidence, iterate, kernel_bank, tap_index, offsets, basis_x, basis_y, basis_z, eigen_x, eigen_y, eigen_z):
    kernels = kernels_of(kernel_bank, tap_index)
    weights = confidence.astype(jnp.float32)
    misfit = observed.astype(jnp.float32) - blur_all(iterate, kernels, offsets)
    gradient = blur_all(weights * misfit, kernels[:, ::-1], -offsets) - tikhonov * iterate
    direction = precondition(gradient, basis_x, basis_y, basis_z, eigen_x, eigen_y, eigen_z)
    descent = jnp.sum(gradient * direction)
    blurred = blur_all(direction, kernels, offsets)
    energy = jnp.sum(weights * blurred * blurred) + tikhonov * jnp.sum(direction * direction)
    step_size = descent / energy
    return iterate + step_size * direction, misfit - step_size * blurred
```

```python
import functools

import jax
import jax.numpy as jnp
from jax import lax
from jax.experimental import pallas as pl
from jax.experimental.pallas import tpu as pltpu
from jax.sharding import PartitionSpec as P

HALF = 16
SHIFT = 4
CHUNKS = 2


highest = lax.Precision.HIGHEST
tikhonov = 0.002


def exchange(block, axis, dim, width):
    count = lax.axis_size(axis)
    forward = [(i, i + 1) for i in range(count - 1)]
    backward = [(target, source) for source, target in forward]
    low = lax.ppermute(
        lax.slice_in_dim(block, block.shape[dim] - width, None, axis=dim), axis, forward
    )
    high = lax.ppermute(lax.slice_in_dim(block, 0, width, axis=dim), axis, backward)
    return low, high


def kernels_of(kernel_bank, tap_index):
    entries = jnp.arange(kernel_bank.shape[1], dtype=jnp.int32)
    chosen = tap_index[:, :, None] == entries[None, None, :]
    raw_taps = jnp.sum(jnp.where(chosen, kernel_bank[:, None, :], 0.0), axis=2)
    return raw_taps / jnp.sum(raw_taps, axis=1, keepdims=True)


def band_matrix(kernel, offset, out_count, in_count, margin):
    center = (kernel.shape[0] - 1) // 2
    row_pos = lax.broadcasted_iota(jnp.int32, (out_count, in_count), 0)
    col_pos = lax.broadcasted_iota(jnp.int32, (out_count, in_count), 1)
    position = col_pos - row_pos - margin + center - offset
    tap_ids = jnp.arange(kernel.shape[0], dtype=jnp.int32)
    chosen = position[None, :, :] == tap_ids[:, None, None]
    return jnp.sum(jnp.where(chosen, kernel[:, None, None], 0.0), axis=0)


def split_dot(spec, matrix, block):
    return jnp.einsum(spec, matrix, block.astype(jnp.float32), precision=lax.Precision.HIGH)


def turned(array, axis_name, dim, sign):
    count = lax.axis_size(axis_name)
    size = array.shape[dim] // count
    mine = lax.axis_index(axis_name)
    pieces = [
        lax.dynamic_slice_in_dim(array, lax.rem(mine + sign * step + count, count) * size, size, dim)
        for step in range(count)
    ]
    return jnp.concatenate(pieces, axis=dim)


def swap(block, axis_name, split, concat, sign):
    count = lax.axis_size(axis_name)
    pieces = jnp.split(block, count, axis=split)
    arrived = [pieces[0]]
    for step in range(1, count):
        pairs = [(i, (i + sign * step) % count) for i in range(count)]
        arrived.append(lax.ppermute(pieces[step], axis_name, pairs))
    return jnp.concatenate(arrived, axis=concat)


def blur_xy(along_z, kernels, offsets):
    rim = HALF + SHIFT
    block_x, block_y, _ = along_z.shape
    x_matrix = band_matrix(kernels[0], offsets[0], block_x, block_x + 2 * rim, rim)
    y_matrix = band_matrix(kernels[1], offsets[1], block_y, block_y + 2 * rim, rim)
    low, high = exchange(along_z, "gx", 0, rim)
    extended = jnp.concatenate([low, along_z, high], axis=0)
    along_x = split_dot("ic,cyz->iyz", x_matrix, extended).astype(jnp.bfloat16)
    low, high = exchange(along_x, "gy", 1, rim)
    inner = split_dot("jc,xcz->xjz", y_matrix[:, rim:-rim], along_x)
    rims = jnp.concatenate([low, high], axis=1)
    rim_matrix = jnp.concatenate([y_matrix[:, :rim], y_matrix[:, -rim:]], axis=1)
    return inner + split_dot("jc,xcz->xjz", rim_matrix, rims)


def apply_blur(source, kernels, offsets):
    depth = source.shape[2]
    z_matrix = band_matrix(kernels[2], offsets[2], depth, depth, 0)
    along_z = jnp.einsum("xyc,zc->xyz", source, z_matrix, precision=lax.Precision.HIGH)
    return blur_xy(along_z.astype(jnp.bfloat16), kernels, offsets)


MESH_ID = pl.DeviceIdType.MESH
PARTS = 4


def transform_kernel(
    parts, size_x, size_y,
    section_ref, x_fwd, x_inv, y_fwd, y_inv, eigen_xy, eigen_z,
    out_ref,
    lines_x, lines_y, lines_back, send_a, send_b, send_c, modes,
    fs, fr, gs, gr, hs, hr, bs, br, fl, gl, hl, bl,
):
    me_x = lax.axis_index("gx")
    me_y = lax.axis_index("gy")
    depth = lines_x.shape[0]
    full = lines_x.shape[1]
    block_y = lines_x.shape[2]
    block_x = section_ref.shape[1]
    share = lines_y.shape[1]
    full_y = lines_y.shape[2]
    part = depth // parts
    slots = send_a.shape[0]

    barrier = pltpu.get_barrier_semaphore()
    for step in range(1, size_x):
        pl.semaphore_signal(
            barrier, inc=1, device_id=(lax.rem(me_x + step, size_x), me_y), device_id_type=MESH_ID
        )
    for step in range(1, size_y):
        pl.semaphore_signal(
            barrier, inc=1, device_id=(me_x, lax.rem(me_y + step, size_y)), device_id_type=MESH_ID
        )
    pl.semaphore_wait(barrier, size_x + size_y - 2)

    def copies(kind, c):
        out = []
        here = pl.ds(c * part, part)
        slot = c % slots
        count = size_x if kind in "fb" else size_y
        for step in range(count):
            mine = step == 0
            if kind in "fb":
                peer = lax.rem(me_x + step, size_x)
                target = (peer, me_y)
            else:
                peer = lax.rem(me_y + step, size_y)
                target = (me_x, peer)
            if kind == "f":
                src = section_ref.at[pl.ds(peer * depth + c * part, part)]
                dst = lines_x.at[here, pl.ds(me_x * block_x, block_x)]
                sems = fs, fr, fl
            elif kind == "g":
                src = send_a.at[slot, :, pl.ds(peer * share, share)]
                dst = lines_y.at[here, :, pl.ds(me_y * block_y, block_y)]
                sems = gs, gr, gl
            elif kind == "h":
                src = send_b.at[slot, :, :, pl.ds(peer * block_y, block_y)]
                dst = lines_back.at[here, pl.ds(me_y * share, share)]
                sems = hs, hr, hl
            else:
                src = send_c.at[slot, :, pl.ds(peer * block_x, block_x)]
                dst = out_ref.at[pl.ds(me_x * depth + c * part, part)]
                sems = bs, br, bl
            if mine:
                out.append(pltpu.make_async_copy(src, dst, sems[2].at[c]))
            else:
                out.append(
                    pltpu.make_async_remote_copy(
                        src, dst, sems[0].at[c, step], sems[1].at[c, step],
                        device_id=target, device_id_type=MESH_ID,
                    )
                )
        return out

    every = {kind: [copies(kind, c) for c in range(parts)] for kind in "fghb"}

    def start(kind, c):
        group = every[kind][c]
        for copy in group[1:] + group[:1]:
            copy.start()

    def landed(kind, c):
        group = every[kind][c]
        if kind != "b":
            group[0].wait()
        for copy in group[1:]:
            copy.wait_recv()

    def sent(kind, c):
        group = every[kind][c]
        if kind == "b":
            group[0].wait()
        for copy in group[1:]:
            copy.wait_send()

    def along_x(matrix, lines, out, c):
        def pair(i, carry):
            k = c * part + 2 * i
            both = jnp.concatenate([lines[k], lines[k + 1]], axis=1)
            for b in range(0, full, 256):
                found = jnp.dot(
                    matrix[pl.ds(b, 256), :], both, preferred_element_type=jnp.float32
                ).astype(jnp.bfloat16)
                out[c % slots, 2 * i, pl.ds(b, 256)] = found[:, :block_y]
                out[c % slots, 2 * i + 1, pl.ds(b, 256)] = found[:, block_y:]
            return carry

        lax.fori_loop(0, part // 2, pair, 0)

    def along_y(c):
        def pair(i, carry):
            k = c * part + 2 * i
            rows = jnp.concatenate([lines_y[k], lines_y[k + 1]], axis=0)
            for b in range(0, full_y, 256):
                found = jnp.dot(rows, y_fwd[:, pl.ds(b, 256)], preferred_element_type=jnp.float32)
                weight = eigen_xy[:, pl.ds(b, 256)]
                modes[pl.ds(0, share), pl.ds(b, 256)] = (
                    found[:share] / (weight * eigen_z[k] + tikhonov)
                ).astype(jnp.bfloat16)
                modes[pl.ds(share, share), pl.ds(b, 256)] = (
                    found[share:] / (weight * eigen_z[k + 1] + tikhonov)
                ).astype(jnp.bfloat16)
            for b in range(0, full_y, 256):
                found = jnp.dot(
                    modes[...], y_inv[:, pl.ds(b, 256)], preferred_element_type=jnp.float32
                ).astype(jnp.bfloat16)
                send_b[c % slots, 2 * i, :, pl.ds(b, 256)] = found[:share]
                send_b[c % slots, 2 * i + 1, :, pl.ds(b, 256)] = found[share:]
            return carry

        lax.fori_loop(0, part // 2, pair, 0)

    ahead = min(2, parts)
    for c in range(ahead):
        start("f", c)
    for step in range(parts + 2):
        c = step
        if c < parts:
            landed("f", c)
            if c + ahead < parts:
                start("f", c + ahead)
            if c >= slots:
                sent("g", c - slots)
            along_x(x_fwd, lines_x, send_a, c)
            start("g", c)
        c = step - 1
        if 0 <= c < parts:
            landed("g", c)
            if c >= slots:
                sent("h", c - slots)
            along_y(c)
            start("h", c)
        c = step - 2
        if 0 <= c < parts:
            landed("h", c)
            if c >= slots:
                sent("b", c - slots)
            along_x(x_inv, lines_back, send_c, c)
            start("b", c)
    for c in range(parts):
        landed("b", c)
        sent("f", c)
        if c >= parts - slots:
            sent("g", c)
            sent("h", c)
            sent("b", c)


def transform(section, x_fwd, x_inv, y_fwd, y_inv, eigen_xy, eigen_z, size_x, size_y):
    modes_z, block_x, block_y = section.shape
    depth = modes_z // size_x
    full_x, full_y = x_fwd.shape[0], y_fwd.shape[0]
    share = full_x // size_y
    parts = PARTS
    part = depth // parts
    slots = 2
    vmem = pl.BlockSpec(memory_space=pltpu.VMEM)
    sem = lambda n: pltpu.SemaphoreType.DMA((parts, n))
    one = pltpu.SemaphoreType.DMA((parts,))
    bf = jnp.bfloat16
    return pl.pallas_call(
        functools.partial(transform_kernel, parts, size_x, size_y),
        out_shape=jax.ShapeDtypeStruct(section.shape, bf),
        in_specs=[pl.BlockSpec(memory_space=pl.ANY)] + [vmem] * 5
        + [pl.BlockSpec(memory_space=pltpu.SMEM)],
        out_specs=pl.BlockSpec(memory_space=pl.ANY),
        scratch_shapes=[
            pltpu.VMEM((depth, full_x, block_y), bf),
            pltpu.VMEM((depth, share, full_y), bf),
            pltpu.VMEM((depth, full_x, block_y), bf),
            pltpu.VMEM((slots, part, full_x, block_y), bf),
            pltpu.VMEM((slots, part, share, full_y), bf),
            pltpu.VMEM((slots, part, full_x, block_y), bf),
            pltpu.VMEM((2 * share, full_y), bf),
            sem(size_x), sem(size_x), sem(size_y), sem(size_y),
            sem(size_y), sem(size_y), sem(size_x), sem(size_x),
            one, one, one, one,
        ],
        compiler_params=pltpu.CompilerParams(
            collective_id=0, has_side_effects=True, vmem_limit_bytes=60 * 2**20
        ),
    )(section, x_fwd, x_inv, y_fwd, y_inv, eigen_xy, eigen_z)


def modes_by_permutes(gradient_b, full_x, full_y, basis_z, eigen_x, eigen_y, eigen_z):
    gx_size = lax.axis_size("gx")
    depth = basis_z.shape[0]
    share_z = depth // gx_size
    chunks = min(CHUNKS, share_z)
    part = share_z // chunks
    z_ahead = turned(basis_z, "gx", 1, 1).reshape(depth, gx_size, chunks, part)
    eigen_part = lax.dynamic_slice_in_dim(eigen_z, lax.axis_index("gx") * share_z, share_z)
    all_x = lax.all_gather(eigen_x, "gx", axis=0, tiled=True)
    share_x = all_x.shape[0] // lax.axis_size("gy")
    part_x = lax.dynamic_slice_in_dim(all_x, lax.axis_index("gy") * share_x, share_x)
    x_rows_behind = turned(full_x, "gx", 0, -1)
    x_ahead = turned(x_rows_behind, "gy", 1, 1)
    x_return = turned(turned(full_x, "gx", 0, 1), "gy", 1, -1)
    y_behind = turned(full_y, "gy", 0, -1)
    y_ahead = turned(full_y, "gy", 0, 1)
    found = []
    for chunk in range(chunks):
        modes = z_ahead[:, :, chunk].reshape(depth, gx_size * part)
        section_one = jnp.einsum(
            "zk,xyz->kxy", modes, gradient_b, preferred_element_type=jnp.float32
        ).astype(jnp.bfloat16)
        lines = swap(section_one, "gx", 0, 1, 1)
        section_two = jnp.einsum(
            "xj,kxy->kjy", x_ahead, lines, preferred_element_type=jnp.float32
        ).astype(jnp.bfloat16)
        lines = swap(section_two, "gy", 1, 2, 1)
        part_z = eigen_part[chunk * part : (chunk + 1) * part]
        inverse = 1.0 / (
            part_x[None, :, None] * eigen_y[None, None, :] * part_z[:, None, None] + tikhonov
        )
        section_four = (
            jnp.einsum("axy,yk->axk", lines, y_behind, preferred_element_type=jnp.float32)
            * inverse
        ).astype(jnp.bfloat16)
        section_five = jnp.einsum(
            "axk,jk->axj", section_four, y_ahead, preferred_element_type=jnp.float32
        ).astype(jnp.bfloat16)
        lines = swap(section_five, "gy", 2, 1, 1)
        section_six = jnp.einsum(
            "jx,kxy->kjy", x_return, lines, preferred_element_type=jnp.float32
        ).astype(jnp.bfloat16)
        found.append(swap(section_six, "gx", 1, 0, 1))
    section_six = jnp.concatenate(found, axis=0)
    basis_z = (
        turned(basis_z, "gx", 1, -1)
        .reshape(depth, gx_size, chunks, part)
        .transpose(0, 2, 1, 3)
        .reshape(depth, depth)
    )
    return section_six, basis_z


def kernel_fits(block, size_x, size_y):
    block_x, block_y, depth = block
    return (
        block_y == 128
        and depth == 128
        and block_x % 128 == 0
        and depth // size_x % (2 * PARTS) == 0
        and block_x * size_x // size_y == 128
        and block_y * size_y % 256 == 0
    )


def modes_by_kernel(gradient_b, full_x, full_y, basis_z, eigen_x, eigen_y, eigen_z):
    size_x, size_y = lax.axis_size("gx"), lax.axis_size("gy")
    section_one = jnp.einsum(
        "zk,xyz->kxy", basis_z, gradient_b, preferred_element_type=jnp.float32
    ).astype(jnp.bfloat16)
    all_x = lax.all_gather(eigen_x, "gx", axis=0, tiled=True)
    share_x = all_x.shape[0] // size_y
    part_x = lax.dynamic_slice_in_dim(all_x, lax.axis_index("gy") * share_x, share_x)
    share_z = eigen_z.shape[0] // size_x
    part_z = lax.dynamic_slice_in_dim(eigen_z, lax.axis_index("gx") * share_z, share_z)
    section_six = transform(
        section_one, full_x.T, full_x, full_y, full_y.T,
        part_x[:, None] * eigen_y[None, :], part_z, size_x, size_y,
    )
    return section_six, basis_z


def shards(
    observed,
    confidence,
    iterate,
    kernel_bank,
    tap_index,
    offsets,
    basis_x,
    basis_y,
    basis_z,
    eigen_x,
    eigen_y,
    eigen_z,
):
    kernels = kernels_of(kernel_bank, tap_index)
    adjoint_kernels = kernels[:, ::-1]
    weights = confidence.astype(jnp.float32)
    misfit = observed.astype(jnp.float32) - apply_blur(iterate, kernels, offsets)
    gradient = apply_blur(weights * misfit, adjoint_kernels, -offsets) - tikhonov * iterate
    full_x = lax.all_gather(basis_x, "gx", axis=0, tiled=True)
    full_y = lax.all_gather(basis_y, "gy", axis=0, tiled=True)

    gradient_b = gradient.astype(jnp.bfloat16)
    fits = kernel_fits(gradient.shape, lax.axis_size("gx"), lax.axis_size("gy"))
    find_modes = modes_by_kernel if fits else modes_by_permutes
    section_six, basis_z = find_modes(
        gradient_b, full_x, full_y, basis_z, eigen_x, eigen_y, eigen_z
    )
    depth = basis_z.shape[0]
    direction = jnp.einsum("kxy,zk->xyz", section_six, basis_z, preferred_element_type=jnp.float32)
    z_matrix = band_matrix(kernels[2], offsets[2], depth, depth, 0)
    z_modes = jnp.dot(z_matrix, basis_z.astype(jnp.float32), precision=highest)
    along_z = jnp.einsum(
        "kxy,zk->xyz", section_six.astype(jnp.float32), z_modes, precision=lax.Precision.HIGH
    ).astype(jnp.bfloat16)
    local_descent = jnp.sum(gradient * direction)
    descent = lax.psum(local_descent, ("gx", "gy"))
    blurred = blur_xy(along_z, kernels, offsets)
    data_sum, norm_sum = lax.psum(
        (jnp.sum(weights * blurred * blurred), jnp.sum(direction * direction)), ("gx", "gy")
    )
    energy = data_sum + tikhonov * norm_sum
    step_size = descent / energy
    return (iterate + step_size * direction, misfit - step_size * blurred)


def solution(mesh):
    return jax.shard_map(
        shards,
        mesh=mesh,
        in_specs=(
            P("gx", "gy", None),
            P("gx", "gy", None),
            P("gx", "gy", None),
            P(),
            P(),
            P(),
            P("gx", None),
            P("gy", None),
            P(),
            P("gx"),
            P(),
            P(),
        ),
        out_specs=(P("gx", "gy", None), P("gx", "gy", None)),
        check_vma=False,
    )
```

```python
import functools

import jax
import jax.numpy as jnp
from jax import lax
from jax.experimental import pallas as pl
from jax.experimental.pallas import tpu as pltpu
from jax.sharding import PartitionSpec as P

HALF = 16
SHIFT = 4
CHUNKS = 2


highest = lax.Precision.HIGHEST
tikhonov = 0.002


def exchange(block, axis, dim, width):
    count = lax.axis_size(axis)
    forward = [(i, i + 1) for i in range(count - 1)]
    backward = [(target, source) for source, target in forward]
    low = lax.ppermute(
        lax.slice_in_dim(block, block.shape[dim] - width, None, axis=dim), axis, forward
    )
    high = lax.ppermute(lax.slice_in_dim(block, 0, width, axis=dim), axis, backward)
    return low, high


def kernels_of(kernel_bank, tap_index):
    entries = jnp.arange(kernel_bank.shape[1], dtype=jnp.int32)
    chosen = tap_index[:, :, None] == entries[None, None, :]
    raw_taps = jnp.sum(jnp.where(chosen, kernel_bank[:, None, :], 0.0), axis=2)
    return raw_taps / jnp.sum(raw_taps, axis=1, keepdims=True)


def band_matrix(kernel, offset, out_count, in_count, margin):
    center = (kernel.shape[0] - 1) // 2
    row_pos = lax.broadcasted_iota(jnp.int32, (out_count, in_count), 0)
    col_pos = lax.broadcasted_iota(jnp.int32, (out_count, in_count), 1)
    position = col_pos - row_pos - margin + center - offset
    tap_ids = jnp.arange(kernel.shape[0], dtype=jnp.int32)
    chosen = position[None, :, :] == tap_ids[:, None, None]
    return jnp.sum(jnp.where(chosen, kernel[:, None, None], 0.0), axis=0)


def split_dot(spec, matrix, block):
    return jnp.einsum(spec, matrix, block.astype(jnp.float32), precision=lax.Precision.HIGH)


def turned(array, axis_name, dim, sign):
    count = lax.axis_size(axis_name)
    size = array.shape[dim] // count
    mine = lax.axis_index(axis_name)
    pieces = [
        lax.dynamic_slice_in_dim(array, lax.rem(mine + sign * step + count, count) * size, size, dim)
        for step in range(count)
    ]
    return jnp.concatenate(pieces, axis=dim)


def swap(block, axis_name, split, concat, sign):
    count = lax.axis_size(axis_name)
    pieces = jnp.split(block, count, axis=split)
    arrived = [pieces[0]]
    for step in range(1, count):
        pairs = [(i, (i + sign * step) % count) for i in range(count)]
        arrived.append(lax.ppermute(pieces[step], axis_name, pairs))
    return jnp.concatenate(arrived, axis=concat)


def blur_xy(along_z, kernels, offsets):
    rim = HALF + SHIFT
    block_x, block_y, _ = along_z.shape
    x_matrix = band_matrix(kernels[0], offsets[0], block_x, block_x + 2 * rim, rim)
    y_matrix = band_matrix(kernels[1], offsets[1], block_y, block_y + 2 * rim, rim)
    low, high = exchange(along_z, "gx", 0, rim)
    extended = jnp.concatenate([low, along_z, high], axis=0)
    along_x = split_dot("ic,cyz->iyz", x_matrix, extended).astype(jnp.bfloat16)
    low, high = exchange(along_x, "gy", 1, rim)
    inner = split_dot("jc,xcz->xjz", y_matrix[:, rim:-rim], along_x)
    rims = jnp.concatenate([low, high], axis=1)
    rim_matrix = jnp.concatenate([y_matrix[:, :rim], y_matrix[:, -rim:]], axis=1)
    return inner + split_dot("jc,xcz->xjz", rim_matrix, rims)


def apply_blur(source, kernels, offsets):
    depth = source.shape[2]
    z_matrix = band_matrix(kernels[2], offsets[2], depth, depth, 0)
    along_z = jnp.einsum("xyc,zc->xyz", source, z_matrix, precision=lax.Precision.HIGH)
    return blur_xy(along_z.astype(jnp.bfloat16), kernels, offsets)


def shards(
    observed,
    confidence,
    iterate,
    kernel_bank,
    tap_index,
    offsets,
    basis_x,
    basis_y,
    basis_z,
    eigen_x,
    eigen_y,
    eigen_z,
):
    kernels = kernels_of(kernel_bank, tap_index)
    adjoint_kernels = kernels[:, ::-1]
    weights = confidence.astype(jnp.float32)
    misfit = observed.astype(jnp.float32) - apply_blur(iterate, kernels, offsets)
    gradient = apply_blur(weights * misfit, adjoint_kernels, -offsets) - tikhonov * iterate
    full_x = lax.all_gather(basis_x, "gx", axis=0, tiled=True)
    full_y = lax.all_gather(basis_y, "gy", axis=0, tiled=True)

    gradient_b = gradient.astype(jnp.bfloat16)
    gx_size = lax.axis_size("gx")
    depth = basis_z.shape[0]
    share_z = depth // gx_size
    chunks = min(CHUNKS, share_z)
    part = share_z // chunks
    z_ahead = turned(basis_z, "gx", 1, 1).reshape(depth, gx_size, chunks, part)
    eigen_part = lax.dynamic_slice_in_dim(eigen_z, lax.axis_index("gx") * share_z, share_z)
    all_x = lax.all_gather(eigen_x, "gx", axis=0, tiled=True)
    share_x = all_x.shape[0] // lax.axis_size("gy")
    part_x = lax.dynamic_slice_in_dim(all_x, lax.axis_index("gy") * share_x, share_x)
    x_rows_behind = turned(full_x, "gx", 0, -1)
    x_ahead = turned(x_rows_behind, "gy", 1, 1)
    x_return = turned(turned(full_x, "gx", 0, 1), "gy", 1, -1)
    y_behind = turned(full_y, "gy", 0, -1)
    y_ahead = turned(full_y, "gy", 0, 1)
    found = []
    for chunk in range(chunks):
        modes = z_ahead[:, :, chunk].reshape(depth, gx_size * part)
        section_one = jnp.einsum(
            "zk,xyz->kxy", modes, gradient_b, preferred_element_type=jnp.float32
        ).astype(jnp.bfloat16)
        lines = swap(section_one, "gx", 0, 1, 1)
        section_two = jnp.einsum(
            "xj,kxy->kjy", x_ahead, lines, preferred_element_type=jnp.float32
        ).astype(jnp.bfloat16)
        lines = swap(section_two, "gy", 1, 2, 1)
        part_z = eigen_part[chunk * part : (chunk + 1) * part]
        inverse = 1.0 / (
            part_x[None, :, None] * eigen_y[None, None, :] * part_z[:, None, None] + tikhonov
        )
        section_four = (
            jnp.einsum("axy,yk->axk", lines, y_behind, preferred_element_type=jnp.float32)
            * inverse
        ).astype(jnp.bfloat16)
        section_five = jnp.einsum(
            "axk,jk->axj", section_four, y_ahead, preferred_element_type=jnp.float32
        ).astype(jnp.bfloat16)
        lines = swap(section_five, "gy", 2, 1, 1)
        section_six = jnp.einsum(
            "jx,kxy->kjy", x_return, lines, preferred_element_type=jnp.float32
        ).astype(jnp.bfloat16)
        found.append(swap(section_six, "gx", 1, 0, 1))
    section_six = jnp.concatenate(found, axis=0)
    basis_z = (
        turned(basis_z, "gx", 1, -1)
        .reshape(depth, gx_size, chunks, part)
        .transpose(0, 2, 1, 3)
        .reshape(depth, depth)
    )
    direction = jnp.einsum("kxy,zk->xyz", section_six, basis_z, preferred_element_type=jnp.float32)
    z_matrix = band_matrix(kernels[2], offsets[2], depth, depth, 0)
    z_modes = jnp.dot(z_matrix, basis_z.astype(jnp.float32), precision=highest)
    along_z = jnp.einsum(
        "kxy,zk->xyz", section_six.astype(jnp.float32), z_modes, precision=lax.Precision.HIGH
    ).astype(jnp.bfloat16)
    local_descent = jnp.sum(gradient * direction)
    descent = lax.psum(local_descent, ("gx", "gy"))
    blurred = blur_xy(along_z, kernels, offsets)
    data_sum, norm_sum = lax.psum(
        (jnp.sum(weights * blurred * blurred), jnp.sum(direction * direction)), ("gx", "gy")
    )
    energy = data_sum + tikhonov * norm_sum
    step_size = descent / energy
    return (iterate + step_size * direction, misfit - step_size * blurred)


MESH_ID = pl.DeviceIdType.MESH
PARTS = 4


def transform_kernel(
    parts, size_x, size_y,
    section_ref, x_fwd, x_inv, y_fwd, y_inv, eigen_xy, eigen_z,
    out_ref,
    lines_x, lines_y, lines_back, send_a, send_b, send_c, modes,
    fs, fr, gs, gr, hs, hr, bs, br, fl, gl, hl, bl,
):
    me_x = lax.axis_index("gx")
    me_y = lax.axis_index("gy")
    depth = lines_x.shape[0]
    full = lines_x.shape[1]
    block_y = lines_x.shape[2]
    block_x = section_ref.shape[1]
    share = lines_y.shape[1]
    full_y = lines_y.shape[2]
    part = depth // parts
    slots = send_a.shape[0]

    barrier = pltpu.get_barrier_semaphore()
    for step in range(1, size_x):
        pl.semaphore_signal(
            barrier, inc=1, device_id=(lax.rem(me_x + step, size_x), me_y), device_id_type=MESH_ID
        )
    for step in range(1, size_y):
        pl.semaphore_signal(
            barrier, inc=1, device_id=(me_x, lax.rem(me_y + step, size_y)), device_id_type=MESH_ID
        )
    pl.semaphore_wait(barrier, size_x + size_y - 2)

    def copies(kind, c):
        out = []
        here = pl.ds(c * part, part)
        slot = c % slots
        count = size_x if kind in "fb" else size_y
        for step in range(count):
            mine = step == 0
            if kind in "fb":
                peer = lax.rem(me_x + step, size_x)
                target = (peer, me_y)
            else:
                peer = lax.rem(me_y + step, size_y)
                target = (me_x, peer)
            if kind == "f":
                src = section_ref.at[pl.ds(peer * depth + c * part, part)]
                dst = lines_x.at[here, pl.ds(me_x * block_x, block_x)]
                sems = fs, fr, fl
            elif kind == "g":
                src = send_a.at[slot, :, pl.ds(peer * share, share)]
                dst = lines_y.at[here, :, pl.ds(me_y * block_y, block_y)]
                sems = gs, gr, gl
            elif kind == "h":
                src = send_b.at[slot, :, :, pl.ds(peer * block_y, block_y)]
                dst = lines_back.at[here, pl.ds(me_y * share, share)]
                sems = hs, hr, hl
            else:
                src = send_c.at[slot, :, pl.ds(peer * block_x, block_x)]
                dst = out_ref.at[pl.ds(me_x * depth + c * part, part)]
                sems = bs, br, bl
            if mine:
                out.append(pltpu.make_async_copy(src, dst, sems[2].at[c]))
            else:
                out.append(
                    pltpu.make_async_remote_copy(
                        src, dst, sems[0].at[c, step], sems[1].at[c, step],
                        device_id=target, device_id_type=MESH_ID,
                    )
                )
        return out

    every = {kind: [copies(kind, c) for c in range(parts)] for kind in "fghb"}

    def start(kind, c):
        group = every[kind][c]
        for copy in group[1:] + group[:1]:
            copy.start()

    def landed(kind, c):
        group = every[kind][c]
        if kind != "b":
            group[0].wait()
        for copy in group[1:]:
            copy.wait_recv()

    def sent(kind, c):
        group = every[kind][c]
        if kind == "b":
            group[0].wait()
        for copy in group[1:]:
            copy.wait_send()

    def along_x(matrix, lines, out, c):
        def pair(i, carry):
            k = c * part + 2 * i
            both = jnp.concatenate([lines[k], lines[k + 1]], axis=1)
            for b in range(0, full, 256):
                found = jnp.dot(
                    matrix[pl.ds(b, 256), :], both, preferred_element_type=jnp.float32
                ).astype(jnp.bfloat16)
                out[c % slots, 2 * i, pl.ds(b, 256)] = found[:, :block_y]
                out[c % slots, 2 * i + 1, pl.ds(b, 256)] = found[:, block_y:]
            return carry

        lax.fori_loop(0, part // 2, pair, 0)

    def along_y(c):
        def pair(i, carry):
            k = c * part + 2 * i
            rows = jnp.concatenate([lines_y[k], lines_y[k + 1]], axis=0)
            for b in range(0, full_y, 256):
                found = jnp.dot(rows, y_fwd[:, pl.ds(b, 256)], preferred_element_type=jnp.float32)
                weight = eigen_xy[:, pl.ds(b, 256)]
                modes[pl.ds(0, share), pl.ds(b, 256)] = (
                    found[:share] / (weight * eigen_z[k] + tikhonov)
                ).astype(jnp.bfloat16)
                modes[pl.ds(share, share), pl.ds(b, 256)] = (
                    found[share:] / (weight * eigen_z[k + 1] + tikhonov)
                ).astype(jnp.bfloat16)
            for b in range(0, full_y, 256):
                found = jnp.dot(
                    modes[...], y_inv[:, pl.ds(b, 256)], preferred_element_type=jnp.float32
                ).astype(jnp.bfloat16)
                send_b[c % slots, 2 * i, :, pl.ds(b, 256)] = found[:share]
                send_b[c % slots, 2 * i + 1, :, pl.ds(b, 256)] = found[share:]
            return carry

        lax.fori_loop(0, part // 2, pair, 0)

    ahead = min(2, parts)
    for c in range(ahead):
        start("f", c)
    for step in range(parts + 2):
        c = step
        if c < parts:
            landed("f", c)
            if c + ahead < parts:
                start("f", c + ahead)
            if c >= slots:
                sent("g", c - slots)
            along_x(x_fwd, lines_x, send_a, c)
            start("g", c)
        c = step - 1
        if 0 <= c < parts:
            landed("g", c)
            if c >= slots:
                sent("h", c - slots)
            along_y(c)
            start("h", c)
        c = step - 2
        if 0 <= c < parts:
            landed("h", c)
            if c >= slots:
                sent("b", c - slots)
            along_x(x_inv, lines_back, send_c, c)
            start("b", c)
    for c in range(parts):
        landed("b", c)
        sent("f", c)
        if c >= parts - slots:
            sent("g", c)
            sent("h", c)
            sent("b", c)


def transform(section, x_fwd, x_inv, y_fwd, y_inv, eigen_xy, eigen_z, size_x, size_y):
    modes_z, block_x, block_y = section.shape
    depth = modes_z // size_x
    full_x, full_y = x_fwd.shape[0], y_fwd.shape[0]
    share = full_x // size_y
    parts = PARTS
    part = depth // parts
    slots = 2
    vmem = pl.BlockSpec(memory_space=pltpu.VMEM)
    sem = lambda n: pltpu.SemaphoreType.DMA((parts, n))
    one = pltpu.SemaphoreType.DMA((parts,))
    bf = jnp.bfloat16
    return pl.pallas_call(
        functools.partial(transform_kernel, parts, size_x, size_y),
        out_shape=jax.ShapeDtypeStruct(section.shape, bf),
        in_specs=[pl.BlockSpec(memory_space=pl.ANY)] + [vmem] * 5
        + [pl.BlockSpec(memory_space=pltpu.SMEM)],
        out_specs=pl.BlockSpec(memory_space=pl.ANY),
        scratch_shapes=[
            pltpu.VMEM((depth, full_x, block_y), bf),
            pltpu.VMEM((depth, share, full_y), bf),
            pltpu.VMEM((depth, full_x, block_y), bf),
            pltpu.VMEM((slots, part, full_x, block_y), bf),
            pltpu.VMEM((slots, part, share, full_y), bf),
            pltpu.VMEM((slots, part, full_x, block_y), bf),
            pltpu.VMEM((2 * share, full_y), bf),
            sem(size_x), sem(size_x), sem(size_y), sem(size_y),
            sem(size_y), sem(size_y), sem(size_x), sem(size_x),
            one, one, one, one,
        ],
        compiler_params=pltpu.CompilerParams(
            collective_id=0, has_side_effects=True, vmem_limit_bytes=60 * 2**20
        ),
    )(section, x_fwd, x_inv, y_fwd, y_inv, eigen_xy, eigen_z)


BAND_ROWS = 16
QUADS = 4
RIM_ROWS = 32
RIM_LANES = 32


def to_modes_kernel(matrix, source, first, second, held):
    rows, depth = source.shape[0], source.shape[2]
    for x in range(0, rows, 2):
        lines = source[pl.ds(x, 2)].reshape(2 * source.shape[1], depth).astype(jnp.bfloat16)
        found = lax.dot_general(
            matrix[...], lines, (((1,), (1,)), ((), ())), preferred_element_type=jnp.float32
        )
        held[:, x, :] = found[:, : source.shape[1]]
        held[:, x + 1, :] = found[:, source.shape[1] :]
    first[...] = held[:depth].reshape(first.shape).astype(first.dtype)
    second[...] = held[depth:].reshape(second.shape).astype(second.dtype)


def modes_block(rows, shape):
    return pl.BlockSpec((shape[0], shape[1], rows, shape[3]), lambda i: (0, 0, i, 0))


def space_block(rows, shape):
    return pl.BlockSpec((rows, shape[1], shape[2]), lambda i: (i, 0, 0))


def whole_block(shape):
    return pl.BlockSpec(shape, lambda i: (0,) * len(shape))


def to_modes(source, matrix):
    block_x, block_y, depth = source.shape
    shape = (QUADS, depth // QUADS, block_x, block_y)
    out = jax.ShapeDtypeStruct(shape, jnp.bfloat16)
    return pl.pallas_call(
        to_modes_kernel,
        grid=(block_x // BAND_ROWS,),
        out_shape=[out, out],
        in_specs=[whole_block(matrix.shape), space_block(BAND_ROWS, source.shape)],
        out_specs=[modes_block(BAND_ROWS, shape)] * 2,
        scratch_shapes=[pltpu.VMEM((2 * depth, BAND_ROWS, block_y), jnp.float32)],
        compiler_params=pltpu.CompilerParams(vmem_limit_bytes=40 * 2**20),
    )(matrix, source)


def spread_kernel(size_x, size_y, parts, final, source, x_band, to_right, to_left, *rest):
    if final:
        y_band, plain, out, along, from_left, from_right = rest[:6]
        rest = rest[6:]
    else:
        along, from_left, from_right = rest[:3]
        rest = rest[3:]
    low, high, right, left, xs, xr, ys, yr = rest
    me_x = lax.axis_index("gx")
    me_y = lax.axis_index("gy")
    block_x = source.shape[2]
    groups = source.shape[1]
    part = groups // parts
    has = (me_x > 0, me_x < size_x - 1, me_y > 0, me_y < size_y - 1)
    peers = ((me_x - 1, me_y), (me_x + 1, me_y), (me_x, me_y - 1), (me_x, me_y + 1))

    barrier = pltpu.get_barrier_semaphore()
    for peer in (
        (lax.rem(me_x + 1, size_x), me_y), (lax.rem(me_x + size_x - 1, size_x), me_y),
        (me_x, lax.rem(me_y + 1, size_y)), (me_x, lax.rem(me_y + size_y - 1, size_y)),
    ):
        pl.semaphore_signal(barrier, inc=1, device_id=peer, device_id_type=MESH_ID)
    pl.semaphore_wait(barrier, 4)

    def x_copy(c, way):
        here = pl.ds(c * part, part)
        if way == 0:
            src, dst, peer = source.at[:, here, pl.ds(0, RIM_ROWS)], high.at[:, here], peers[0]
        else:
            src = source.at[:, here, pl.ds(block_x - RIM_ROWS, RIM_ROWS)]
            dst, peer = low.at[:, here], peers[1]
        return pltpu.make_async_remote_copy(
            src, dst, xs.at[c, way], xr.at[c, way], device_id=peer, device_id_type=MESH_ID
        )

    def y_copy(c, way):
        here = pl.ds(c * part, part)
        if way == 0:
            src, dst, peer = left.at[here], from_right.at[here], peers[2]
        else:
            src, dst, peer = right.at[here], from_left.at[here], peers[3]
        return pltpu.make_async_remote_copy(
            src, dst, ys.at[c, way], yr.at[c, way], device_id=peer, device_id_type=MESH_ID
        )

    for c in range(parts):
        for way in range(2):

            @pl.when(has[way])
            def _():
                x_copy(c, way).start()

    for there, ref in zip(has, (low, high, from_left, from_right)):

        @pl.when(jnp.logical_not(there))
        def _():
            ref[...] = jnp.zeros_like(ref)

    def blur_x(c):
        def step(i, carry):
            g = c * part + i
            for q in range(0, QUADS, 2):
                both = jnp.concatenate(
                    [
                        jnp.concatenate([low[p, g], source[p, g], high[p, g]], axis=0)
                        for p in (q, q + 1)
                    ],
                    axis=1,
                )
                found = jnp.dot(
                    x_band[...], both, preferred_element_type=jnp.float32
                ).astype(jnp.bfloat16)
                along[q, g] = found[:, : found.shape[1] // 2]
                along[q + 1, g] = found[:, found.shape[1] // 2 :]
            wide = jnp.concatenate([along[q, g] for q in range(QUADS)], axis=1)
            right[g] = jnp.dot(
                wide, to_right[...], preferred_element_type=jnp.float32
            ).astype(jnp.bfloat16)
            left[g] = jnp.dot(
                wide, to_left[...], preferred_element_type=jnp.float32
            ).astype(jnp.bfloat16)
            return carry

        lax.fori_loop(0, part, step, 0)

    def blur_y(c):
        def step(i, carry):
            g = c * part + i
            for q in range(QUADS):
                wide = jnp.concatenate([along[q, g], from_left[g], from_right[g]], axis=1)
                found = jnp.dot(wide, y_band[q], preferred_element_type=jnp.float32)
                out[q, g] = (found - tikhonov * plain[q, g].astype(jnp.float32)).astype(out.dtype)
            return carry

        lax.fori_loop(0, part, step, 0)

    def receive(copy, c):
        for way in range(2):

            @pl.when(has[(0, 2)[copy is y_copy] + 1 - way])
            def _():
                copy(c, way).wait_recv()

    for c in range(parts):
        receive(x_copy, c)
        blur_x(c)
        for way in range(2):

            @pl.when(has[2 + way])
            def _():
                y_copy(c, way).start()

        if final and c > 0:
            receive(y_copy, c - 1)
            blur_y(c - 1)
    if final:
        receive(y_copy, parts - 1)
        blur_y(parts - 1)
    else:
        for c in range(parts):
            receive(y_copy, c)
    for c in range(parts):
        for way in range(2):

            @pl.when(has[way])
            def _():
                x_copy(c, way).wait_send()

            @pl.when(has[2 + way])
            def _():
                y_copy(c, way).wait_send()


def spread(source, x_band, selects, size_x, size_y, number, final=()):
    quads, groups, block_x, block_y = source.shape
    bf = jnp.bfloat16
    whole = jax.ShapeDtypeStruct(source.shape, bf)
    rims = jax.ShapeDtypeStruct((groups, block_x, block_y), bf)
    vmem = pl.BlockSpec(memory_space=pltpu.VMEM)
    parts = PARTS
    outs = [whole] if final else [whole, rims, rims]
    scratch = [pltpu.VMEM(s.shape, bf) for s in (whole, rims, rims)] if final else []
    edge = pltpu.VMEM((quads, groups, RIM_ROWS, block_y), bf)
    packed = pltpu.VMEM(rims.shape, bf)
    sem = pltpu.SemaphoreType.DMA((parts, 2))
    found = pl.pallas_call(
        functools.partial(spread_kernel, size_x, size_y, parts, bool(final)),
        out_shape=outs,
        in_specs=[vmem] * (4 + len(final)),
        out_specs=[vmem] * len(outs),
        scratch_shapes=scratch + [edge, edge, packed, packed, sem, sem, sem, sem],
        compiler_params=pltpu.CompilerParams(
            collective_id=number, has_side_effects=True, vmem_limit_bytes=56 * 2**20
        ),
    )(source, x_band, *selects, *final)
    return found


def blur_y_rows(along, from_left, from_right, y_band, held):
    quads, groups, rows, block_y = along.shape
    count = groups * rows
    sides = [from_left[...].reshape(count, block_y), from_right[...].reshape(count, block_y)]
    for q in range(quads):
        wide = jnp.concatenate([along[q].reshape(count, block_y)] + sides, axis=1)
        found = jnp.dot(wide, y_band[q], preferred_element_type=jnp.float32)
        held[pl.ds(q * groups, groups)] = found.reshape(groups, rows, block_y)


def misfit_kernel(
    along, from_left, from_right, observed, confidence, y_band, matrix,
    misfit, weighted, held, turned_back,
):
    blur_y_rows(along, from_left, from_right, y_band, held)
    for x in range(observed.shape[0]):
        found = observed[x].astype(jnp.float32) - held[:, x, :].T
        misfit[x] = found
        lines = (confidence[x].astype(jnp.float32) * found).astype(jnp.bfloat16)
        turned_back[:, x, :] = lax.dot_general(
            matrix[...], lines, (((1,), (1,)), ((), ())), preferred_element_type=jnp.float32
        )
    weighted[...] = turned_back[...].reshape(weighted.shape).astype(weighted.dtype)


def find_misfit(along, from_left, from_right, observed, confidence, y_band, matrix):
    shape, space = along.shape, observed.shape
    rims = pl.BlockSpec((shape[1], BAND_ROWS, shape[3]), lambda i: (0, i, 0))
    held = pltpu.VMEM((space[2], BAND_ROWS, shape[3]), jnp.float32)
    return pl.pallas_call(
        misfit_kernel,
        grid=(shape[2] // BAND_ROWS,),
        out_shape=[
            jax.ShapeDtypeStruct(space, jnp.float32),
            jax.ShapeDtypeStruct(shape, jnp.bfloat16),
        ],
        in_specs=[
            modes_block(BAND_ROWS, shape), rims, rims,
            space_block(BAND_ROWS, space), space_block(BAND_ROWS, space),
            whole_block(y_band.shape), whole_block(matrix.shape),
        ],
        out_specs=[space_block(BAND_ROWS, space), modes_block(BAND_ROWS, shape)],
        scratch_shapes=[held, held],
        compiler_params=pltpu.CompilerParams(vmem_limit_bytes=40 * 2**20),
    )(along, from_left, from_right, observed, confidence, y_band, matrix)


def folded(values):
    return jnp.sum(values.reshape(-1, 8, values.shape[-1]), axis=0)


def direction_kernel(
    along, from_left, from_right, section_six, section_one, confidence, y_band, basis, blurring,
    direction, blurred, sums, held, held_six,
):
    @pl.when(pl.program_id(0) == 0)
    def _():
        sums[...] = jnp.zeros_like(sums)

    blur_y_rows(along, from_left, from_right, y_band, held)
    six = section_six[...].astype(jnp.float32)
    sums[0] += folded((six * section_one[...].astype(jnp.float32)).reshape(-1, six.shape[-1]))
    held_six[...] = six.reshape(held_six.shape)
    for x in range(confidence.shape[0]):
        lines = held_six[:, x, :].T.astype(jnp.bfloat16)
        found = jnp.dot(lines, basis[...], preferred_element_type=jnp.float32)
        direction[x] = found
        sums[2] += folded(found * found)
        lines = held[:, x, :].T.astype(jnp.bfloat16)
        found = jnp.dot(
            jnp.concatenate([lines, lines], axis=1), blurring[...],
            preferred_element_type=jnp.float32,
        )
        blurred[x] = found
        sums[1] += folded(confidence[x].astype(jnp.float32) * found * found)


def find_direction(
    along, from_left, from_right, section_six, section_one, confidence, y_band, basis, blurring
):
    shape, space = along.shape, confidence.shape
    rims = pl.BlockSpec((shape[1], BAND_ROWS, shape[3]), lambda i: (0, i, 0))
    held = pltpu.VMEM((space[2], BAND_ROWS, shape[3]), jnp.float32)
    sums = (3, 8, space[2])
    return pl.pallas_call(
        direction_kernel,
        grid=(shape[2] // BAND_ROWS,),
        out_shape=[
            jax.ShapeDtypeStruct(space, jnp.float32),
            jax.ShapeDtypeStruct(space, jnp.float32),
            jax.ShapeDtypeStruct(sums, jnp.float32),
        ],
        in_specs=[
            modes_block(BAND_ROWS, shape), rims, rims,
            modes_block(BAND_ROWS, shape), modes_block(BAND_ROWS, shape),
            space_block(BAND_ROWS, space),
            whole_block(y_band.shape), whole_block(basis.shape), whole_block(blurring.shape),
        ],
        out_specs=[
            space_block(BAND_ROWS, space), space_block(BAND_ROWS, space), whole_block(sums),
        ],
        scratch_shapes=[held, held],
        compiler_params=pltpu.CompilerParams(vmem_limit_bytes=40 * 2**20),
    )(
        along, from_left, from_right, section_six, section_one, confidence, y_band, basis, blurring
    )


def total_kernel(size_x, size_y, values, total, from_x, from_y, held, sx, rx, sy, ry):
    me_x = lax.axis_index("gx")
    me_y = lax.axis_index("gy")
    x_peers = [(lax.rem(me_x + s, size_x), me_y) for s in range(1, size_x)]
    y_peers = [(me_x, lax.rem(me_y + s, size_y)) for s in range(1, size_y)]
    barrier = pltpu.get_barrier_semaphore()
    for peer in x_peers + y_peers:
        pl.semaphore_signal(barrier, inc=1, device_id=peer, device_id_type=MESH_ID)
    pl.semaphore_wait(barrier, size_x + size_y - 2)

    def gather(source, landing, peers, sends, receives):
        copies = [
            pltpu.make_async_remote_copy(
                source, landing.at[s], sends.at[s], receives.at[s],
                device_id=peer, device_id_type=MESH_ID,
            )
            for s, peer in enumerate(peers)
        ]
        for copy in copies:
            copy.start()
        for copy in copies:
            copy.wait()
        return source[...] + jnp.sum(landing[...], axis=0)

    held[...] = jnp.sum(values[...], axis=1)
    held[...] = gather(held, from_x, x_peers, sx, rx)
    total[...] = gather(held, from_y, y_peers, sy, ry)


def total_sums(sums, size_x, size_y, number):
    lanes = sums.shape[2]
    padded = jnp.pad(sums, ((0, 5), (0, 0), (0, 0)))
    vmem = pl.BlockSpec(memory_space=pltpu.VMEM)
    sem = lambda n: pltpu.SemaphoreType.DMA((n - 1,))
    f32 = jnp.float32
    return pl.pallas_call(
        functools.partial(total_kernel, size_x, size_y),
        out_shape=jax.ShapeDtypeStruct((8, lanes), f32),
        in_specs=[vmem],
        out_specs=vmem,
        scratch_shapes=[
            pltpu.VMEM((size_x - 1, 8, lanes), f32),
            pltpu.VMEM((size_y - 1, 8, lanes), f32),
            pltpu.VMEM((8, lanes), f32),
            sem(size_x), sem(size_x), sem(size_y), sem(size_y),
        ],
        compiler_params=pltpu.CompilerParams(collective_id=number, has_side_effects=True),
    )(padded)


def y_bands(kernel, offset, block_y):
    rim = HALF + SHIFT
    band = band_matrix(kernel, offset, block_y, block_y + 2 * rim, rim).T
    lanes = QUADS * RIM_LANES
    stacks = []
    for q in range(QUADS):
        before = q * RIM_LANES
        pads = ((before, lanes - before - rim), (0, 0))
        stacks.append(
            jnp.concatenate(
                [band[rim:-rim], jnp.pad(band[:rim], pads), jnp.pad(band[-rim:], pads)], axis=0
            )
        )
    return jnp.stack(stacks).astype(jnp.bfloat16)


def rim_selects(block_y):
    rim = HALF + SHIFT
    row = lax.broadcasted_iota(jnp.int32, (QUADS * block_y, QUADS * RIM_LANES), 0)
    lane = lax.broadcasted_iota(jnp.int32, (QUADS * block_y, QUADS * RIM_LANES), 1)
    same = row // block_y == lane // RIM_LANES
    place = lane % RIM_LANES
    within = jnp.logical_and(same, place < rim)
    spot = row % block_y
    right = jnp.logical_and(within, spot == block_y - rim + place)
    left = jnp.logical_and(within, spot == place)
    return right.astype(jnp.bfloat16), left.astype(jnp.bfloat16)


def kernel_shards(
    observed, confidence, iterate, kernel_bank, tap_index, offsets,
    basis_x, basis_y, basis_z, eigen_x, eigen_y, eigen_z,
):
    size_x, size_y = lax.axis_size("gx"), lax.axis_size("gy")
    block_x, block_y, depth = iterate.shape
    bf = jnp.bfloat16
    kernels = kernels_of(kernel_bank, tap_index)
    adjoint = kernels[:, ::-1]
    full_x = lax.all_gather(basis_x, "gx", axis=0, tiled=True)
    full_y = lax.all_gather(basis_y, "gy", axis=0, tiled=True)
    all_x = lax.all_gather(eigen_x, "gx", axis=0, tiled=True)
    share_x = all_x.shape[0] // size_y
    part_x = lax.dynamic_slice_in_dim(all_x, lax.axis_index("gy") * share_x, share_x)
    share_z = depth // size_x
    part_z = lax.dynamic_slice_in_dim(eigen_z, lax.axis_index("gx") * share_z, share_z)

    wide_x = block_x + 2 * RIM_ROWS
    x_band = band_matrix(kernels[0], offsets[0], block_x, wide_x, RIM_ROWS).astype(bf)
    x_back = band_matrix(adjoint[0], -offsets[0], block_x, wide_x, RIM_ROWS).astype(bf)
    y_band = y_bands(kernels[1], offsets[1], block_y)
    y_back = y_bands(adjoint[1], -offsets[1], block_y)
    z_band = band_matrix(kernels[2], offsets[2], depth, depth, 0)
    selects = rim_selects(block_y)
    basis_f = basis_z.astype(jnp.float32)
    blurring = jnp.dot(z_band, basis_f, precision=highest)
    entry = jnp.concatenate([z_band.astype(bf), basis_z.T], axis=0)

    along_z, plain = to_modes(iterate, entry)
    rims = spread(along_z, x_band, selects, size_x, size_y, 1)
    misfit, weighted = find_misfit(
        *rims, observed, confidence, y_band, blurring.T.astype(bf)
    )
    section_one = spread(
        weighted, x_back, selects, size_x, size_y, 2, (y_back, plain)
    )[0]
    section_six = transform(
        section_one.reshape(depth, block_x, block_y), full_x.T, full_x, full_y, full_y.T,
        part_x[:, None] * eigen_y[None, :], part_z, size_x, size_y,
    ).reshape(section_one.shape)
    rims = spread(section_six, x_band, selects, size_x, size_y, 3)
    coarse = blurring.T.astype(bf)
    fine = (blurring.T - coarse.astype(jnp.float32)).astype(bf)
    direction, blurred, sums = find_direction(
        *rims, section_six, section_one, confidence, y_band, basis_z.T,
        jnp.concatenate([coarse, fine], axis=0),
    )
    totals = jnp.sum(total_sums(sums, size_x, size_y, 4), axis=1)
    step_size = totals[0] / (totals[1] + tikhonov * totals[2])
    return (iterate + step_size * direction, misfit - step_size * blurred)


def kernels_fit(block, size_x, size_y):
    block_x, block_y, depth = block
    return (
        block_y == 128
        and depth == 128
        and block_x == 256
        and depth // size_x == 32
        and block_x * size_x // size_y == 128
        and block_y * size_y % 256 == 0
    )


def step_shards(*arrays):
    fits = kernels_fit(arrays[2].shape, lax.axis_size("gx"), lax.axis_size("gy"))
    return (kernel_shards if fits else shards)(*arrays)


def solution(mesh):
    return jax.shard_map(
        step_shards,
        mesh=mesh,
        in_specs=(
            P("gx", "gy", None),
            P("gx", "gy", None),
            P("gx", "gy", None),
            P(),
            P(),
            P(),
            P("gx", None),
            P("gy", None),
            P(),
            P("gx"),
            P(),
            P(),
        ),
        out_specs=(P("gx", "gy", None), P("gx", "gy", None)),
        check_vma=False,
    )
```

```python
import functools

import jax
import jax.numpy as jnp
from jax import lax
from jax.experimental import pallas as pl
from jax.experimental.pallas import tpu as pltpu
from jax.sharding import PartitionSpec as P

HALF = 16
SHIFT = 4
CHUNKS = 2


highest = lax.Precision.HIGHEST
tikhonov = 0.002


def exchange(block, axis, dim, width):
    count = lax.axis_size(axis)
    forward = [(i, i + 1) for i in range(count - 1)]
    backward = [(target, source) for source, target in forward]
    low = lax.ppermute(
        lax.slice_in_dim(block, block.shape[dim] - width, None, axis=dim), axis, forward
    )
    high = lax.ppermute(lax.slice_in_dim(block, 0, width, axis=dim), axis, backward)
    return low, high


def kernels_of(kernel_bank, tap_index):
    entries = jnp.arange(kernel_bank.shape[1], dtype=jnp.int32)
    chosen = tap_index[:, :, None] == entries[None, None, :]
    raw_taps = jnp.sum(jnp.where(chosen, kernel_bank[:, None, :], 0.0), axis=2)
    return raw_taps / jnp.sum(raw_taps, axis=1, keepdims=True)


def band_matrix(kernel, offset, out_count, in_count, margin):
    center = (kernel.shape[0] - 1) // 2
    row_pos = lax.broadcasted_iota(jnp.int32, (out_count, in_count), 0)
    col_pos = lax.broadcasted_iota(jnp.int32, (out_count, in_count), 1)
    position = col_pos - row_pos - margin + center - offset
    tap_ids = jnp.arange(kernel.shape[0], dtype=jnp.int32)
    chosen = position[None, :, :] == tap_ids[:, None, None]
    return jnp.sum(jnp.where(chosen, kernel[:, None, None], 0.0), axis=0)


def split_dot(spec, matrix, block):
    return jnp.einsum(spec, matrix, block.astype(jnp.float32), precision=lax.Precision.HIGH)


def turned(array, axis_name, dim, sign):
    count = lax.axis_size(axis_name)
    size = array.shape[dim] // count
    mine = lax.axis_index(axis_name)
    pieces = [
        lax.dynamic_slice_in_dim(array, lax.rem(mine + sign * step + count, count) * size, size, dim)
        for step in range(count)
    ]
    return jnp.concatenate(pieces, axis=dim)


def swap(block, axis_name, split, concat, sign):
    count = lax.axis_size(axis_name)
    pieces = jnp.split(block, count, axis=split)
    arrived = [pieces[0]]
    for step in range(1, count):
        pairs = [(i, (i + sign * step) % count) for i in range(count)]
        arrived.append(lax.ppermute(pieces[step], axis_name, pairs))
    return jnp.concatenate(arrived, axis=concat)


def blur_xy(along_z, kernels, offsets):
    rim = HALF + SHIFT
    block_x, block_y, _ = along_z.shape
    x_matrix = band_matrix(kernels[0], offsets[0], block_x, block_x + 2 * rim, rim)
    y_matrix = band_matrix(kernels[1], offsets[1], block_y, block_y + 2 * rim, rim)
    low, high = exchange(along_z, "gx", 0, rim)
    extended = jnp.concatenate([low, along_z, high], axis=0)
    along_x = split_dot("ic,cyz->iyz", x_matrix, extended).astype(jnp.bfloat16)
    low, high = exchange(along_x, "gy", 1, rim)
    inner = split_dot("jc,xcz->xjz", y_matrix[:, rim:-rim], along_x)
    rims = jnp.concatenate([low, high], axis=1)
    rim_matrix = jnp.concatenate([y_matrix[:, :rim], y_matrix[:, -rim:]], axis=1)
    return inner + split_dot("jc,xcz->xjz", rim_matrix, rims)


def apply_blur(source, kernels, offsets):
    depth = source.shape[2]
    z_matrix = band_matrix(kernels[2], offsets[2], depth, depth, 0)
    along_z = jnp.einsum("xyc,zc->xyz", source, z_matrix, precision=lax.Precision.HIGH)
    return blur_xy(along_z.astype(jnp.bfloat16), kernels, offsets)


def shards(
    observed,
    confidence,
    iterate,
    kernel_bank,
    tap_index,
    offsets,
    basis_x,
    basis_y,
    basis_z,
    eigen_x,
    eigen_y,
    eigen_z,
):
    kernels = kernels_of(kernel_bank, tap_index)
    adjoint_kernels = kernels[:, ::-1]
    weights = confidence.astype(jnp.float32)
    misfit = observed.astype(jnp.float32) - apply_blur(iterate, kernels, offsets)
    gradient = apply_blur(weights * misfit, adjoint_kernels, -offsets) - tikhonov * iterate
    full_x = lax.all_gather(basis_x, "gx", axis=0, tiled=True)
    full_y = lax.all_gather(basis_y, "gy", axis=0, tiled=True)

    gradient_b = gradient.astype(jnp.bfloat16)
    gx_size = lax.axis_size("gx")
    depth = basis_z.shape[0]
    share_z = depth // gx_size
    chunks = min(CHUNKS, share_z)
    part = share_z // chunks
    z_ahead = turned(basis_z, "gx", 1, 1).reshape(depth, gx_size, chunks, part)
    eigen_part = lax.dynamic_slice_in_dim(eigen_z, lax.axis_index("gx") * share_z, share_z)
    all_x = lax.all_gather(eigen_x, "gx", axis=0, tiled=True)
    share_x = all_x.shape[0] // lax.axis_size("gy")
    part_x = lax.dynamic_slice_in_dim(all_x, lax.axis_index("gy") * share_x, share_x)
    x_rows_behind = turned(full_x, "gx", 0, -1)
    x_ahead = turned(x_rows_behind, "gy", 1, 1)
    x_return = turned(turned(full_x, "gx", 0, 1), "gy", 1, -1)
    y_behind = turned(full_y, "gy", 0, -1)
    y_ahead = turned(full_y, "gy", 0, 1)
    found = []
    for chunk in range(chunks):
        modes = z_ahead[:, :, chunk].reshape(depth, gx_size * part)
        section_one = jnp.einsum(
            "zk,xyz->kxy", modes, gradient_b, preferred_element_type=jnp.float32
        ).astype(jnp.bfloat16)
        lines = swap(section_one, "gx", 0, 1, 1)
        section_two = jnp.einsum(
            "xj,kxy->kjy", x_ahead, lines, preferred_element_type=jnp.float32
        ).astype(jnp.bfloat16)
        lines = swap(section_two, "gy", 1, 2, 1)
        part_z = eigen_part[chunk * part : (chunk + 1) * part]
        inverse = 1.0 / (
            part_x[None, :, None] * eigen_y[None, None, :] * part_z[:, None, None] + tikhonov
        )
        section_four = (
            jnp.einsum("axy,yk->axk", lines, y_behind, preferred_element_type=jnp.float32)
            * inverse
        ).astype(jnp.bfloat16)
        section_five = jnp.einsum(
            "axk,jk->axj", section_four, y_ahead, preferred_element_type=jnp.float32
        ).astype(jnp.bfloat16)
        lines = swap(section_five, "gy", 2, 1, 1)
        section_six = jnp.einsum(
            "jx,kxy->kjy", x_return, lines, preferred_element_type=jnp.float32
        ).astype(jnp.bfloat16)
        found.append(swap(section_six, "gx", 1, 0, 1))
    section_six = jnp.concatenate(found, axis=0)
    basis_z = (
        turned(basis_z, "gx", 1, -1)
        .reshape(depth, gx_size, chunks, part)
        .transpose(0, 2, 1, 3)
        .reshape(depth, depth)
    )
    direction = jnp.einsum("kxy,zk->xyz", section_six, basis_z, preferred_element_type=jnp.float32)
    z_matrix = band_matrix(kernels[2], offsets[2], depth, depth, 0)
    z_modes = jnp.dot(z_matrix, basis_z.astype(jnp.float32), precision=highest)
    along_z = jnp.einsum(
        "kxy,zk->xyz", section_six.astype(jnp.float32), z_modes, precision=lax.Precision.HIGH
    ).astype(jnp.bfloat16)
    local_descent = jnp.sum(gradient * direction)
    descent = lax.psum(local_descent, ("gx", "gy"))
    blurred = blur_xy(along_z, kernels, offsets)
    data_sum, norm_sum = lax.psum(
        (jnp.sum(weights * blurred * blurred), jnp.sum(direction * direction)), ("gx", "gy")
    )
    energy = data_sum + tikhonov * norm_sum
    step_size = descent / energy
    return (iterate + step_size * direction, misfit - step_size * blurred)


MESH_ID = pl.DeviceIdType.MESH
PARTS = 4


def transform_kernel(
    parts, size_x, size_y,
    weighted, plain, x_back, x_band, y_band, rim_select, x_fwd, x_inv, y_fwd, eigen_xy, eigen_z,
    section_one, section_six, spread_out, left_out, right_out,
    lines_x, lines_y, lines_back, send_a, send_b, send_c, modes, along, low, high, rims,
    from_left, from_right,
    fs, fr, gs, gr, hs, hr, bs, br, fl, gl, hl, bl, xs, xr, ys, yr, us, ur, vs, vr, loads,
):
    me_x = lax.axis_index("gx")
    me_y = lax.axis_index("gy")
    depth, full = lines_x.shape[0], lines_x.shape[1]
    block_y = lines_x.shape[2]
    block_x = section_one.shape[2]
    share, full_y = lines_y.shape[1], lines_y.shape[2]
    part = depth // parts
    slots = send_a.shape[0]
    halves = block_x // share
    bf = jnp.bfloat16

    barrier = pltpu.get_barrier_semaphore()
    for step in range(1, size_x):
        pl.semaphore_signal(
            barrier, inc=1, device_id=(lax.rem(me_x + step, size_x), me_y), device_id_type=MESH_ID
        )
    for step in range(1, size_y):
        pl.semaphore_signal(
            barrier, inc=1, device_id=(me_x, lax.rem(me_y + step, size_y)), device_id_type=MESH_ID
        )
    pl.semaphore_wait(barrier, size_x + size_y - 2)

    has = (me_x > 0, me_x < size_x - 1, me_y > 0, me_y < size_y - 1)
    peers = ((me_x - 1, me_y), (me_x + 1, me_y), (me_x, me_y - 1), (me_x, me_y + 1))

    def remote(src, dst, send, receive, peer):
        return pltpu.make_async_remote_copy(
            src, dst, send, receive, device_id=peer, device_id_type=MESH_ID
        )

    def x_halo(source, sends, receives):
        def copy(c, way):
            here = pl.ds(c * part, part)
            if way == 0:
                src, dst = source.at[here, :, pl.ds(0, RIM_ROWS)], high.at[here]
            else:
                src = source.at[here, :, pl.ds(block_x - RIM_ROWS, RIM_ROWS)]
                dst = low.at[here]
            return remote(src, dst, sends.at[c, way], receives.at[c, way], peers[way])

        return copy, 0

    def y_halo(landing, sends, receives):
        def copy(c, way):
            src = rims.at[c % slots, 1 - way]
            dst = landing[1 - way].at[pl.ds(c * part, part)]
            return remote(src, dst, sends.at[c, way], receives.at[c, way], peers[2 + way])

        return copy, 2

    def halo_start(kind, c):
        copy, base = kind
        for way in range(2):

            @pl.when(has[base + way])
            def _():
                copy(c, way).start()

    def halo_landed(kind, c):
        copy, base = kind
        for way in range(2):

            @pl.when(has[base + 1 - way])
            def _():
                copy(c, way).wait_recv()

    def halo_sent(kind, c):
        copy, base = kind
        for way in range(2):

            @pl.when(has[base + way])
            def _():
                copy(c, way).wait_send()

    def local(source, target, kind, c):
        return pltpu.make_async_copy(source, target, loads.at[kind, c])

    def whole(ref, c):
        return ref.at[pl.ds(c * part, part)]

    def copies(kind, c):
        out = []
        here = pl.ds(c * part, part)
        slot = c % slots
        count = size_x if kind in "fb" else size_y
        for step in range(count):
            if kind in "fb":
                peer = lax.rem(me_x + step, size_x)
                target = (peer, me_y)
            else:
                peer = lax.rem(me_y + step, size_y)
                target = (me_x, peer)
            if kind == "f":
                src = section_one.at[here, peer]
                dst = lines_x.at[here, pl.ds(me_x * block_x, block_x)]
                sems = fs, fr, fl
            elif kind == "g":
                src = send_a.at[
                    slot, :, peer // halves, pl.ds(lax.rem(peer, halves) * share, share)
                ]
                dst = lines_y.at[here, :, pl.ds(me_y * block_y, block_y)]
                sems = gs, gr, gl
            elif kind == "h":
                src = send_b.at[slot, :, :, pl.ds(peer * block_y, block_y)]
                dst = lines_back.at[here, pl.ds(me_y * share, share)]
                sems = hs, hr, hl
            else:
                src = send_c.at[slot, :, peer]
                dst = section_six.at[here, me_x]
                sems = bs, br, bl
            if step == 0:
                out.append(pltpu.make_async_copy(src, dst, sems[2].at[c]))
            else:
                out.append(remote(src, dst, sems[0].at[c, step], sems[1].at[c, step], target))
        return out

    every = {kind: [copies(kind, c) for c in range(parts)] for kind in "fghb"}

    def start(kind, c):
        group = every[kind][c]
        for copy in group[1:] + group[:1]:
            copy.start()

    def landed(kind, c):
        group = every[kind][c]
        if kind != "b":
            group[0].wait()
        for copy in group[1:]:
            copy.wait_recv()

    def sent(kind, c):
        group = every[kind][c]
        if kind == "b":
            group[0].wait()
        for copy in group[1:]:
            copy.wait_send()

    def along_x(matrix, lines, out, c):
        def pair(i, carry):
            k = c * part + 2 * i
            both = jnp.concatenate([lines[k], lines[k + 1]], axis=1)
            for b in range(full // block_x):
                found = jnp.dot(
                    matrix[pl.ds(b * block_x, block_x), :], both,
                    preferred_element_type=jnp.float32,
                ).astype(bf)
                out[c % slots, 2 * i, b] = found[:, :block_y]
                out[c % slots, 2 * i + 1, b] = found[:, block_y:]
            return carry

        lax.fori_loop(0, part // 2, pair, 0)

    def along_y(c):
        def pair(i, carry):
            k = c * part + 2 * i
            rows = jnp.concatenate([lines_y[k], lines_y[k + 1]], axis=0)
            for b in range(0, full_y, 256):
                found = jnp.dot(rows, y_fwd[:, pl.ds(b, 256)], preferred_element_type=jnp.float32)
                weight = eigen_xy[:, pl.ds(b, 256)]
                modes[pl.ds(0, share), pl.ds(b, 256)] = (
                    found[:share] / (weight * eigen_z[k] + tikhonov)
                ).astype(bf)
                modes[pl.ds(share, share), pl.ds(b, 256)] = (
                    found[share:] / (weight * eigen_z[k + 1] + tikhonov)
                ).astype(bf)
            for b in range(0, full_y, 256):
                found = lax.dot_general(
                    modes[...], y_fwd[pl.ds(b, 256), :], (((1,), (1,)), ((), ())),
                    preferred_element_type=jnp.float32,
                ).astype(bf)
                send_b[c % slots, 2 * i, :, pl.ds(b, 256)] = found[:share]
                send_b[c % slots, 2 * i + 1, :, pl.ds(b, 256)] = found[share:]
            return carry

        lax.fori_loop(0, part // 2, pair, 0)

    def blur_x(source, band, c):
        def step(i, carry):
            blur_x_lines(
                [source[c % slots, i, q] for q in range(QUADS)],
                low.at[c * part + i], high.at[c * part + i], band,
                along.at[c % slots, i], rims.at[c % slots, 0, i], rims.at[c % slots, 1, i],
                rim_select,
            )
            return carry

        lax.fori_loop(0, part, step, 0)

    def blur_y(c):
        some = part // 2

        def step(i, carry):
            here = pl.ds(i * some, some)
            there = pl.ds(c * part + i * some, some)
            rows = some * block_x
            sides = [r[there].reshape(rows, block_y) for r in (from_left, from_right)]
            for q in range(QUADS):
                wide = jnp.concatenate(
                    [along[c % slots, here, q].reshape(rows, block_y)] + sides, axis=1
                )
                found = jnp.dot(wide, y_band[q], preferred_element_type=jnp.float32)
                term = send_c[c % slots, here, q].reshape(rows, block_y).astype(jnp.float32)
                send_c[c % slots, here, q] = (
                    (found - tikhonov * term).astype(bf).reshape(some, block_x, block_y)
                )
            return carry

        lax.fori_loop(0, 2, step, 0)

    x_first = x_halo(weighted, xs, xr)
    y_first = y_halo((from_left, from_right), ys, yr)
    load_u = [local(whole(weighted, c), send_a.at[c % slots], 0, c) for c in range(parts)]
    load_p = [local(whole(plain, c), send_c.at[c % slots], 1, c) for c in range(parts)]
    store_one = [local(send_c.at[c % slots], whole(section_one, c), 2, c) for c in range(parts)]
    for c in range(parts):
        halo_start(x_first, c)
    for c in range(slots):
        load_u[c].start()
        load_p[c].start()
    for there, ref in zip(has, (low, high, from_left, from_right)):

        @pl.when(jnp.logical_not(there))
        def _():
            ref[...] = jnp.zeros_like(ref)

    ahead = 2
    for c in range(parts + 1):
        if c < parts:
            load_u[c].wait()
            halo_landed(x_first, c)
            if c >= slots:
                halo_sent(y_first, c - slots)
            blur_x(send_a, x_back, c)
            halo_start(y_first, c)
            if c + slots < parts:
                load_u[c + slots].start()
        if c > 0:
            halo_landed(y_first, c - 1)
            load_p[c - 1].wait()
            blur_y(c - 1)
            store_one[c - 1].start()
            store_one[c - 1].wait()
            if c - 1 < ahead:
                start("f", c - 1)
            if c - 1 + slots < parts:
                load_p[c - 1 + slots].start()
    for c in range(parts):
        halo_sent(x_first, c)
        if c >= parts - slots:
            halo_sent(y_first, c)

    for step in range(parts + 2):
        c = step
        if c < parts:
            landed("f", c)
            if c + ahead < parts:
                start("f", c + ahead)
            if c >= slots:
                sent("g", c - slots)
            along_x(x_fwd, lines_x, send_a, c)
            start("g", c)
        c = step - 1
        if 0 <= c < parts:
            landed("g", c)
            if c >= slots:
                sent("h", c - slots)
            along_y(c)
            start("h", c)
        c = step - 2
        if 0 <= c < parts:
            landed("h", c)
            if c >= slots:
                sent("b", c - slots)
            along_x(x_inv, lines_back, send_c, c)
            start("b", c)
    for c in range(parts):
        sent("f", c)
        if c >= parts - slots:
            sent("g", c)
            sent("h", c)

    x_last = x_halo(section_six, us, ur)
    y_last = y_halo((left_out, right_out), vs, vr)
    load_s = [local(whole(section_six, c), send_a.at[c % slots], 3, c) for c in range(parts)]
    store_a = [local(along.at[c % slots], whole(spread_out, c), 4, c) for c in range(parts)]
    empty = [
        pltpu.make_async_copy(ref, out, loads.at[5, n])
        for n, (ref, out) in enumerate(((from_left, left_out), (from_right, right_out)))
    ]
    for there, copy in zip(has[2:], empty):

        @pl.when(jnp.logical_not(there))
        def _():
            copy.start()

    for c in range(parts + 1):
        if c < parts:
            if c >= parts - slots:
                sent("b", c)
            landed("b", c)
            halo_start(x_last, c)
            load_s[c].start()
        if c > 0:
            d = c - 1
            load_s[d].wait()
            halo_landed(x_last, d)
            if d >= slots:
                halo_sent(y_last, d - slots)
                store_a[d - slots].wait()
            blur_x(send_a, x_band, d)
            halo_start(y_last, d)
            store_a[d].start()
    for c in range(parts):
        halo_landed(y_last, c)
        halo_sent(x_last, c)
        if c >= parts - slots:
            halo_sent(y_last, c)
            store_a[c].wait()
    for there, copy in zip(has[2:], empty):

        @pl.when(jnp.logical_not(there))
        def _():
            copy.wait()


def transform(
    weighted, plain, x_back, x_band, y_back, rim_select, x_fwd, x_inv, y_fwd, eigen_xy, eigen_z,
    size_x, size_y,
):
    depth, quads, block_x, block_y = weighted.shape
    full_x, full_y = x_fwd.shape[0], y_fwd.shape[0]
    share = full_x // size_y
    parts = PARTS
    part = depth // parts
    slots = 2
    vmem = pl.BlockSpec(memory_space=pltpu.VMEM)
    hbm = pl.BlockSpec(memory_space=pl.ANY)
    sem = lambda n: pltpu.SemaphoreType.DMA((parts, n))
    one = pltpu.SemaphoreType.DMA((parts,))
    bf = jnp.bfloat16
    modes = jax.ShapeDtypeStruct(weighted.shape, bf)
    side = jax.ShapeDtypeStruct((depth, block_x, block_y), bf)
    chunk = pltpu.VMEM((slots, part, quads, block_x, block_y), bf)
    edge = pltpu.VMEM((depth, quads, RIM_ROWS, block_y), bf)
    return pl.pallas_call(
        functools.partial(transform_kernel, parts, size_x, size_y),
        out_shape=[modes, modes, modes, side, side],
        in_specs=[hbm, hbm] + [vmem] * 8 + [pl.BlockSpec(memory_space=pltpu.SMEM)],
        out_specs=[hbm] * 5,
        scratch_shapes=[
            pltpu.VMEM((depth, full_x, block_y), bf),
            pltpu.VMEM((depth, share, full_y), bf),
            pltpu.VMEM((depth, full_x, block_y), bf),
            chunk,
            pltpu.VMEM((slots, part, share, full_y), bf),
            chunk,
            pltpu.VMEM((2 * share, full_y), bf),
            chunk,
            edge, edge,
            pltpu.VMEM((slots, 2, part, block_x, block_y), bf),
            pltpu.VMEM(side.shape, bf), pltpu.VMEM(side.shape, bf),
            sem(size_x), sem(size_x), sem(size_y), sem(size_y),
            sem(size_y), sem(size_y), sem(size_x), sem(size_x),
            one, one, one, one,
            sem(2), sem(2), sem(2), sem(2), sem(2), sem(2), sem(2), sem(2),
            pltpu.SemaphoreType.DMA((6, parts)),
        ],
        compiler_params=pltpu.CompilerParams(
            collective_id=0, has_side_effects=True, vmem_limit_bytes=62 * 2**20
        ),
    )(
        weighted, plain, x_back, x_band, y_back, rim_select, x_fwd, x_inv, y_fwd, eigen_xy, eigen_z
    )


def blur_x_lines(lines, low, high, band, along, to_right, to_left, rim_select):
    half = lines[0].shape[1]
    for q in range(0, QUADS, 2):
        both = jnp.concatenate(
            [jnp.concatenate([low[p], lines[p], high[p]], axis=0) for p in (q, q + 1)], axis=1
        )
        found = jnp.dot(band[...], both, preferred_element_type=jnp.float32).astype(jnp.bfloat16)
        along[q] = found[:, :half]
        along[q + 1] = found[:, half:]
    wide = jnp.concatenate([along[q] for q in range(QUADS)], axis=1)
    found = jnp.dot(
        wide, rim_select[...], preferred_element_type=jnp.float32
    ).astype(jnp.bfloat16)
    to_left[...] = found[:, half:]
    to_right[...] = found[:, :half]


BAND_ROWS = 16
QUADS = 4
RIM_ROWS = 32
RIM_LANES = 32


def to_modes_kernel(matrix, source, first, second, held):
    rows, depth = source.shape[0], source.shape[2]
    for x in range(0, rows, 2):
        lines = source[pl.ds(x, 2)].reshape(2 * source.shape[1], depth).astype(jnp.bfloat16)
        found = lax.dot_general(
            matrix[...], lines, (((1,), (1,)), ((), ())), preferred_element_type=jnp.float32
        )
        held[:, x, :] = found[:, : source.shape[1]]
        held[:, x + 1, :] = found[:, source.shape[1] :]
    groups = first.shape[0]
    for q in range(QUADS):
        first[:, q] = held[pl.ds(q * groups, groups)].astype(first.dtype)
        second[:, q] = held[pl.ds(depth + q * groups, groups)].astype(second.dtype)


def modes_block(rows, shape):
    return pl.BlockSpec((shape[0], shape[1], rows, shape[3]), lambda i: (0, 0, i, 0))


def space_block(rows, shape):
    return pl.BlockSpec((rows, shape[1], shape[2]), lambda i: (i, 0, 0))


def whole_block(shape):
    return pl.BlockSpec(shape, lambda i: (0,) * len(shape))


def to_modes(source, matrix):
    block_x, block_y, depth = source.shape
    shape = (depth // QUADS, QUADS, block_x, block_y)
    out = jax.ShapeDtypeStruct(shape, jnp.bfloat16)
    return pl.pallas_call(
        to_modes_kernel,
        grid=(block_x // BAND_ROWS,),
        out_shape=[out, out],
        in_specs=[whole_block(matrix.shape), space_block(BAND_ROWS, source.shape)],
        out_specs=[modes_block(BAND_ROWS, shape)] * 2,
        scratch_shapes=[pltpu.VMEM((2 * depth, BAND_ROWS, block_y), jnp.float32)],
        compiler_params=pltpu.CompilerParams(vmem_limit_bytes=40 * 2**20),
    )(matrix, source)


def spread_kernel(
    size_x, size_y, parts, source, x_band, rim_select, along, from_left, from_right,
    low, high, right, left, xs, xr, ys, yr,
):
    me_x = lax.axis_index("gx")
    me_y = lax.axis_index("gy")
    block_x = source.shape[2]
    groups = source.shape[0]
    part = groups // parts
    has = (me_x > 0, me_x < size_x - 1, me_y > 0, me_y < size_y - 1)
    peers = ((me_x - 1, me_y), (me_x + 1, me_y), (me_x, me_y - 1), (me_x, me_y + 1))

    barrier = pltpu.get_barrier_semaphore()
    for peer in (
        (lax.rem(me_x + 1, size_x), me_y), (lax.rem(me_x + size_x - 1, size_x), me_y),
        (me_x, lax.rem(me_y + 1, size_y)), (me_x, lax.rem(me_y + size_y - 1, size_y)),
    ):
        pl.semaphore_signal(barrier, inc=1, device_id=peer, device_id_type=MESH_ID)
    pl.semaphore_wait(barrier, 4)

    def x_copy(c, way):
        here = pl.ds(c * part, part)
        if way == 0:
            src, dst = source.at[here, :, pl.ds(0, RIM_ROWS)], high.at[here]
        else:
            src = source.at[here, :, pl.ds(block_x - RIM_ROWS, RIM_ROWS)]
            dst = low.at[here]
        return pltpu.make_async_remote_copy(
            src, dst, xs.at[c, way], xr.at[c, way], device_id=peers[way], device_id_type=MESH_ID
        )

    def y_copy(c, way):
        here = pl.ds(c * part, part)
        if way == 0:
            src, dst = left.at[here], from_right.at[here]
        else:
            src, dst = right.at[here], from_left.at[here]
        return pltpu.make_async_remote_copy(
            src, dst, ys.at[c, way], yr.at[c, way], device_id=peers[2 + way],
            device_id_type=MESH_ID,
        )

    for c in range(parts):
        for way in range(2):

            @pl.when(has[way])
            def _():
                x_copy(c, way).start()

    for there, ref in zip(has, (low, high, from_left, from_right)):

        @pl.when(jnp.logical_not(there))
        def _():
            ref[...] = jnp.zeros_like(ref)

    def blur_x(c):
        def step(i, carry):
            g = c * part + i
            blur_x_lines(
                [source[g, q] for q in range(QUADS)], low.at[g], high.at[g], x_band,
                along.at[g], right.at[g], left.at[g], rim_select,
            )
            return carry

        lax.fori_loop(0, part, step, 0)

    for c in range(parts):
        for way in range(2):

            @pl.when(has[1 - way])
            def _():
                x_copy(c, way).wait_recv()

        blur_x(c)
        for way in range(2):

            @pl.when(has[2 + way])
            def _():
                y_copy(c, way).start()

    for c in range(parts):
        for way in range(2):

            @pl.when(has[3 - way])
            def _():
                y_copy(c, way).wait_recv()

            @pl.when(has[way])
            def _():
                x_copy(c, way).wait_send()

            @pl.when(has[2 + way])
            def _():
                y_copy(c, way).wait_send()


def spread(source, x_band, rim_select, size_x, size_y, number):
    groups, quads, block_x, block_y = source.shape
    bf = jnp.bfloat16
    whole = jax.ShapeDtypeStruct(source.shape, bf)
    rims = jax.ShapeDtypeStruct((groups, block_x, block_y), bf)
    vmem = pl.BlockSpec(memory_space=pltpu.VMEM)
    edge = pltpu.VMEM((groups, quads, RIM_ROWS, block_y), bf)
    packed = pltpu.VMEM(rims.shape, bf)
    sem = pltpu.SemaphoreType.DMA((PARTS, 2))
    return pl.pallas_call(
        functools.partial(spread_kernel, size_x, size_y, PARTS),
        out_shape=[whole, rims, rims],
        in_specs=[vmem] * 3,
        out_specs=[vmem] * 3,
        scratch_shapes=[edge, edge, packed, packed, sem, sem, sem, sem],
        compiler_params=pltpu.CompilerParams(
            collective_id=number, has_side_effects=True, vmem_limit_bytes=56 * 2**20
        ),
    )(source, x_band, rim_select)


def blur_y_rows(along, from_left, from_right, y_band, held):
    groups, quads, rows, block_y = along.shape
    count = groups * rows
    sides = [from_left[...].reshape(count, block_y), from_right[...].reshape(count, block_y)]
    for q in range(quads):
        wide = jnp.concatenate([along[:, q].reshape(count, block_y)] + sides, axis=1)
        found = jnp.dot(wide, y_band[q], preferred_element_type=jnp.float32)
        held[pl.ds(q * groups, groups)] = found.reshape(groups, rows, block_y)


def misfit_kernel(
    along, from_left, from_right, observed, confidence, y_band, matrix,
    misfit, weighted, held, turned_back,
):
    blur_y_rows(along, from_left, from_right, y_band, held)
    for x in range(observed.shape[0]):
        found = observed[x].astype(jnp.float32) - held[:, x, :].T
        misfit[x] = found
        lines = (confidence[x].astype(jnp.float32) * found).astype(jnp.bfloat16)
        turned_back[:, x, :] = lax.dot_general(
            matrix[...], lines, (((1,), (1,)), ((), ())), preferred_element_type=jnp.float32
        )
    groups = weighted.shape[0]
    for q in range(QUADS):
        weighted[:, q] = turned_back[pl.ds(q * groups, groups)].astype(weighted.dtype)


def find_misfit(along, from_left, from_right, observed, confidence, y_band, matrix):
    shape, space = along.shape, observed.shape
    rims = pl.BlockSpec((shape[0], BAND_ROWS, shape[3]), lambda i: (0, i, 0))
    held = pltpu.VMEM((space[2], BAND_ROWS, shape[3]), jnp.float32)
    return pl.pallas_call(
        misfit_kernel,
        grid=(shape[2] // BAND_ROWS,),
        out_shape=[
            jax.ShapeDtypeStruct(space, jnp.float32),
            jax.ShapeDtypeStruct(shape, jnp.bfloat16),
        ],
        in_specs=[
            modes_block(BAND_ROWS, shape), rims, rims,
            space_block(BAND_ROWS, space), space_block(BAND_ROWS, space),
            whole_block(y_band.shape), whole_block(matrix.shape),
        ],
        out_specs=[space_block(BAND_ROWS, space), modes_block(BAND_ROWS, shape)],
        scratch_shapes=[held, held],
        compiler_params=pltpu.CompilerParams(vmem_limit_bytes=40 * 2**20),
    )(along, from_left, from_right, observed, confidence, y_band, matrix)


def folded(values):
    return jnp.sum(values.reshape(-1, 8, values.shape[-1]), axis=0)


def direction_kernel(
    along, from_left, from_right, section_six, section_one, confidence, y_band, basis, blurring,
    direction, blurred, sums, held, held_six,
):
    @pl.when(pl.program_id(0) == 0)
    def _():
        sums[...] = jnp.zeros_like(sums)

    blur_y_rows(along, from_left, from_right, y_band, held)
    six = section_six[...].astype(jnp.float32)
    sums[0] += folded((six * section_one[...].astype(jnp.float32)).reshape(-1, six.shape[-1]))
    groups = six.shape[0]
    for q in range(QUADS):
        held_six[pl.ds(q * groups, groups)] = six[:, q]
    for x in range(confidence.shape[0]):
        lines = held_six[:, x, :].T.astype(jnp.bfloat16)
        found = jnp.dot(lines, basis[...], preferred_element_type=jnp.float32)
        direction[x] = found
        sums[2] += folded(found * found)
        lines = held[:, x, :].T.astype(jnp.bfloat16)
        found = jnp.dot(
            jnp.concatenate([lines, lines], axis=1), blurring[...],
            preferred_element_type=jnp.float32,
        )
        blurred[x] = found
        sums[1] += folded(confidence[x].astype(jnp.float32) * found * found)


def find_direction(
    along, from_left, from_right, section_six, section_one, confidence, y_band, basis, blurring
):
    shape, space = along.shape, confidence.shape
    rims = pl.BlockSpec((shape[0], BAND_ROWS, shape[3]), lambda i: (0, i, 0))
    held = pltpu.VMEM((space[2], BAND_ROWS, shape[3]), jnp.float32)
    sums = (3, 8, space[2])
    return pl.pallas_call(
        direction_kernel,
        grid=(shape[2] // BAND_ROWS,),
        out_shape=[
            jax.ShapeDtypeStruct(space, jnp.float32),
            jax.ShapeDtypeStruct(space, jnp.float32),
            jax.ShapeDtypeStruct(sums, jnp.float32),
        ],
        in_specs=[
            modes_block(BAND_ROWS, shape), rims, rims,
            modes_block(BAND_ROWS, shape), modes_block(BAND_ROWS, shape),
            space_block(BAND_ROWS, space),
            whole_block(y_band.shape), whole_block(basis.shape), whole_block(blurring.shape),
        ],
        out_specs=[
            space_block(BAND_ROWS, space), space_block(BAND_ROWS, space), whole_block(sums),
        ],
        scratch_shapes=[held, held],
        compiler_params=pltpu.CompilerParams(vmem_limit_bytes=40 * 2**20),
    )(
        along, from_left, from_right, section_six, section_one, confidence, y_band, basis, blurring
    )


def total_kernel(size_x, size_y, values, total, from_x, from_y, held, sx, rx, sy, ry):
    me_x = lax.axis_index("gx")
    me_y = lax.axis_index("gy")
    x_peers = [(lax.rem(me_x + s, size_x), me_y) for s in range(1, size_x)]
    y_peers = [(me_x, lax.rem(me_y + s, size_y)) for s in range(1, size_y)]
    barrier = pltpu.get_barrier_semaphore()
    for peer in x_peers + y_peers:
        pl.semaphore_signal(barrier, inc=1, device_id=peer, device_id_type=MESH_ID)
    pl.semaphore_wait(barrier, size_x + size_y - 2)

    def gather(source, landing, peers, sends, receives):
        copies = [
            pltpu.make_async_remote_copy(
                source, landing.at[s], sends.at[s], receives.at[s],
                device_id=peer, device_id_type=MESH_ID,
            )
            for s, peer in enumerate(peers)
        ]
        for copy in copies:
            copy.start()
        for copy in copies:
            copy.wait()
        return source[...] + jnp.sum(landing[...], axis=0)

    held[...] = jnp.sum(values[...], axis=1)
    held[...] = gather(held, from_x, x_peers, sx, rx)
    total[...] = gather(held, from_y, y_peers, sy, ry)


def total_sums(sums, size_x, size_y, number):
    lanes = sums.shape[2]
    padded = jnp.pad(sums, ((0, 5), (0, 0), (0, 0)))
    vmem = pl.BlockSpec(memory_space=pltpu.VMEM)
    sem = lambda n: pltpu.SemaphoreType.DMA((n - 1,))
    f32 = jnp.float32
    return pl.pallas_call(
        functools.partial(total_kernel, size_x, size_y),
        out_shape=jax.ShapeDtypeStruct((8, lanes), f32),
        in_specs=[vmem],
        out_specs=vmem,
        scratch_shapes=[
            pltpu.VMEM((size_x - 1, 8, lanes), f32),
            pltpu.VMEM((size_y - 1, 8, lanes), f32),
            pltpu.VMEM((8, lanes), f32),
            sem(size_x), sem(size_x), sem(size_y), sem(size_y),
        ],
        compiler_params=pltpu.CompilerParams(collective_id=number, has_side_effects=True),
    )(padded)


def y_bands(kernel, offset, block_y):
    rim = HALF + SHIFT
    band = band_matrix(kernel, offset, block_y, block_y + 2 * rim, rim).T
    lanes = QUADS * RIM_LANES
    stacks = []
    for q in range(QUADS):
        before = q * RIM_LANES
        pads = ((before, lanes - before - rim), (0, 0))
        stacks.append(
            jnp.concatenate(
                [band[rim:-rim], jnp.pad(band[:rim], pads), jnp.pad(band[-rim:], pads)], axis=0
            )
        )
    return jnp.stack(stacks).astype(jnp.bfloat16)


def rim_selects(block_y):
    rim = HALF + SHIFT
    row = lax.broadcasted_iota(jnp.int32, (QUADS * block_y, QUADS * RIM_LANES), 0)
    lane = lax.broadcasted_iota(jnp.int32, (QUADS * block_y, QUADS * RIM_LANES), 1)
    same = row // block_y == lane // RIM_LANES
    place = lane % RIM_LANES
    within = jnp.logical_and(same, place < rim)
    spot = row % block_y
    right = jnp.logical_and(within, spot == block_y - rim + place)
    left = jnp.logical_and(within, spot == place)
    return jnp.concatenate([right, left], axis=1).astype(jnp.bfloat16)


def kernel_shards(
    observed, confidence, iterate, kernel_bank, tap_index, offsets,
    basis_x, basis_y, basis_z, eigen_x, eigen_y, eigen_z,
):
    size_x, size_y = lax.axis_size("gx"), lax.axis_size("gy")
    block_x, block_y, depth = iterate.shape
    bf = jnp.bfloat16
    kernels = kernels_of(kernel_bank, tap_index)
    adjoint = kernels[:, ::-1]
    full_x = lax.all_gather(basis_x, "gx", axis=0, tiled=True)
    full_y = lax.all_gather(basis_y, "gy", axis=0, tiled=True)
    all_x = lax.all_gather(eigen_x, "gx", axis=0, tiled=True)
    share_x = all_x.shape[0] // size_y
    part_x = lax.dynamic_slice_in_dim(all_x, lax.axis_index("gy") * share_x, share_x)
    share_z = depth // size_x
    part_z = lax.dynamic_slice_in_dim(eigen_z, lax.axis_index("gx") * share_z, share_z)

    wide_x = block_x + 2 * RIM_ROWS
    x_band = band_matrix(kernels[0], offsets[0], block_x, wide_x, RIM_ROWS).astype(bf)
    x_back = band_matrix(adjoint[0], -offsets[0], block_x, wide_x, RIM_ROWS).astype(bf)
    y_band = y_bands(kernels[1], offsets[1], block_y)
    y_back = y_bands(adjoint[1], -offsets[1], block_y)
    z_band = band_matrix(kernels[2], offsets[2], depth, depth, 0)
    rim_select = rim_selects(block_y)
    basis_f = basis_z.astype(jnp.float32)
    blurring = jnp.dot(z_band, basis_f, precision=highest)
    entry = jnp.concatenate([z_band.astype(bf), basis_z.T], axis=0)

    along_z, plain = to_modes(iterate, entry)
    rims = spread(along_z, x_band, rim_select, size_x, size_y, 1)
    misfit, weighted = find_misfit(
        *rims, observed, confidence, y_band, blurring.T.astype(bf)
    )
    section_one, section_six, *rims = transform(
        weighted, plain, x_back, x_band, y_back, rim_select, full_x.T, full_x, full_y,
        part_x[:, None] * eigen_y[None, :], part_z, size_x, size_y,
    )
    coarse = blurring.T.astype(bf)
    fine = (blurring.T - coarse.astype(jnp.float32)).astype(bf)
    direction, blurred, sums = find_direction(
        *rims, section_six, section_one, confidence, y_band, basis_z.T,
        jnp.concatenate([coarse, fine], axis=0),
    )
    totals = jnp.sum(total_sums(sums, size_x, size_y, 2), axis=1)
    step_size = totals[0] / (totals[1] + tikhonov * totals[2])
    return (iterate + step_size * direction, misfit - step_size * blurred)


def kernels_fit(block, size_x, size_y):
    block_x, block_y, depth = block
    return (
        block_y == 128
        and depth == 128
        and block_x == 256
        and depth // size_x == 32
        and block_x * size_x // size_y == 128
        and block_y * size_y % 256 == 0
    )


def step_shards(*arrays):
    fits = kernels_fit(arrays[2].shape, lax.axis_size("gx"), lax.axis_size("gy"))
    return (kernel_shards if fits else shards)(*arrays)


def solution(mesh):
    return jax.shard_map(
        step_shards,
        mesh=mesh,
        in_specs=(
            P("gx", "gy", None),
            P("gx", "gy", None),
            P("gx", "gy", None),
            P(),
            P(),
            P(),
            P("gx", None),
            P("gy", None),
            P(),
            P("gx"),
            P(),
            P(),
        ),
        out_specs=(P("gx", "gy", None), P("gx", "gy", None)),
        check_vma=False,
    )
```

```python
import functools

import jax
import jax.numpy as jnp
from jax import lax
from jax.experimental import pallas as pl
from jax.experimental.pallas import tpu as pltpu
from jax.sharding import PartitionSpec as P

HALF = 16
SHIFT = 4
CHUNKS = 2


highest = lax.Precision.HIGHEST
tikhonov = 0.002


def exchange(block, axis, dim, width):
    count = lax.axis_size(axis)
    forward = [(i, i + 1) for i in range(count - 1)]
    backward = [(target, source) for source, target in forward]
    low = lax.ppermute(
        lax.slice_in_dim(block, block.shape[dim] - width, None, axis=dim), axis, forward
    )
    high = lax.ppermute(lax.slice_in_dim(block, 0, width, axis=dim), axis, backward)
    return low, high


def kernels_of(kernel_bank, tap_index):
    entries = jnp.arange(kernel_bank.shape[1], dtype=jnp.int32)
    chosen = tap_index[:, :, None] == entries[None, None, :]
    raw_taps = jnp.sum(jnp.where(chosen, kernel_bank[:, None, :], 0.0), axis=2)
    return raw_taps / jnp.sum(raw_taps, axis=1, keepdims=True)


def band_matrix(kernel, offset, out_count, in_count, margin):
    center = (kernel.shape[0] - 1) // 2
    row_pos = lax.broadcasted_iota(jnp.int32, (out_count, in_count), 0)
    col_pos = lax.broadcasted_iota(jnp.int32, (out_count, in_count), 1)
    position = col_pos - row_pos - margin + center - offset
    tap_ids = jnp.arange(kernel.shape[0], dtype=jnp.int32)
    chosen = position[None, :, :] == tap_ids[:, None, None]
    return jnp.sum(jnp.where(chosen, kernel[:, None, None], 0.0), axis=0)


def split_dot(spec, matrix, block):
    return jnp.einsum(spec, matrix, block.astype(jnp.float32), precision=lax.Precision.HIGH)


def turned(array, axis_name, dim, sign):
    count = lax.axis_size(axis_name)
    size = array.shape[dim] // count
    mine = lax.axis_index(axis_name)
    pieces = [
        lax.dynamic_slice_in_dim(array, lax.rem(mine + sign * step + count, count) * size, size, dim)
        for step in range(count)
    ]
    return jnp.concatenate(pieces, axis=dim)


def swap(block, axis_name, split, concat, sign):
    count = lax.axis_size(axis_name)
    pieces = jnp.split(block, count, axis=split)
    arrived = [pieces[0]]
    for step in range(1, count):
        pairs = [(i, (i + sign * step) % count) for i in range(count)]
        arrived.append(lax.ppermute(pieces[step], axis_name, pairs))
    return jnp.concatenate(arrived, axis=concat)


def blur_xy(along_z, kernels, offsets):
    rim = HALF + SHIFT
    block_x, block_y, _ = along_z.shape
    x_matrix = band_matrix(kernels[0], offsets[0], block_x, block_x + 2 * rim, rim)
    y_matrix = band_matrix(kernels[1], offsets[1], block_y, block_y + 2 * rim, rim)
    low, high = exchange(along_z, "gx", 0, rim)
    extended = jnp.concatenate([low, along_z, high], axis=0)
    along_x = split_dot("ic,cyz->iyz", x_matrix, extended).astype(jnp.bfloat16)
    low, high = exchange(along_x, "gy", 1, rim)
    inner = split_dot("jc,xcz->xjz", y_matrix[:, rim:-rim], along_x)
    rims = jnp.concatenate([low, high], axis=1)
    rim_matrix = jnp.concatenate([y_matrix[:, :rim], y_matrix[:, -rim:]], axis=1)
    return inner + split_dot("jc,xcz->xjz", rim_matrix, rims)


def apply_blur(source, kernels, offsets):
    depth = source.shape[2]
    z_matrix = band_matrix(kernels[2], offsets[2], depth, depth, 0)
    along_z = jnp.einsum("xyc,zc->xyz", source, z_matrix, precision=lax.Precision.HIGH)
    return blur_xy(along_z.astype(jnp.bfloat16), kernels, offsets)


def shards(
    observed,
    confidence,
    iterate,
    kernel_bank,
    tap_index,
    offsets,
    basis_x,
    basis_y,
    basis_z,
    eigen_x,
    eigen_y,
    eigen_z,
):
    kernels = kernels_of(kernel_bank, tap_index)
    adjoint_kernels = kernels[:, ::-1]
    weights = confidence.astype(jnp.float32)
    misfit = observed.astype(jnp.float32) - apply_blur(iterate, kernels, offsets)
    gradient = apply_blur(weights * misfit, adjoint_kernels, -offsets) - tikhonov * iterate
    full_x = lax.all_gather(basis_x, "gx", axis=0, tiled=True)
    full_y = lax.all_gather(basis_y, "gy", axis=0, tiled=True)

    gradient_b = gradient.astype(jnp.bfloat16)
    gx_size = lax.axis_size("gx")
    depth = basis_z.shape[0]
    share_z = depth // gx_size
    chunks = min(CHUNKS, share_z)
    part = share_z // chunks
    z_ahead = turned(basis_z, "gx", 1, 1).reshape(depth, gx_size, chunks, part)
    eigen_part = lax.dynamic_slice_in_dim(eigen_z, lax.axis_index("gx") * share_z, share_z)
    all_x = lax.all_gather(eigen_x, "gx", axis=0, tiled=True)
    share_x = all_x.shape[0] // lax.axis_size("gy")
    part_x = lax.dynamic_slice_in_dim(all_x, lax.axis_index("gy") * share_x, share_x)
    x_rows_behind = turned(full_x, "gx", 0, -1)
    x_ahead = turned(x_rows_behind, "gy", 1, 1)
    x_return = turned(turned(full_x, "gx", 0, 1), "gy", 1, -1)
    y_behind = turned(full_y, "gy", 0, -1)
    y_ahead = turned(full_y, "gy", 0, 1)
    found = []
    for chunk in range(chunks):
        modes = z_ahead[:, :, chunk].reshape(depth, gx_size * part)
        section_one = jnp.einsum(
            "zk,xyz->kxy", modes, gradient_b, preferred_element_type=jnp.float32
        ).astype(jnp.bfloat16)
        lines = swap(section_one, "gx", 0, 1, 1)
        section_two = jnp.einsum(
            "xj,kxy->kjy", x_ahead, lines, preferred_element_type=jnp.float32
        ).astype(jnp.bfloat16)
        lines = swap(section_two, "gy", 1, 2, 1)
        part_z = eigen_part[chunk * part : (chunk + 1) * part]
        inverse = 1.0 / (
            part_x[None, :, None] * eigen_y[None, None, :] * part_z[:, None, None] + tikhonov
        )
        section_four = (
            jnp.einsum("axy,yk->axk", lines, y_behind, preferred_element_type=jnp.float32)
            * inverse
        ).astype(jnp.bfloat16)
        section_five = jnp.einsum(
            "axk,jk->axj", section_four, y_ahead, preferred_element_type=jnp.float32
        ).astype(jnp.bfloat16)
        lines = swap(section_five, "gy", 2, 1, 1)
        section_six = jnp.einsum(
            "jx,kxy->kjy", x_return, lines, preferred_element_type=jnp.float32
        ).astype(jnp.bfloat16)
        found.append(swap(section_six, "gx", 1, 0, 1))
    section_six = jnp.concatenate(found, axis=0)
    basis_z = (
        turned(basis_z, "gx", 1, -1)
        .reshape(depth, gx_size, chunks, part)
        .transpose(0, 2, 1, 3)
        .reshape(depth, depth)
    )
    direction = jnp.einsum("kxy,zk->xyz", section_six, basis_z, preferred_element_type=jnp.float32)
    z_matrix = band_matrix(kernels[2], offsets[2], depth, depth, 0)
    z_modes = jnp.dot(z_matrix, basis_z.astype(jnp.float32), precision=highest)
    along_z = jnp.einsum(
        "kxy,zk->xyz", section_six.astype(jnp.float32), z_modes, precision=lax.Precision.HIGH
    ).astype(jnp.bfloat16)
    local_descent = jnp.sum(gradient * direction)
    descent = lax.psum(local_descent, ("gx", "gy"))
    blurred = blur_xy(along_z, kernels, offsets)
    data_sum, norm_sum = lax.psum(
        (jnp.sum(weights * blurred * blurred), jnp.sum(direction * direction)), ("gx", "gy")
    )
    energy = data_sum + tikhonov * norm_sum
    step_size = descent / energy
    return (iterate + step_size * direction, misfit - step_size * blurred)


MESH_ID = pl.DeviceIdType.MESH
PARTS = 8


def transform_kernel(
    parts, size_x, size_y,
    weighted, plain, x_back, x_band, y_band, rim_select, x_inv, y_fwd, rows_x, rows_y, eigen_z,
    section_one, section_six, spread_out, left_out, right_out,
    lines_x, lines_y, lines_back, send_a, send_b, send_c, modes, along, low, high, rims,
    from_left, from_right, x_fwd, eigen_xy, all_x,
    fs, fr, gs, gr, hs, hr, bs, br, fl, gl, hl, bl, xs, xr, ys, yr, us, ur, vs, vr, loads, es, er,
):
    me_x = lax.axis_index("gx")
    me_y = lax.axis_index("gy")
    depth, full = lines_x.shape[0], lines_x.shape[1]
    block_y = lines_x.shape[2]
    block_x = section_one.shape[2]
    share, full_y = lines_y.shape[1], lines_y.shape[2]
    part = depth // parts
    slots = send_a.shape[0]
    halves = block_x // share
    bf = jnp.bfloat16

    barrier = pltpu.get_barrier_semaphore()
    for step in range(1, size_x):
        pl.semaphore_signal(
            barrier, inc=1, device_id=(lax.rem(me_x + step, size_x), me_y), device_id_type=MESH_ID
        )
    for step in range(1, size_y):
        pl.semaphore_signal(
            barrier, inc=1, device_id=(me_x, lax.rem(me_y + step, size_y)), device_id_type=MESH_ID
        )
    pl.semaphore_wait(barrier, size_x + size_y - 2)

    has = (me_x > 0, me_x < size_x - 1, me_y > 0, me_y < size_y - 1)
    peers = ((me_x - 1, me_y), (me_x + 1, me_y), (me_x, me_y - 1), (me_x, me_y + 1))

    def remote(src, dst, send, receive, peer):
        return pltpu.make_async_remote_copy(
            src, dst, send, receive, device_id=peer, device_id_type=MESH_ID
        )

    def x_halo(source, sends, receives):
        def copy(c, way):
            here = pl.ds(c * part, part)
            if way == 0:
                src, dst = source.at[here, :, pl.ds(0, RIM_ROWS)], high.at[here]
            else:
                src = source.at[here, :, pl.ds(block_x - RIM_ROWS, RIM_ROWS)]
                dst = low.at[here]
            return remote(src, dst, sends.at[c, way], receives.at[c, way], peers[way])

        return copy, 0

    def y_halo(landing, sends, receives):
        def copy(c, way):
            src = rims.at[c % slots, 1 - way]
            dst = landing[1 - way].at[pl.ds(c * part, part)]
            return remote(src, dst, sends.at[c, way], receives.at[c, way], peers[2 + way])

        return copy, 2

    def halo_start(kind, c):
        copy, base = kind
        for way in range(2):

            @pl.when(has[base + way])
            def _():
                copy(c, way).start()

    def halo_landed(kind, c):
        copy, base = kind
        for way in range(2):

            @pl.when(has[base + 1 - way])
            def _():
                copy(c, way).wait_recv()

    def halo_sent(kind, c):
        copy, base = kind
        for way in range(2):

            @pl.when(has[base + way])
            def _():
                copy(c, way).wait_send()

    def local(source, target, kind, c):
        return pltpu.make_async_copy(source, target, loads.at[kind, c])

    def whole(ref, c):
        return ref.at[pl.ds(c * part, part)]

    def copies(kind, c):
        out = []
        here = pl.ds(c * part, part)
        slot = c % slots
        count = size_x if kind in "fb" else size_y
        for step in range(count):
            if kind in "fb":
                peer = lax.rem(me_x + step, size_x)
                target = (peer, me_y)
            else:
                peer = lax.rem(me_y + step, size_y)
                target = (me_x, peer)
            if kind == "f":
                src = section_one.at[here, peer]
                dst = lines_x.at[here, pl.ds(me_x * block_x, block_x)]
                sems = fs, fr, fl
            elif kind == "g":
                src = send_a.at[
                    slot, :, peer // halves, pl.ds(lax.rem(peer, halves) * share, share)
                ]
                dst = lines_y.at[here, :, pl.ds(me_y * block_y, block_y)]
                sems = gs, gr, gl
            elif kind == "h":
                src = send_b.at[slot, :, :, pl.ds(peer * block_y, block_y)]
                dst = lines_back.at[here, pl.ds(me_y * share, share)]
                sems = hs, hr, hl
            else:
                src = send_c.at[slot, :, peer]
                dst = section_six.at[here, me_x]
                sems = bs, br, bl
            if step == 0:
                out.append(pltpu.make_async_copy(src, dst, sems[2].at[c]))
            else:
                out.append(remote(src, dst, sems[0].at[c, step], sems[1].at[c, step], target))
        return out

    every = {kind: [copies(kind, c) for c in range(parts)] for kind in "fghb"}

    def start(kind, c):
        group = every[kind][c]
        for copy in group[1:] + group[:1]:
            copy.start()

    def landed(kind, c):
        group = every[kind][c]
        if kind != "b":
            group[0].wait()
        for copy in group[1:]:
            copy.wait_recv()

    def sent(kind, c):
        group = every[kind][c]
        if kind == "b":
            group[0].wait()
        for copy in group[1:]:
            copy.wait_send()

    def along_x(matrix, lines, out, c):
        def pair(i, carry):
            k = c * part + 2 * i
            both = jnp.concatenate([lines[k], lines[k + 1]], axis=1)
            for b in range(full // block_x):
                found = jnp.dot(
                    matrix[pl.ds(b * block_x, block_x), :], both,
                    preferred_element_type=jnp.float32,
                ).astype(bf)
                out[c % slots, 2 * i, b] = found[:, :block_y]
                out[c % slots, 2 * i + 1, b] = found[:, block_y:]
            return carry

        lax.fori_loop(0, part // 2, pair, 0)

    def along_y(c):
        def pair(i, carry):
            k = c * part + 2 * i
            rows = jnp.concatenate([lines_y[k], lines_y[k + 1]], axis=0)
            for b in range(0, full_y, 256):
                found = jnp.dot(rows, y_fwd[:, pl.ds(b, 256)], preferred_element_type=jnp.float32)
                weight = eigen_xy[:, pl.ds(b, 256)]
                modes[pl.ds(0, share), pl.ds(b, 256)] = (
                    found[:share] / (weight * eigen_z[k] + tikhonov)
                ).astype(bf)
                modes[pl.ds(share, share), pl.ds(b, 256)] = (
                    found[share:] / (weight * eigen_z[k + 1] + tikhonov)
                ).astype(bf)
            for b in range(0, full_y, 256):
                found = lax.dot_general(
                    modes[...], y_fwd[pl.ds(b, 256), :], (((1,), (1,)), ((), ())),
                    preferred_element_type=jnp.float32,
                ).astype(bf)
                send_b[c % slots, 2 * i, :, pl.ds(b, 256)] = found[:share]
                send_b[c % slots, 2 * i + 1, :, pl.ds(b, 256)] = found[share:]
            return carry

        lax.fori_loop(0, part // 2, pair, 0)

    def blur_x(source, band, c):
        def step(i, carry):
            blur_x_lines(
                [source[c % slots, i, q] for q in range(QUADS)],
                low.at[c * part + i], high.at[c * part + i], band,
                along.at[c % slots, i], rims.at[c % slots, 0, i], rims.at[c % slots, 1, i],
                rim_select,
            )
            return carry

        lax.fori_loop(0, part, step, 0)

    def blur_y(c):
        some = part // 2

        def step(i, carry):
            here = pl.ds(i * some, some)
            there = pl.ds(c * part + i * some, some)
            rows = some * block_x
            sides = [r[there].reshape(rows, block_y) for r in (from_left, from_right)]
            for q in range(QUADS):
                wide = jnp.concatenate(
                    [along[c % slots, here, q].reshape(rows, block_y)] + sides, axis=1
                )
                found = jnp.dot(wide, y_band[q], preferred_element_type=jnp.float32)
                term = send_c[c % slots, here, q].reshape(rows, block_y).astype(jnp.float32)
                send_c[c % slots, here, q] = (
                    (found - tikhonov * term).astype(bf).reshape(some, block_x, block_y)
                )
            return carry

        lax.fori_loop(0, 2, step, 0)

    x_first = x_halo(weighted, xs, xr)
    y_first = y_halo((from_left, from_right), ys, yr)
    load_u = [local(whole(weighted, c), send_a.at[c % slots], 0, c) for c in range(parts)]
    load_p = [local(whole(plain, c), send_c.at[c % slots], 1, c) for c in range(parts)]
    store_one = [local(send_c.at[c % slots], whole(section_one, c), 2, c) for c in range(parts)]
    for c in range(parts):
        halo_start(x_first, c)
    for c in range(slots):
        load_u[c].start()
        load_p[c].start()
    for there, ref in zip(has, (low, high, from_left, from_right)):

        @pl.when(jnp.logical_not(there))
        def _():
            ref[...] = jnp.zeros_like(ref)

    eigen_copies = [
        remote(rows_x, all_x.at[me_x], es.at[step], er.at[step],
               (lax.rem(me_x + step, size_x), me_y))
        for step in range(1, size_x)
    ]
    for copy in eigen_copies:
        copy.start()
    all_x[me_x] = rows_x[...]
    for b in range(0, full, block_y):
        x_fwd[pl.ds(b, block_y), :] = x_inv[:, pl.ds(b, block_y)].astype(jnp.float32).T.astype(bf)

    ahead = 2
    for c in range(parts + 1):
        if c < parts:
            load_u[c].wait()
            halo_landed(x_first, c)
            if c >= slots:
                halo_sent(y_first, c - slots)
            blur_x(send_a, x_back, c)
            halo_start(y_first, c)
            if c + slots < parts:
                load_u[c + slots].start()
        if c > 0:
            halo_landed(y_first, c - 1)
            load_p[c - 1].wait()
            blur_y(c - 1)
            store_one[c - 1].start()
            store_one[c - 1].wait()
            if c - 1 < ahead:
                start("f", c - 1)
            if c - 1 + slots < parts:
                load_p[c - 1 + slots].start()
    for c in range(parts):
        halo_sent(x_first, c)
        if c >= parts - slots:
            halo_sent(y_first, c)

    for copy in eigen_copies:
        copy.wait()
    row = all_x[me_y // halves, lax.rem(me_y, halves)][:1]
    column = jnp.broadcast_to(row, (share, share)).T
    for b in range(0, full_y, share):
        eigen_xy[:, pl.ds(b, share)] = column * rows_y[:1, pl.ds(b, share)]
    for step in range(parts + 2):
        c = step
        if c < parts:
            landed("f", c)
            if c + ahead < parts:
                start("f", c + ahead)
            if c >= slots:
                sent("g", c - slots)
            along_x(x_fwd, lines_x, send_a, c)
            start("g", c)
        c = step - 1
        if 0 <= c < parts:
            landed("g", c)
            if c >= slots:
                sent("h", c - slots)
            along_y(c)
            start("h", c)
        c = step - 2
        if 0 <= c < parts:
            landed("h", c)
            if c >= slots:
                sent("b", c - slots)
            along_x(x_inv, lines_back, send_c, c)
            start("b", c)
    for c in range(parts):
        sent("f", c)
        if c >= parts - slots:
            sent("g", c)
            sent("h", c)

    x_last = x_halo(section_six, us, ur)
    y_last = y_halo((left_out, right_out), vs, vr)
    load_s = [local(whole(section_six, c), send_a.at[c % slots], 3, c) for c in range(parts)]
    store_a = [local(along.at[c % slots], whole(spread_out, c), 4, c) for c in range(parts)]
    empty = [
        pltpu.make_async_copy(ref, out, loads.at[5, n])
        for n, (ref, out) in enumerate(((from_left, left_out), (from_right, right_out)))
    ]
    for there, copy in zip(has[2:], empty):

        @pl.when(jnp.logical_not(there))
        def _():
            copy.start()

    for c in range(parts + 1):
        if c < parts:
            if c >= parts - slots:
                sent("b", c)
            landed("b", c)
            halo_start(x_last, c)
            load_s[c].start()
        if c > 0:
            d = c - 1
            load_s[d].wait()
            halo_landed(x_last, d)
            if d >= slots:
                halo_sent(y_last, d - slots)
                store_a[d - slots].wait()
            blur_x(send_a, x_band, d)
            halo_start(y_last, d)
            store_a[d].start()
    for c in range(parts):
        halo_landed(y_last, c)
        halo_sent(x_last, c)
        if c >= parts - slots:
            halo_sent(y_last, c)
            store_a[c].wait()
    for there, copy in zip(has[2:], empty):

        @pl.when(jnp.logical_not(there))
        def _():
            copy.wait()


def transform(
    weighted, plain, x_back, x_band, y_back, rim_select, x_inv, y_fwd, rows_x, rows_y, eigen_z,
    size_x, size_y,
):
    depth, quads, block_x, block_y = weighted.shape
    full_x, full_y = x_inv.shape[0], y_fwd.shape[0]
    share = full_x // size_y
    parts = PARTS
    part = depth // parts
    slots = 2
    vmem = pl.BlockSpec(memory_space=pltpu.VMEM)
    hbm = pl.BlockSpec(memory_space=pl.ANY)
    sem = lambda n: pltpu.SemaphoreType.DMA((parts, n))
    one = pltpu.SemaphoreType.DMA((parts,))
    bf = jnp.bfloat16
    modes = jax.ShapeDtypeStruct(weighted.shape, bf)
    side = jax.ShapeDtypeStruct((depth, block_x, block_y), bf)
    chunk = pltpu.VMEM((slots, part, quads, block_x, block_y), bf)
    edge = pltpu.VMEM((depth, quads, RIM_ROWS, block_y), bf)
    return pl.pallas_call(
        functools.partial(transform_kernel, parts, size_x, size_y),
        out_shape=[modes, modes, modes, side, side],
        in_specs=[hbm, hbm] + [vmem] * 8 + [pl.BlockSpec(memory_space=pltpu.SMEM)],
        out_specs=[hbm] * 5,
        scratch_shapes=[
            pltpu.VMEM((depth, full_x, block_y), bf),
            pltpu.VMEM((depth, share, full_y), bf),
            pltpu.VMEM((depth, full_x, block_y), bf),
            chunk,
            pltpu.VMEM((slots, part, share, full_y), bf),
            chunk,
            pltpu.VMEM((2 * share, full_y), bf),
            chunk,
            edge, edge,
            pltpu.VMEM((slots, 2, part, block_x, block_y), bf),
            pltpu.VMEM(side.shape, bf), pltpu.VMEM(side.shape, bf),
            pltpu.VMEM((full_x, full_x), bf),
            pltpu.VMEM((share, full_y), jnp.float32),
            pltpu.VMEM((size_x,) + rows_x.shape, jnp.float32),
            sem(size_x), sem(size_x), sem(size_y), sem(size_y),
            sem(size_y), sem(size_y), sem(size_x), sem(size_x),
            one, one, one, one,
            sem(2), sem(2), sem(2), sem(2), sem(2), sem(2), sem(2), sem(2),
            pltpu.SemaphoreType.DMA((6, parts)),
            pltpu.SemaphoreType.DMA((size_x,)), pltpu.SemaphoreType.DMA((size_x,)),
        ],
        compiler_params=pltpu.CompilerParams(
            collective_id=0, has_side_effects=True, vmem_limit_bytes=62 * 2**20
        ),
    )(
        weighted, plain, x_back, x_band, y_back, rim_select, x_inv, y_fwd, rows_x, rows_y, eigen_z
    )


def blur_x_lines(lines, low, high, band, along, to_right, to_left, rim_select):
    half = lines[0].shape[1]
    for q in range(0, len(lines), 2):
        both = jnp.concatenate(
            [jnp.concatenate([low[p], lines[p], high[p]], axis=0) for p in (q, q + 1)], axis=1
        )
        found = jnp.dot(band[...], both, preferred_element_type=jnp.float32).astype(jnp.bfloat16)
        along[q] = found[:, :half]
        along[q + 1] = found[:, half:]
    wide = jnp.concatenate([along[q] for q in range(len(lines))], axis=1)
    found = jnp.dot(
        wide, rim_select[...], preferred_element_type=jnp.float32
    ).astype(jnp.bfloat16)
    to_left[...] = found[:, half:]
    to_right[...] = found[:, :half]


BAND_ROWS = 16
QUADS = 4
RIM_ROWS = 32
SIXES = 6


def to_modes_kernel(matrix, source, first, second, held):
    rows, depth = source.shape[0], source.shape[2]
    for x in range(0, rows, 2):
        lines = source[pl.ds(x, 2)].reshape(2 * source.shape[1], depth).astype(jnp.bfloat16)
        found = lax.dot_general(
            matrix[...], lines, (((1,), (1,)), ((), ())), preferred_element_type=jnp.float32
        )
        held[:, x, :] = found[:, : source.shape[1]]
        held[:, x + 1, :] = found[:, source.shape[1] :]
    full = depth // SIXES
    first[:full] = held[: full * SIXES].reshape((full,) + first.shape[1:]).astype(first.dtype)
    left = depth - full * SIXES
    first[full, :left] = held[full * SIXES : depth].astype(first.dtype)
    first[full, left:] = jnp.zeros((SIXES - left,) + first.shape[2:], first.dtype)
    groups = second.shape[0]
    for q in range(QUADS):
        second[:, q] = held[pl.ds(depth + q * groups, groups)].astype(second.dtype)


def modes_block(rows, shape):
    return pl.BlockSpec((shape[0], shape[1], rows, shape[3]), lambda i: (0, 0, i, 0))


def space_block(rows, shape):
    return pl.BlockSpec((rows, shape[1], shape[2]), lambda i: (i, 0, 0))


def whole_block(shape):
    return pl.BlockSpec(shape, lambda i: (0,) * len(shape))


def to_modes(source, matrix):
    block_x, block_y, depth = source.shape
    shapes = [
        (depth // SIXES + 1, SIXES, block_x, block_y), (depth // QUADS, QUADS, block_x, block_y)
    ]
    return pl.pallas_call(
        to_modes_kernel,
        grid=(block_x // BAND_ROWS,),
        out_shape=[jax.ShapeDtypeStruct(shape, jnp.bfloat16) for shape in shapes],
        in_specs=[whole_block(matrix.shape), space_block(BAND_ROWS, source.shape)],
        out_specs=[modes_block(BAND_ROWS, shape) for shape in shapes],
        scratch_shapes=[pltpu.VMEM((2 * depth, BAND_ROWS, block_y), jnp.float32)],
        compiler_params=pltpu.CompilerParams(vmem_limit_bytes=60 * 2**20),
    )(matrix, source)


def spread_kernel(
    size_x, size_y, parts, source, x_band, rim_select, along, from_left, from_right,
    low, high, right, left, xs, xr, ys, yr,
):
    me_x = lax.axis_index("gx")
    me_y = lax.axis_index("gy")
    block_x = source.shape[2]
    groups = source.shape[0]
    part = groups // parts
    has = (me_x > 0, me_x < size_x - 1, me_y > 0, me_y < size_y - 1)
    peers = ((me_x - 1, me_y), (me_x + 1, me_y), (me_x, me_y - 1), (me_x, me_y + 1))

    barrier = pltpu.get_barrier_semaphore()
    for peer in (
        (lax.rem(me_x + 1, size_x), me_y), (lax.rem(me_x + size_x - 1, size_x), me_y),
        (me_x, lax.rem(me_y + 1, size_y)), (me_x, lax.rem(me_y + size_y - 1, size_y)),
    ):
        pl.semaphore_signal(barrier, inc=1, device_id=peer, device_id_type=MESH_ID)
    pl.semaphore_wait(barrier, 4)

    def x_copy(c, way):
        here = pl.ds(c * part, part)
        if way == 0:
            src, dst = source.at[here, :, pl.ds(0, RIM_ROWS)], high.at[here]
        else:
            src = source.at[here, :, pl.ds(block_x - RIM_ROWS, RIM_ROWS)]
            dst = low.at[here]
        return pltpu.make_async_remote_copy(
            src, dst, xs.at[c, way], xr.at[c, way], device_id=peers[way], device_id_type=MESH_ID
        )

    def y_copy(c, way):
        here = pl.ds(c * part, part)
        if way == 0:
            src, dst = left.at[here], from_right.at[here]
        else:
            src, dst = right.at[here], from_left.at[here]
        return pltpu.make_async_remote_copy(
            src, dst, ys.at[c, way], yr.at[c, way], device_id=peers[2 + way],
            device_id_type=MESH_ID,
        )

    for c in range(parts):
        for way in range(2):

            @pl.when(has[way])
            def _():
                x_copy(c, way).start()

    for there, ref in zip(has, (low, high, from_left, from_right)):

        @pl.when(jnp.logical_not(there))
        def _():
            ref[...] = jnp.zeros_like(ref)

    def blur_x(c):
        def step(i, carry):
            g = c * part + i
            blur_x_lines(
                [source[g, q] for q in range(source.shape[1])], low.at[g], high.at[g], x_band,
                along.at[g], right.at[g], left.at[g], rim_select,
            )
            return carry

        lax.fori_loop(0, part, step, 0)

    for c in range(parts):
        for way in range(2):

            @pl.when(has[1 - way])
            def _():
                x_copy(c, way).wait_recv()

        blur_x(c)
        for way in range(2):

            @pl.when(has[2 + way])
            def _():
                y_copy(c, way).start()

    for c in range(parts):
        for way in range(2):

            @pl.when(has[3 - way])
            def _():
                y_copy(c, way).wait_recv()

            @pl.when(has[way])
            def _():
                x_copy(c, way).wait_send()

            @pl.when(has[2 + way])
            def _():
                y_copy(c, way).wait_send()


def spread(source, x_band, rim_select, size_x, size_y, number):
    groups, quads, block_x, block_y = source.shape
    bf = jnp.bfloat16
    whole = jax.ShapeDtypeStruct(source.shape, bf)
    rims = jax.ShapeDtypeStruct((groups, block_x, block_y), bf)
    vmem = pl.BlockSpec(memory_space=pltpu.VMEM)
    edge = pltpu.VMEM((groups, quads, RIM_ROWS, block_y), bf)
    packed = pltpu.VMEM(rims.shape, bf)
    sem = pltpu.SemaphoreType.DMA((groups // 2, 2))
    return pl.pallas_call(
        functools.partial(spread_kernel, size_x, size_y, groups // 2),
        out_shape=[whole, rims, rims],
        in_specs=[vmem] * 3,
        out_specs=[vmem] * 3,
        scratch_shapes=[edge, edge, packed, packed, sem, sem, sem, sem],
        compiler_params=pltpu.CompilerParams(
            collective_id=number, has_side_effects=True, vmem_limit_bytes=56 * 2**20
        ),
    )(source, x_band, rim_select)


def blur_y_rows(along, from_left, from_right, y_band, put):
    groups, quads, rows, block_y = along.shape
    count = groups * rows
    sides = [from_left[...].reshape(count, block_y), from_right[...].reshape(count, block_y)]
    for q in range(quads):
        wide = jnp.concatenate([along[:, q].reshape(count, block_y)] + sides, axis=1)
        found = jnp.dot(wide, y_band[q], preferred_element_type=jnp.float32)
        put(q, found.reshape(groups, rows, block_y))


def misfit_kernel(
    along, from_left, from_right, observed, confidence, y_band, matrix,
    misfit, weighted, held, turned_back,
):
    def put(s, found):
        for r in range(found.shape[0]):
            held[r * SIXES + s] = found[r]

    blur_y_rows(along, from_left, from_right, y_band, put)
    depth = observed.shape[2]
    for x in range(observed.shape[0]):
        found = observed[x].astype(jnp.float32) - held[:depth, x, :].T
        misfit[x] = found
        lines = (confidence[x].astype(jnp.float32) * found).astype(jnp.bfloat16)
        turned_back[:, x, :] = lax.dot_general(
            matrix[...], lines, (((1,), (1,)), ((), ())), preferred_element_type=jnp.float32
        )
    groups = weighted.shape[0]
    for q in range(QUADS):
        weighted[:, q] = turned_back[pl.ds(q * groups, groups)].astype(weighted.dtype)


def find_misfit(along, from_left, from_right, observed, confidence, y_band, matrix):
    shape, space = along.shape, observed.shape
    modes = (space[2] // QUADS, QUADS, shape[2], shape[3])
    rims = pl.BlockSpec((shape[0], BAND_ROWS, shape[3]), lambda i: (0, i, 0))
    held = pltpu.VMEM((shape[0] * SIXES, BAND_ROWS, shape[3]), jnp.float32)
    turned = pltpu.VMEM((space[2], BAND_ROWS, shape[3]), jnp.float32)
    return pl.pallas_call(
        misfit_kernel,
        grid=(shape[2] // BAND_ROWS,),
        out_shape=[
            jax.ShapeDtypeStruct(space, jnp.float32),
            jax.ShapeDtypeStruct(modes, jnp.bfloat16),
        ],
        in_specs=[
            modes_block(BAND_ROWS, shape), rims, rims,
            space_block(BAND_ROWS, space), space_block(BAND_ROWS, space),
            whole_block(y_band.shape), whole_block(matrix.shape),
        ],
        out_specs=[space_block(BAND_ROWS, space), modes_block(BAND_ROWS, modes)],
        scratch_shapes=[held, turned],
        compiler_params=pltpu.CompilerParams(vmem_limit_bytes=60 * 2**20),
    )(along, from_left, from_right, observed, confidence, y_band, matrix)


def folded(values):
    return jnp.sum(values.reshape(-1, 8, values.shape[-1]), axis=0)


def direction_kernel(
    along, from_left, from_right, section_six, section_one, confidence, y_band, basis, blurring,
    direction, blurred, sums, held, held_six,
):
    @pl.when(pl.program_id(0) == 0)
    def _():
        sums[...] = jnp.zeros_like(sums)

    def put(q, found):
        held[pl.ds(q * found.shape[0], found.shape[0])] = found

    blur_y_rows(along, from_left, from_right, y_band, put)
    six = section_six[...].astype(jnp.float32)
    sums[0] += folded((six * section_one[...].astype(jnp.float32)).reshape(-1, six.shape[-1]))
    groups = six.shape[0]
    for q in range(QUADS):
        held_six[pl.ds(q * groups, groups)] = six[:, q]
    for x in range(confidence.shape[0]):
        lines = held_six[:, x, :].T.astype(jnp.bfloat16)
        found = jnp.dot(lines, basis[...], preferred_element_type=jnp.float32)
        direction[x] = found
        sums[2] += folded(found * found)
        lines = held[:, x, :].T.astype(jnp.bfloat16)
        found = jnp.dot(
            jnp.concatenate([lines, lines], axis=1), blurring[...],
            preferred_element_type=jnp.float32,
        )
        blurred[x] = found
        sums[1] += folded(confidence[x].astype(jnp.float32) * found * found)


def find_direction(
    along, from_left, from_right, section_six, section_one, confidence, y_band, basis, blurring
):
    shape, space = along.shape, confidence.shape
    rims = pl.BlockSpec((shape[0], BAND_ROWS, shape[3]), lambda i: (0, i, 0))
    held = pltpu.VMEM((space[2], BAND_ROWS, shape[3]), jnp.float32)
    sums = (3, 8, space[2])
    return pl.pallas_call(
        direction_kernel,
        grid=(shape[2] // BAND_ROWS,),
        out_shape=[
            jax.ShapeDtypeStruct(space, jnp.float32),
            jax.ShapeDtypeStruct(space, jnp.float32),
            jax.ShapeDtypeStruct(sums, jnp.float32),
        ],
        in_specs=[
            modes_block(BAND_ROWS, shape), rims, rims,
            modes_block(BAND_ROWS, shape), modes_block(BAND_ROWS, shape),
            space_block(BAND_ROWS, space),
            whole_block(y_band.shape), whole_block(basis.shape), whole_block(blurring.shape),
        ],
        out_specs=[
            space_block(BAND_ROWS, space), space_block(BAND_ROWS, space), whole_block(sums),
        ],
        scratch_shapes=[held, held],
        compiler_params=pltpu.CompilerParams(vmem_limit_bytes=60 * 2**20),
    )(
        along, from_left, from_right, section_six, section_one, confidence, y_band, basis, blurring
    )


def total_kernel(size_x, size_y, values, total, from_x, from_y, held, sx, rx, sy, ry):
    me_x = lax.axis_index("gx")
    me_y = lax.axis_index("gy")
    x_peers = [(lax.rem(me_x + s, size_x), me_y) for s in range(1, size_x)]
    y_peers = [(me_x, lax.rem(me_y + s, size_y)) for s in range(1, size_y)]
    barrier = pltpu.get_barrier_semaphore()
    for peer in x_peers + y_peers:
        pl.semaphore_signal(barrier, inc=1, device_id=peer, device_id_type=MESH_ID)
    pl.semaphore_wait(barrier, size_x + size_y - 2)

    def gather(source, landing, peers, sends, receives):
        copies = [
            pltpu.make_async_remote_copy(
                source, landing.at[s], sends.at[s], receives.at[s],
                device_id=peer, device_id_type=MESH_ID,
            )
            for s, peer in enumerate(peers)
        ]
        for copy in copies:
            copy.start()
        for copy in copies:
            copy.wait()
        return source[...] + jnp.sum(landing[...], axis=0)

    held[...] = jnp.sum(values[...], axis=1)
    held[...] = gather(held, from_x, x_peers, sx, rx)
    total[...] = gather(held, from_y, y_peers, sy, ry)


def total_sums(sums, size_x, size_y, number):
    lanes = sums.shape[2]
    padded = jnp.pad(sums, ((0, 5), (0, 0), (0, 0)))
    vmem = pl.BlockSpec(memory_space=pltpu.VMEM)
    sem = lambda n: pltpu.SemaphoreType.DMA((n - 1,))
    f32 = jnp.float32
    return pl.pallas_call(
        functools.partial(total_kernel, size_x, size_y),
        out_shape=jax.ShapeDtypeStruct((8, lanes), f32),
        in_specs=[vmem],
        out_specs=vmem,
        scratch_shapes=[
            pltpu.VMEM((size_x - 1, 8, lanes), f32),
            pltpu.VMEM((size_y - 1, 8, lanes), f32),
            pltpu.VMEM((8, lanes), f32),
            sem(size_x), sem(size_x), sem(size_y), sem(size_y),
        ],
        compiler_params=pltpu.CompilerParams(collective_id=number, has_side_effects=True),
    )(padded)


def y_bands(kernel, offset, block_y, count):
    rim = HALF + SHIFT
    band = band_matrix(kernel, offset, block_y, block_y + 2 * rim, rim).T
    stacks = []
    for q in range(count):
        before = q * (block_y // count)
        pads = ((before, block_y - before - rim), (0, 0))
        stacks.append(
            jnp.concatenate(
                [band[rim:-rim], jnp.pad(band[:rim], pads), jnp.pad(band[-rim:], pads)], axis=0
            )
        )
    return jnp.stack(stacks).astype(jnp.bfloat16)


def rim_selects(block_y, count):
    rim = HALF + SHIFT
    row = lax.broadcasted_iota(jnp.int32, (count * block_y, block_y), 0)
    lane = lax.broadcasted_iota(jnp.int32, (count * block_y, block_y), 1)
    width = block_y // count
    same = row // block_y == lane // width
    place = lane % width
    within = jnp.logical_and(same, place < rim)
    spot = row % block_y
    right = jnp.logical_and(within, spot == block_y - rim + place)
    left = jnp.logical_and(within, spot == place)
    return jnp.concatenate([right, left], axis=1).astype(jnp.bfloat16)


def kernel_shards(
    observed, confidence, iterate, kernel_bank, tap_index, offsets,
    basis_x, basis_y, basis_z, eigen_x, eigen_y, eigen_z,
):
    size_x, size_y = lax.axis_size("gx"), lax.axis_size("gy")
    block_x, block_y, depth = iterate.shape
    bf = jnp.bfloat16
    kernels = kernels_of(kernel_bank, tap_index)
    adjoint = kernels[:, ::-1]
    full_x = lax.all_gather(basis_x, "gx", axis=0, tiled=True)
    full_y = lax.all_gather(basis_y, "gy", axis=0, tiled=True)
    share_x = block_x * size_x // size_y
    rows_x = jnp.broadcast_to(eigen_x.reshape(-1, 1, share_x), (block_x // share_x, 8, share_x))
    rows_y = jnp.broadcast_to(eigen_y[None, :], (8, eigen_y.shape[0]))
    share_z = depth // size_x
    part_z = lax.dynamic_slice_in_dim(eigen_z, lax.axis_index("gx") * share_z, share_z)

    wide_x = block_x + 2 * RIM_ROWS
    x_band = band_matrix(kernels[0], offsets[0], block_x, wide_x, RIM_ROWS).astype(bf)
    x_back = band_matrix(adjoint[0], -offsets[0], block_x, wide_x, RIM_ROWS).astype(bf)
    y_first = y_bands(kernels[1], offsets[1], block_y, SIXES)
    y_band = y_bands(kernels[1], offsets[1], block_y, QUADS)
    y_back = y_bands(adjoint[1], -offsets[1], block_y, QUADS)
    z_band = band_matrix(kernels[2], offsets[2], depth, depth, 0)
    rim_select = rim_selects(block_y, QUADS)
    basis_f = basis_z.astype(jnp.float32)
    blurring = jnp.dot(z_band, basis_f, precision=highest)
    entry = jnp.concatenate([z_band.astype(bf), basis_z.T], axis=0)

    along_z, plain = to_modes(iterate, entry)
    rims = spread(along_z, x_band, rim_selects(block_y, SIXES), size_x, size_y, 1)
    misfit, weighted = find_misfit(
        *rims, observed, confidence, y_first, blurring.T.astype(bf)
    )
    section_one, section_six, *rims = transform(
        weighted, plain, x_back, x_band, y_back, rim_select, full_x, full_y,
        rows_x, rows_y, part_z, size_x, size_y,
    )
    coarse = blurring.T.astype(bf)
    fine = (blurring.T - coarse.astype(jnp.float32)).astype(bf)
    direction, blurred, sums = find_direction(
        *rims, section_six, section_one, confidence, y_band, basis_z.T,
        jnp.concatenate([coarse, fine], axis=0),
    )
    totals = jnp.sum(total_sums(sums, size_x, size_y, 2), axis=1)
    step_size = totals[0] / (totals[1] + tikhonov * totals[2])
    return (iterate + step_size * direction, misfit - step_size * blurred)


def kernels_fit(block, size_x, size_y):
    block_x, block_y, depth = block
    return (
        block_y == 128
        and depth == 128
        and block_x == 256
        and depth // size_x == 32
        and block_x * size_x // size_y == 128
        and block_y * size_y % 256 == 0
    )


def step_shards(*arrays):
    fits = kernels_fit(arrays[2].shape, lax.axis_size("gx"), lax.axis_size("gy"))
    return (kernel_shards if fits else shards)(*arrays)


def solution(mesh):
    return jax.shard_map(
        step_shards,
        mesh=mesh,
        in_specs=(
            P("gx", "gy", None),
            P("gx", "gy", None),
            P("gx", "gy", None),
            P(),
            P(),
            P(),
            P("gx", None),
            P("gy", None),
            P(),
            P("gx"),
            P(),
            P(),
        ),
        out_specs=(P("gx", "gy", None), P("gx", "gy", None)),
        check_vma=False,
    )
```

```python
import functools

import jax
import jax.numpy as jnp
from jax import lax
from jax.experimental import pallas as pl
from jax.experimental.pallas import tpu as pltpu
from jax.sharding import PartitionSpec as P

HALF = 16
SHIFT = 4
CHUNKS = 2


highest = lax.Precision.HIGHEST
tikhonov = 0.002


def exchange(block, axis, dim, width):
    count = lax.axis_size(axis)
    forward = [(i, i + 1) for i in range(count - 1)]
    backward = [(target, source) for source, target in forward]
    low = lax.ppermute(
        lax.slice_in_dim(block, block.shape[dim] - width, None, axis=dim), axis, forward
    )
    high = lax.ppermute(lax.slice_in_dim(block, 0, width, axis=dim), axis, backward)
    return low, high


def kernels_of(kernel_bank, tap_index):
    entries = jnp.arange(kernel_bank.shape[1], dtype=jnp.int32)
    chosen = tap_index[:, :, None] == entries[None, None, :]
    raw_taps = jnp.sum(jnp.where(chosen, kernel_bank[:, None, :], 0.0), axis=2)
    return raw_taps / jnp.sum(raw_taps, axis=1, keepdims=True)


def band_matrix(kernel, offset, out_count, in_count, margin):
    center = (kernel.shape[0] - 1) // 2
    row_pos = lax.broadcasted_iota(jnp.int32, (out_count, in_count), 0)
    col_pos = lax.broadcasted_iota(jnp.int32, (out_count, in_count), 1)
    position = col_pos - row_pos - margin + center - offset
    tap_ids = jnp.arange(kernel.shape[0], dtype=jnp.int32)
    chosen = position[None, :, :] == tap_ids[:, None, None]
    return jnp.sum(jnp.where(chosen, kernel[:, None, None], 0.0), axis=0)


def split_dot(spec, matrix, block):
    return jnp.einsum(spec, matrix, block.astype(jnp.float32), precision=lax.Precision.HIGH)


def turned(array, axis_name, dim, sign):
    count = lax.axis_size(axis_name)
    size = array.shape[dim] // count
    mine = lax.axis_index(axis_name)
    pieces = [
        lax.dynamic_slice_in_dim(array, lax.rem(mine + sign * step + count, count) * size, size, dim)
        for step in range(count)
    ]
    return jnp.concatenate(pieces, axis=dim)


def swap(block, axis_name, split, concat, sign):
    count = lax.axis_size(axis_name)
    pieces = jnp.split(block, count, axis=split)
    arrived = [pieces[0]]
    for step in range(1, count):
        pairs = [(i, (i + sign * step) % count) for i in range(count)]
        arrived.append(lax.ppermute(pieces[step], axis_name, pairs))
    return jnp.concatenate(arrived, axis=concat)


def blur_xy(along_z, kernels, offsets):
    rim = HALF + SHIFT
    block_x, block_y, _ = along_z.shape
    x_matrix = band_matrix(kernels[0], offsets[0], block_x, block_x + 2 * rim, rim)
    y_matrix = band_matrix(kernels[1], offsets[1], block_y, block_y + 2 * rim, rim)
    low, high = exchange(along_z, "gx", 0, rim)
    extended = jnp.concatenate([low, along_z, high], axis=0)
    along_x = split_dot("ic,cyz->iyz", x_matrix, extended).astype(jnp.bfloat16)
    low, high = exchange(along_x, "gy", 1, rim)
    inner = split_dot("jc,xcz->xjz", y_matrix[:, rim:-rim], along_x)
    rims = jnp.concatenate([low, high], axis=1)
    rim_matrix = jnp.concatenate([y_matrix[:, :rim], y_matrix[:, -rim:]], axis=1)
    return inner + split_dot("jc,xcz->xjz", rim_matrix, rims)


def apply_blur(source, kernels, offsets):
    depth = source.shape[2]
    z_matrix = band_matrix(kernels[2], offsets[2], depth, depth, 0)
    along_z = jnp.einsum("xyc,zc->xyz", source, z_matrix, precision=lax.Precision.HIGH)
    return blur_xy(along_z.astype(jnp.bfloat16), kernels, offsets)


def shards(
    observed,
    confidence,
    iterate,
    kernel_bank,
    tap_index,
    offsets,
    basis_x,
    basis_y,
    basis_z,
    eigen_x,
    eigen_y,
    eigen_z,
):
    kernels = kernels_of(kernel_bank, tap_index)
    adjoint_kernels = kernels[:, ::-1]
    weights = confidence.astype(jnp.float32)
    misfit = observed.astype(jnp.float32) - apply_blur(iterate, kernels, offsets)
    gradient = apply_blur(weights * misfit, adjoint_kernels, -offsets) - tikhonov * iterate
    full_x = lax.all_gather(basis_x, "gx", axis=0, tiled=True)
    full_y = lax.all_gather(basis_y, "gy", axis=0, tiled=True)

    gradient_b = gradient.astype(jnp.bfloat16)
    gx_size = lax.axis_size("gx")
    depth = basis_z.shape[0]
    share_z = depth // gx_size
    chunks = min(CHUNKS, share_z)
    part = share_z // chunks
    z_ahead = turned(basis_z, "gx", 1, 1).reshape(depth, gx_size, chunks, part)
    eigen_part = lax.dynamic_slice_in_dim(eigen_z, lax.axis_index("gx") * share_z, share_z)
    all_x = lax.all_gather(eigen_x, "gx", axis=0, tiled=True)
    share_x = all_x.shape[0] // lax.axis_size("gy")
    part_x = lax.dynamic_slice_in_dim(all_x, lax.axis_index("gy") * share_x, share_x)
    x_rows_behind = turned(full_x, "gx", 0, -1)
    x_ahead = turned(x_rows_behind, "gy", 1, 1)
    x_return = turned(turned(full_x, "gx", 0, 1), "gy", 1, -1)
    y_behind = turned(full_y, "gy", 0, -1)
    y_ahead = turned(full_y, "gy", 0, 1)
    found = []
    for chunk in range(chunks):
        modes = z_ahead[:, :, chunk].reshape(depth, gx_size * part)
        section_one = jnp.einsum(
            "zk,xyz->kxy", modes, gradient_b, preferred_element_type=jnp.float32
        ).astype(jnp.bfloat16)
        lines = swap(section_one, "gx", 0, 1, 1)
        section_two = jnp.einsum(
            "xj,kxy->kjy", x_ahead, lines, preferred_element_type=jnp.float32
        ).astype(jnp.bfloat16)
        lines = swap(section_two, "gy", 1, 2, 1)
        part_z = eigen_part[chunk * part : (chunk + 1) * part]
        inverse = 1.0 / (
            part_x[None, :, None] * eigen_y[None, None, :] * part_z[:, None, None] + tikhonov
        )
        section_four = (
            jnp.einsum("axy,yk->axk", lines, y_behind, preferred_element_type=jnp.float32)
            * inverse
        ).astype(jnp.bfloat16)
        section_five = jnp.einsum(
            "axk,jk->axj", section_four, y_ahead, preferred_element_type=jnp.float32
        ).astype(jnp.bfloat16)
        lines = swap(section_five, "gy", 2, 1, 1)
        section_six = jnp.einsum(
            "jx,kxy->kjy", x_return, lines, preferred_element_type=jnp.float32
        ).astype(jnp.bfloat16)
        found.append(swap(section_six, "gx", 1, 0, 1))
    section_six = jnp.concatenate(found, axis=0)
    basis_z = (
        turned(basis_z, "gx", 1, -1)
        .reshape(depth, gx_size, chunks, part)
        .transpose(0, 2, 1, 3)
        .reshape(depth, depth)
    )
    direction = jnp.einsum("kxy,zk->xyz", section_six, basis_z, preferred_element_type=jnp.float32)
    z_matrix = band_matrix(kernels[2], offsets[2], depth, depth, 0)
    z_modes = jnp.dot(z_matrix, basis_z.astype(jnp.float32), precision=highest)
    along_z = jnp.einsum(
        "kxy,zk->xyz", section_six.astype(jnp.float32), z_modes, precision=lax.Precision.HIGH
    ).astype(jnp.bfloat16)
    local_descent = jnp.sum(gradient * direction)
    descent = lax.psum(local_descent, ("gx", "gy"))
    blurred = blur_xy(along_z, kernels, offsets)
    data_sum, norm_sum = lax.psum(
        (jnp.sum(weights * blurred * blurred), jnp.sum(direction * direction)), ("gx", "gy")
    )
    energy = data_sum + tikhonov * norm_sum
    step_size = descent / energy
    return (iterate + step_size * direction, misfit - step_size * blurred)


MESH_ID = pl.DeviceIdType.MESH
PARTS = 8


def transform_kernel(
    parts, size_x, size_y,
    weighted, plain, first_rest, last_rest,
    x_back, x_band, y_band, rim_select, x_inv, y_fwd, rows_x, rows_y, eigen_z,
    section_one, section_six, spread_out, left_out, right_out,
    lines_x, lines_y, lines_back, send_a, send_b, send_c, modes, along, low, high, low_rest, high_rest,
    found_rest, rims,
    from_left, from_right, x_fwd, eigen_xy, all_x,
    fs, fr, gs, gr, hs, hr, bs, br, fl, gl, hl, bl, xs, xr, ys, yr, us, ur, vs, vr, loads, es, er,
):
    me_x = lax.axis_index("gx")
    me_y = lax.axis_index("gy")
    depth, full = lines_x.shape[0], lines_x.shape[1]
    block_y = lines_x.shape[2]
    block_x = section_one.shape[2]
    share, full_y = lines_y.shape[1], lines_y.shape[2]
    part = depth // parts
    slots = send_a.shape[0]
    halves = block_x // share
    bf = jnp.bfloat16

    barrier = pltpu.get_barrier_semaphore()
    for step in range(1, size_x):
        pl.semaphore_signal(
            barrier, inc=1, device_id=(lax.rem(me_x + step, size_x), me_y), device_id_type=MESH_ID
        )
    for step in range(1, size_y):
        pl.semaphore_signal(
            barrier, inc=1, device_id=(me_x, lax.rem(me_y + step, size_y)), device_id_type=MESH_ID
        )
    pl.semaphore_wait(barrier, size_x + size_y - 2)

    has = (me_x > 0, me_x < size_x - 1, me_y > 0, me_y < size_y - 1)
    peers = ((me_x - 1, me_y), (me_x + 1, me_y), (me_x, me_y - 1), (me_x, me_y + 1))

    def remote(src, dst, send, receive, peer):
        return pltpu.make_async_remote_copy(
            src, dst, send, receive, device_id=peer, device_id_type=MESH_ID
        )

    def x_halo(source, rests, sends, receives):
        def copies_of(c, way):
            here = pl.ds(c * part, part)
            if way == 0:
                near = source.at[here, :, pl.ds(0, NEAR)], high.at[here]
                rest = rests[0].at[here], high_rest.at[here]
            else:
                near = source.at[here, :, pl.ds(block_x - NEAR, NEAR)], low.at[here]
                rest = rests[1].at[here], low_rest.at[here]
            return [
                remote(*pair, sends.at[c, 2 * way + n], receives.at[c, 2 * way + n], peers[way])
                for n, pair in enumerate((near, rest))
            ]

        return copies_of, 0

    def y_halo(landing, sends, receives):
        def copies_of(c, way):
            src = rims.at[c % slots, 1 - way]
            dst = landing[1 - way].at[pl.ds(c * part, part)]
            return [remote(src, dst, sends.at[c, way], receives.at[c, way], peers[2 + way])]

        return copies_of, 2

    def halo_start(kind, c):
        copies_of, base = kind
        for way in range(2):

            @pl.when(has[base + way])
            def _():
                for copy in copies_of(c, way):
                    copy.start()

    def halo_landed(kind, c):
        copies_of, base = kind
        for way in range(2):

            @pl.when(has[base + 1 - way])
            def _():
                for copy in copies_of(c, way):
                    copy.wait_recv()

    def halo_sent(kind, c):
        copies_of, base = kind
        for way in range(2):

            @pl.when(has[base + way])
            def _():
                for copy in copies_of(c, way):
                    copy.wait_send()

    def local(source, target, kind, c):
        return pltpu.make_async_copy(source, target, loads.at[kind, c])

    def whole(ref, c):
        return ref.at[pl.ds(c * part, part)]

    def copies(kind, c):
        out = []
        here = pl.ds(c * part, part)
        slot = c % slots
        count = size_x if kind in "fb" else size_y
        for step in range(count):
            if kind in "fb":
                peer = lax.rem(me_x + step, size_x)
                target = (peer, me_y)
            else:
                peer = lax.rem(me_y + step, size_y)
                target = (me_x, peer)
            if kind == "f":
                src = section_one.at[here, peer]
                dst = lines_x.at[here, pl.ds(me_x * block_x, block_x)]
                sems = fs, fr, fl
            elif kind == "g":
                src = send_a.at[
                    slot, :, peer // halves, pl.ds(lax.rem(peer, halves) * share, share)
                ]
                dst = lines_y.at[here, :, pl.ds(me_y * block_y, block_y)]
                sems = gs, gr, gl
            elif kind == "h":
                src = send_b.at[slot, :, :, pl.ds(peer * block_y, block_y)]
                dst = lines_back.at[here, pl.ds(me_y * share, share)]
                sems = hs, hr, hl
            else:
                src = send_c.at[slot, :, peer]
                dst = section_six.at[here, me_x]
                sems = bs, br, bl
            if step == 0:
                out.append(pltpu.make_async_copy(src, dst, sems[2].at[c]))
            else:
                out.append(remote(src, dst, sems[0].at[c, step], sems[1].at[c, step], target))
        return out

    every = {kind: [copies(kind, c) for c in range(parts)] for kind in "fghb"}

    def start(kind, c):
        group = every[kind][c]
        for copy in group[1:] + group[:1]:
            copy.start()

    def landed(kind, c):
        group = every[kind][c]
        if kind != "b":
            group[0].wait()
        for copy in group[1:]:
            copy.wait_recv()

    def sent(kind, c):
        group = every[kind][c]
        if kind == "b":
            group[0].wait()
        for copy in group[1:]:
            copy.wait_send()

    def along_x(matrix, lines, out, c):
        def pair(i, carry):
            k = c * part + 2 * i
            both = jnp.concatenate([lines[k], lines[k + 1]], axis=1)
            for b in range(full // block_x):
                found = jnp.dot(
                    matrix[pl.ds(b * block_x, block_x), :], both,
                    preferred_element_type=jnp.float32,
                ).astype(bf)
                out[c % slots, 2 * i, b] = found[:, :block_y]
                out[c % slots, 2 * i + 1, b] = found[:, block_y:]
            return carry

        lax.fori_loop(0, part // 2, pair, 0)

    def along_y(c):
        def pair(i, carry):
            k = c * part + 2 * i
            rows = jnp.concatenate([lines_y[k], lines_y[k + 1]], axis=0)
            for b in range(0, full_y, 256):
                found = jnp.dot(rows, y_fwd[:, pl.ds(b, 256)], preferred_element_type=jnp.float32)
                weight = eigen_xy[:, pl.ds(b, 256)]
                modes[pl.ds(0, share), pl.ds(b, 256)] = (
                    found[:share] / (weight * eigen_z[me_x * depth + k] + tikhonov)
                ).astype(bf)
                modes[pl.ds(share, share), pl.ds(b, 256)] = (
                    found[share:] / (weight * eigen_z[me_x * depth + k + 1] + tikhonov)
                ).astype(bf)
            for b in range(0, full_y, 256):
                found = lax.dot_general(
                    modes[...], y_fwd[pl.ds(b, 256), :], (((1,), (1,)), ((), ())),
                    preferred_element_type=jnp.float32,
                ).astype(bf)
                send_b[c % slots, 2 * i, :, pl.ds(b, 256)] = found[:share]
                send_b[c % slots, 2 * i + 1, :, pl.ds(b, 256)] = found[share:]
            return carry

        lax.fori_loop(0, part // 2, pair, 0)

    def blur_x(source, band, c):
        slot = c % slots

        def step(i, carry):
            for q in range(QUADS):
                both = jnp.concatenate(
                    [
                        jnp.concatenate(
                            [
                                low[c * part + p, q], low_rest[c * part + p], source[slot, p, q],
                                high[c * part + p, q], high_rest[c * part + p],
                            ],
                            axis=0,
                        )
                        for p in (2 * i, 2 * i + 1)
                    ],
                    axis=1,
                )
                found = jnp.dot(band[q], both, preferred_element_type=jnp.float32).astype(bf)
                along[slot, 2 * i, q] = found[:, :block_y]
                along[slot, 2 * i + 1, q] = found[:, block_y:]
            for p in (2 * i, 2 * i + 1):
                pack_rims(
                    [along[slot, p, q] for q in range(QUADS)],
                    rims.at[slot, 0, p], rims.at[slot, 1, p], rim_select,
                )
            return carry

        lax.fori_loop(0, part // 2, step, 0)

    def pack_rest(source, c):
        def step(i, carry):
            for n, row, skip in ((0, NEAR, 0), (1, block_x - 2 * NEAR, NEAR - REST)):
                lines = [
                    source[c % slots, i, q, pl.ds(row, NEAR)].astype(jnp.float32)[
                        skip : skip + REST
                    ]
                    for q in range(QUADS)
                ]
                found_rest[n, c * part + i] = jnp.concatenate(lines, axis=0).astype(bf)
            return carry

        lax.fori_loop(0, part, step, 0)

    def blur_y(c):
        some = part // 2

        def step(i, carry):
            here = pl.ds(i * some, some)
            there = pl.ds(c * part + i * some, some)
            rows = some * block_x
            sides = [r[there].reshape(rows, block_y) for r in (from_left, from_right)]
            for q in range(QUADS):
                wide = jnp.concatenate(
                    [along[c % slots, here, q].reshape(rows, block_y)] + sides, axis=1
                )
                found = jnp.dot(wide, y_band[q], preferred_element_type=jnp.float32)
                term = send_c[c % slots, here, q].reshape(rows, block_y).astype(jnp.float32)
                send_c[c % slots, here, q] = (
                    (found - tikhonov * term).astype(bf).reshape(some, block_x, block_y)
                )
            return carry

        lax.fori_loop(0, 2, step, 0)

    x_first = x_halo(weighted, (first_rest, last_rest), xs, xr)
    y_first = y_halo((from_left, from_right), ys, yr)
    load_u = [local(whole(weighted, c), send_a.at[c % slots], 0, c) for c in range(parts)]
    load_p = [local(whole(plain, c), send_c.at[c % slots], 1, c) for c in range(parts)]
    store_one = [local(send_c.at[c % slots], whole(section_one, c), 2, c) for c in range(parts)]
    for c in range(parts):
        halo_start(x_first, c)
    for c in range(slots):
        load_u[c].start()
        load_p[c].start()
    for there, ref in zip(
        has + has[:2], (low, high, from_left, from_right, low_rest, high_rest)
    ):

        @pl.when(jnp.logical_not(there))
        def _():
            ref[...] = jnp.zeros_like(ref)

    eigen_copies = [
        remote(rows_x, all_x.at[me_x], es.at[step], er.at[step],
               (lax.rem(me_x + step, size_x), me_y))
        for step in range(1, size_x)
    ]
    for copy in eigen_copies:
        copy.start()
    all_x[me_x] = rows_x[...]
    for b in range(0, full, block_y):
        x_fwd[pl.ds(b, block_y), :] = x_inv[:, pl.ds(b, block_y)].astype(jnp.float32).T.astype(bf)

    ahead = 2
    for c in range(parts + 1):
        if c < parts:
            load_u[c].wait()
            halo_landed(x_first, c)
            if c >= slots:
                halo_sent(y_first, c - slots)
            blur_x(send_a, x_back, c)
            halo_start(y_first, c)
            if c + slots < parts:
                load_u[c + slots].start()
        if c > 0:
            halo_landed(y_first, c - 1)
            load_p[c - 1].wait()
            blur_y(c - 1)
            store_one[c - 1].start()
            store_one[c - 1].wait()
            if c - 1 < ahead:
                start("f", c - 1)
            if c - 1 + slots < parts:
                load_p[c - 1 + slots].start()
    for c in range(parts):
        halo_sent(x_first, c)
        if c >= parts - slots:
            halo_sent(y_first, c)

    for copy in eigen_copies:
        copy.wait()
    row = all_x[me_y // halves, lax.rem(me_y, halves)][:1]
    column = jnp.broadcast_to(row, (share, share)).T
    for b in range(0, full_y, share):
        eigen_xy[:, pl.ds(b, share)] = column * rows_y[:1, pl.ds(b, share)]
    for step in range(parts + 2):
        c = step
        if c < parts:
            landed("f", c)
            if c + ahead < parts:
                start("f", c + ahead)
            if c >= slots:
                sent("g", c - slots)
            along_x(x_fwd, lines_x, send_a, c)
            start("g", c)
        c = step - 1
        if 0 <= c < parts:
            landed("g", c)
            if c >= slots:
                sent("h", c - slots)
            along_y(c)
            start("h", c)
        c = step - 2
        if 0 <= c < parts:
            landed("h", c)
            if c >= slots:
                sent("b", c - slots)
            along_x(x_inv, lines_back, send_c, c)
            start("b", c)
    for c in range(parts):
        sent("f", c)
        if c >= parts - slots:
            sent("g", c)
            sent("h", c)

    x_last = x_halo(section_six, (found_rest.at[0], found_rest.at[1]), us, ur)
    y_last = y_halo((left_out, right_out), vs, vr)
    load_s = [local(whole(section_six, c), send_a.at[c % slots], 3, c) for c in range(parts)]
    store_a = [local(along.at[c % slots], whole(spread_out, c), 4, c) for c in range(parts)]
    empty = [
        pltpu.make_async_copy(ref, out, loads.at[5, n])
        for n, (ref, out) in enumerate(((from_left, left_out), (from_right, right_out)))
    ]
    for there, copy in zip(has[2:], empty):

        @pl.when(jnp.logical_not(there))
        def _():
            copy.start()

    for c in range(parts + 1):
        if c < parts:
            if c >= parts - slots:
                sent("b", c)
            landed("b", c)
            load_s[c].start()
            load_s[c].wait()
            pack_rest(send_a, c)
            halo_start(x_last, c)
        if c > 0:
            d = c - 1
            halo_landed(x_last, d)
            if d >= slots:
                halo_sent(y_last, d - slots)
                store_a[d - slots].wait()
            blur_x(send_a, x_band, d)
            halo_start(y_last, d)
            store_a[d].start()
    for c in range(parts):
        halo_landed(y_last, c)
        halo_sent(x_last, c)
        if c >= parts - slots:
            halo_sent(y_last, c)
            store_a[c].wait()
    for there, copy in zip(has[2:], empty):

        @pl.when(jnp.logical_not(there))
        def _():
            copy.wait()


def transform(
    weighted, plain, first_rest, last_rest,
    x_back, x_band, y_back, rim_select, x_inv, y_fwd, rows_x, rows_y, eigen_z,
    size_x, size_y,
):
    depth, quads, block_x, block_y = weighted.shape
    full_x, full_y = x_inv.shape[0], y_fwd.shape[0]
    share = full_x // size_y
    parts = PARTS
    part = depth // parts
    slots = 2
    vmem = pl.BlockSpec(memory_space=pltpu.VMEM)
    hbm = pl.BlockSpec(memory_space=pl.ANY)
    sem = lambda n: pltpu.SemaphoreType.DMA((parts, n))
    one = pltpu.SemaphoreType.DMA((parts,))
    bf = jnp.bfloat16
    modes = jax.ShapeDtypeStruct(weighted.shape, bf)
    side = jax.ShapeDtypeStruct((depth, block_x, block_y), bf)
    chunk = pltpu.VMEM((slots, part, quads, block_x, block_y), bf)
    edge = pltpu.VMEM((depth, quads, NEAR, block_y), bf)
    rest = pltpu.VMEM((depth, quads * REST, block_y), bf)
    return pl.pallas_call(
        functools.partial(transform_kernel, parts, size_x, size_y),
        out_shape=[modes, modes, modes, side, side],
        in_specs=[hbm] * 4 + [vmem] * 8 + [pl.BlockSpec(memory_space=pltpu.SMEM)],
        out_specs=[hbm] * 5,
        scratch_shapes=[
            pltpu.VMEM((depth, full_x, block_y), bf),
            pltpu.VMEM((depth, share, full_y), bf),
            pltpu.VMEM((depth, full_x, block_y), bf),
            chunk,
            pltpu.VMEM((slots, part, share, full_y), bf),
            chunk,
            pltpu.VMEM((2 * share, full_y), bf),
            chunk,
            edge, edge, rest, rest,
            pltpu.VMEM((2, depth, quads * REST, block_y), bf),
            pltpu.VMEM((slots, 2, part, block_x, block_y), bf),
            pltpu.VMEM(side.shape, bf), pltpu.VMEM(side.shape, bf),
            pltpu.VMEM((full_x, full_x), bf),
            pltpu.VMEM((share, full_y), jnp.float32),
            pltpu.VMEM((size_x,) + rows_x.shape, jnp.float32),
            sem(size_x), sem(size_x), sem(size_y), sem(size_y),
            sem(size_y), sem(size_y), sem(size_x), sem(size_x),
            one, one, one, one,
            sem(4), sem(4), sem(2), sem(2), sem(4), sem(4), sem(2), sem(2),
            pltpu.SemaphoreType.DMA((6, parts)),
            pltpu.SemaphoreType.DMA((size_x,)), pltpu.SemaphoreType.DMA((size_x,)),
        ],
        compiler_params=pltpu.CompilerParams(
            collective_id=0, has_side_effects=True, vmem_limit_bytes=62 * 2**20
        ),
    )(
        weighted, plain, first_rest, last_rest,
        x_back, x_band, y_back, rim_select, x_inv, y_fwd, rows_x, rows_y, eigen_z,
    )


def blur_x_lines(lines, low, high, band, along, to_right, to_left, rim_select):
    half = lines[0].shape[1]
    for q in range(0, len(lines), 2):
        both = jnp.concatenate(
            [jnp.concatenate([low[p], lines[p], high[p]], axis=0) for p in (q, q + 1)], axis=1
        )
        found = jnp.dot(band[...], both, preferred_element_type=jnp.float32).astype(jnp.bfloat16)
        along[q] = found[:, :half]
        along[q + 1] = found[:, half:]
    pack_rims([along[q] for q in range(len(lines))], to_right, to_left, rim_select)


def pack_rims(lines, to_right, to_left, rim_select):
    half = lines[0].shape[1]
    found = jnp.dot(
        jnp.concatenate(lines, axis=1), rim_select[...], preferred_element_type=jnp.float32
    ).astype(jnp.bfloat16)
    to_left[...] = found[:, half:]
    to_right[...] = found[:, :half]


BAND_ROWS = 16
QUADS = 4
RIM_ROWS = 32
NEAR = 16
REST = HALF + SHIFT - NEAR
SIXES = 6


def to_modes_kernel(matrix, source, first, second, held):
    rows, depth = source.shape[0], source.shape[2]
    for x in range(0, rows, 2):
        lines = source[pl.ds(x, 2)].reshape(2 * source.shape[1], depth).astype(jnp.bfloat16)
        found = lax.dot_general(
            matrix[...], lines, (((1,), (1,)), ((), ())), preferred_element_type=jnp.float32
        )
        held[:, x, :] = found[:, : source.shape[1]]
        held[:, x + 1, :] = found[:, source.shape[1] :]
    full = depth // SIXES
    first[:full] = held[: full * SIXES].reshape((full,) + first.shape[1:]).astype(first.dtype)
    left = depth - full * SIXES
    first[full, :left] = held[full * SIXES : depth].astype(first.dtype)
    first[full, left:] = jnp.zeros((SIXES - left,) + first.shape[2:], first.dtype)
    groups = second.shape[0]
    for q in range(QUADS):
        second[:, q] = held[pl.ds(depth + q * groups, groups)].astype(second.dtype)


def modes_block(rows, shape):
    return pl.BlockSpec((shape[0], shape[1], rows, shape[3]), lambda i: (0, 0, i, 0))


def space_block(rows, shape):
    return pl.BlockSpec((rows, shape[1], shape[2]), lambda i: (i, 0, 0))


def whole_block(shape):
    return pl.BlockSpec(shape, lambda i: (0,) * len(shape))


def to_modes(source, matrix):
    block_x, block_y, depth = source.shape
    shapes = [
        (depth // SIXES + 1, SIXES, block_x, block_y), (depth // QUADS, QUADS, block_x, block_y)
    ]
    return pl.pallas_call(
        to_modes_kernel,
        grid=(block_x // BAND_ROWS,),
        out_shape=[jax.ShapeDtypeStruct(shape, jnp.bfloat16) for shape in shapes],
        in_specs=[whole_block(matrix.shape), space_block(BAND_ROWS, source.shape)],
        out_specs=[modes_block(BAND_ROWS, shape) for shape in shapes],
        scratch_shapes=[pltpu.VMEM((2 * depth, BAND_ROWS, block_y), jnp.float32)],
        compiler_params=pltpu.CompilerParams(vmem_limit_bytes=60 * 2**20),
    )(matrix, source)


def spread_kernel(
    size_x, size_y, parts, source, x_band, rim_select, along, from_left, from_right,
    low, high, right, left, xs, xr, ys, yr,
):
    me_x = lax.axis_index("gx")
    me_y = lax.axis_index("gy")
    block_x = source.shape[2]
    groups = source.shape[0]
    part = groups // parts
    has = (me_x > 0, me_x < size_x - 1, me_y > 0, me_y < size_y - 1)
    peers = ((me_x - 1, me_y), (me_x + 1, me_y), (me_x, me_y - 1), (me_x, me_y + 1))

    barrier = pltpu.get_barrier_semaphore()
    for peer in (
        (lax.rem(me_x + 1, size_x), me_y), (lax.rem(me_x + size_x - 1, size_x), me_y),
        (me_x, lax.rem(me_y + 1, size_y)), (me_x, lax.rem(me_y + size_y - 1, size_y)),
    ):
        pl.semaphore_signal(barrier, inc=1, device_id=peer, device_id_type=MESH_ID)
    pl.semaphore_wait(barrier, 4)

    def x_copy(c, way):
        here = pl.ds(c * part, part)
        if way == 0:
            src, dst = source.at[here, :, pl.ds(0, RIM_ROWS)], high.at[here]
        else:
            src = source.at[here, :, pl.ds(block_x - RIM_ROWS, RIM_ROWS)]
            dst = low.at[here]
        return pltpu.make_async_remote_copy(
            src, dst, xs.at[c, way], xr.at[c, way], device_id=peers[way], device_id_type=MESH_ID
        )

    def y_copy(c, way):
        here = pl.ds(c * part, part)
        if way == 0:
            src, dst = left.at[here], from_right.at[here]
        else:
            src, dst = right.at[here], from_left.at[here]
        return pltpu.make_async_remote_copy(
            src, dst, ys.at[c, way], yr.at[c, way], device_id=peers[2 + way],
            device_id_type=MESH_ID,
        )

    for c in range(parts):
        for way in range(2):

            @pl.when(has[way])
            def _():
                x_copy(c, way).start()

    for there, ref in zip(has, (low, high, from_left, from_right)):

        @pl.when(jnp.logical_not(there))
        def _():
            ref[...] = jnp.zeros_like(ref)

    def blur_x(c):
        def step(i, carry):
            g = c * part + i
            blur_x_lines(
                [source[g, q] for q in range(source.shape[1])], low.at[g], high.at[g], x_band,
                along.at[g], right.at[g], left.at[g], rim_select,
            )
            return carry

        lax.fori_loop(0, part, step, 0)

    for c in range(parts):
        for way in range(2):

            @pl.when(has[1 - way])
            def _():
                x_copy(c, way).wait_recv()

        blur_x(c)
        for way in range(2):

            @pl.when(has[2 + way])
            def _():
                y_copy(c, way).start()

    for c in range(parts):
        for way in range(2):

            @pl.when(has[3 - way])
            def _():
                y_copy(c, way).wait_recv()

            @pl.when(has[way])
            def _():
                x_copy(c, way).wait_send()

            @pl.when(has[2 + way])
            def _():
                y_copy(c, way).wait_send()


def spread(source, x_band, rim_select, size_x, size_y, number):
    groups, quads, block_x, block_y = source.shape
    bf = jnp.bfloat16
    whole = jax.ShapeDtypeStruct(source.shape, bf)
    rims = jax.ShapeDtypeStruct((groups, block_x, block_y), bf)
    vmem = pl.BlockSpec(memory_space=pltpu.VMEM)
    edge = pltpu.VMEM((groups, quads, RIM_ROWS, block_y), bf)
    packed = pltpu.VMEM(rims.shape, bf)
    sem = pltpu.SemaphoreType.DMA((groups // 2, 2))
    return pl.pallas_call(
        functools.partial(spread_kernel, size_x, size_y, groups // 2),
        out_shape=[whole, rims, rims],
        in_specs=[vmem] * 3,
        out_specs=[vmem] * 3,
        scratch_shapes=[edge, edge, packed, packed, sem, sem, sem, sem],
        compiler_params=pltpu.CompilerParams(
            collective_id=number, has_side_effects=True, vmem_limit_bytes=56 * 2**20
        ),
    )(source, x_band, rim_select)


def blur_y_rows(along, from_left, from_right, y_band, put):
    groups, quads, rows, block_y = along.shape
    count = groups * rows
    sides = [from_left[...].reshape(count, block_y), from_right[...].reshape(count, block_y)]
    for q in range(quads):
        wide = jnp.concatenate([along[:, q].reshape(count, block_y)] + sides, axis=1)
        found = jnp.dot(wide, y_band[q], preferred_element_type=jnp.float32)
        put(q, found.reshape(groups, rows, block_y))


def misfit_kernel(
    along, from_left, from_right, observed, confidence, y_band, matrix,
    misfit, weighted, first_rest, last_rest, held, turned_back,
):
    def put(s, found):
        for r in range(found.shape[0]):
            held[r * SIXES + s] = found[r]

    blur_y_rows(along, from_left, from_right, y_band, put)
    depth = observed.shape[2]
    for x in range(observed.shape[0]):
        found = observed[x].astype(jnp.float32) - held[:depth, x, :].T
        misfit[x] = found
        lines = (confidence[x].astype(jnp.float32) * found).astype(jnp.bfloat16)
        turned_back[:, x, :] = lax.dot_general(
            matrix[...], lines, (((1,), (1,)), ((), ())), preferred_element_type=jnp.float32
        )
    groups = weighted.shape[0]
    for q in range(QUADS):
        weighted[:, q] = turned_back[pl.ds(q * groups, groups)].astype(weighted.dtype)

    def rest(row):
        return jnp.concatenate(
            [turned_back[pl.ds(q * groups, groups), pl.ds(row, REST)] for q in range(QUADS)],
            axis=1,
        ).astype(weighted.dtype)

    @pl.when(pl.program_id(0) == 1)
    def _():
        first_rest[...] = rest(0)

    @pl.when(pl.program_id(0) == pl.num_programs(0) - 2)
    def _():
        last_rest[...] = rest(BAND_ROWS - REST)


def find_misfit(along, from_left, from_right, observed, confidence, y_band, matrix):
    shape, space = along.shape, observed.shape
    modes = (space[2] // QUADS, QUADS, shape[2], shape[3])
    rest = (modes[0], QUADS * REST, shape[3])
    rims = pl.BlockSpec((shape[0], BAND_ROWS, shape[3]), lambda i: (0, i, 0))
    held = pltpu.VMEM((shape[0] * SIXES, BAND_ROWS, shape[3]), jnp.float32)
    turned = pltpu.VMEM((space[2], BAND_ROWS, shape[3]), jnp.float32)
    return pl.pallas_call(
        misfit_kernel,
        grid=(shape[2] // BAND_ROWS,),
        out_shape=[
            jax.ShapeDtypeStruct(space, jnp.float32),
            jax.ShapeDtypeStruct(modes, jnp.bfloat16),
            jax.ShapeDtypeStruct(rest, jnp.bfloat16),
            jax.ShapeDtypeStruct(rest, jnp.bfloat16),
        ],
        in_specs=[
            modes_block(BAND_ROWS, shape), rims, rims,
            space_block(BAND_ROWS, space), space_block(BAND_ROWS, space),
            whole_block(y_band.shape), whole_block(matrix.shape),
        ],
        out_specs=[
            space_block(BAND_ROWS, space), modes_block(BAND_ROWS, modes),
            whole_block(rest), whole_block(rest),
        ],
        scratch_shapes=[held, turned],
        compiler_params=pltpu.CompilerParams(vmem_limit_bytes=60 * 2**20),
    )(along, from_left, from_right, observed, confidence, y_band, matrix)


def folded(values):
    return jnp.sum(values.reshape(-1, 8, values.shape[-1]), axis=0)


def direction_kernel(
    along, from_left, from_right, section_six, section_one, confidence, y_band, basis, blurring,
    direction, blurred, sums, held, held_six,
):
    @pl.when(pl.program_id(0) == 0)
    def _():
        sums[...] = jnp.zeros_like(sums)

    def put(q, found):
        held[pl.ds(q * found.shape[0], found.shape[0])] = found

    blur_y_rows(along, from_left, from_right, y_band, put)
    six = section_six[...].astype(jnp.float32)
    sums[0] += folded((six * section_one[...].astype(jnp.float32)).reshape(-1, six.shape[-1]))
    groups = six.shape[0]
    for q in range(QUADS):
        held_six[pl.ds(q * groups, groups)] = six[:, q]
    for x in range(confidence.shape[0]):
        lines = held_six[:, x, :].T.astype(jnp.bfloat16)
        found = jnp.dot(lines, basis[...], preferred_element_type=jnp.float32)
        direction[x] = found
        sums[2] += folded(found * found)
        lines = held[:, x, :].T.astype(jnp.bfloat16)
        found = jnp.dot(
            jnp.concatenate([lines, lines], axis=1), blurring[...],
            preferred_element_type=jnp.float32,
        )
        blurred[x] = found
        sums[1] += folded(confidence[x].astype(jnp.float32) * found * found)


def find_direction(
    along, from_left, from_right, section_six, section_one, confidence, y_band, basis, blurring
):
    shape, space = along.shape, confidence.shape
    rims = pl.BlockSpec((shape[0], BAND_ROWS, shape[3]), lambda i: (0, i, 0))
    held = pltpu.VMEM((space[2], BAND_ROWS, shape[3]), jnp.float32)
    sums = (8, 8, space[2])
    return pl.pallas_call(
        direction_kernel,
        grid=(shape[2] // BAND_ROWS,),
        out_shape=[
            jax.ShapeDtypeStruct(space, jnp.float32),
            jax.ShapeDtypeStruct(space, jnp.float32),
            jax.ShapeDtypeStruct(sums, jnp.float32),
        ],
        in_specs=[
            modes_block(BAND_ROWS, shape), rims, rims,
            modes_block(BAND_ROWS, shape), modes_block(BAND_ROWS, shape),
            space_block(BAND_ROWS, space),
            whole_block(y_band.shape), whole_block(basis.shape), whole_block(blurring.shape),
        ],
        out_specs=[
            space_block(BAND_ROWS, space), space_block(BAND_ROWS, space), whole_block(sums),
        ],
        scratch_shapes=[held, held],
        compiler_params=pltpu.CompilerParams(vmem_limit_bytes=60 * 2**20),
    )(
        along, from_left, from_right, section_six, section_one, confidence, y_band, basis, blurring
    )


def total_kernel(size_x, size_y, values, total, from_x, from_y, held, sx, rx, sy, ry):
    me_x = lax.axis_index("gx")
    me_y = lax.axis_index("gy")
    x_peers = [(lax.rem(me_x + s, size_x), me_y) for s in range(1, size_x)]
    y_peers = [(me_x, lax.rem(me_y + s, size_y)) for s in range(1, size_y)]
    barrier = pltpu.get_barrier_semaphore()
    for peer in x_peers + y_peers:
        pl.semaphore_signal(barrier, inc=1, device_id=peer, device_id_type=MESH_ID)
    pl.semaphore_wait(barrier, size_x + size_y - 2)

    def gather(source, landing, peers, sends, receives):
        copies = [
            pltpu.make_async_remote_copy(
                source, landing.at[s], sends.at[s], receives.at[s],
                device_id=peer, device_id_type=MESH_ID,
            )
            for s, peer in enumerate(peers)
        ]
        for copy in copies:
            copy.start()
        for copy in copies:
            copy.wait()
        return source[...] + jnp.sum(landing[...], axis=0)

    held[...] = jnp.sum(values[...], axis=1)
    held[...] = gather(held, from_x, x_peers, sx, rx)
    total[...] = gather(held, from_y, y_peers, sy, ry)


def total_sums(sums, size_x, size_y, number):
    lanes = sums.shape[2]
    vmem = pl.BlockSpec(memory_space=pltpu.VMEM)
    sem = lambda n: pltpu.SemaphoreType.DMA((n - 1,))
    f32 = jnp.float32
    return pl.pallas_call(
        functools.partial(total_kernel, size_x, size_y),
        out_shape=jax.ShapeDtypeStruct((8, lanes), f32),
        in_specs=[vmem],
        out_specs=vmem,
        scratch_shapes=[
            pltpu.VMEM((size_x - 1, 8, lanes), f32),
            pltpu.VMEM((size_y - 1, 8, lanes), f32),
            pltpu.VMEM((8, lanes), f32),
            sem(size_x), sem(size_x), sem(size_y), sem(size_y),
        ],
        compiler_params=pltpu.CompilerParams(collective_id=number, has_side_effects=True),
    )(sums)


def x_bands(kernel, offset, block_x):
    rim = HALF + SHIFT
    band = band_matrix(kernel, offset, block_x, block_x + 2 * rim, rim)
    stacks = []
    for q in range(QUADS):
        pads = ((0, 0), (q * REST, (QUADS - 1 - q) * REST))
        stacks.append(
            jnp.concatenate(
                [
                    band[:, REST:rim], jnp.pad(band[:, :REST], pads), band[:, rim:-rim],
                    band[:, -rim:-REST], jnp.pad(band[:, -REST:], pads),
                ],
                axis=1,
            )
        )
    return jnp.stack(stacks).astype(jnp.bfloat16)


def y_bands(kernel, offset, block_y, count):
    rim = HALF + SHIFT
    band = band_matrix(kernel, offset, block_y, block_y + 2 * rim, rim).T
    stacks = []
    for q in range(count):
        before = q * (block_y // count)
        pads = ((before, block_y - before - rim), (0, 0))
        stacks.append(
            jnp.concatenate(
                [band[rim:-rim], jnp.pad(band[:rim], pads), jnp.pad(band[-rim:], pads)], axis=0
            )
        )
    return jnp.stack(stacks).astype(jnp.bfloat16)


def rim_selects(block_y, count):
    rim = HALF + SHIFT
    row = lax.broadcasted_iota(jnp.int32, (count * block_y, block_y), 0)
    lane = lax.broadcasted_iota(jnp.int32, (count * block_y, block_y), 1)
    width = block_y // count
    same = row // block_y == lane // width
    place = lane % width
    within = jnp.logical_and(same, place < rim)
    spot = row % block_y
    right = jnp.logical_and(within, spot == block_y - rim + place)
    left = jnp.logical_and(within, spot == place)
    return jnp.concatenate([right, left], axis=1).astype(jnp.bfloat16)


def kernel_shards(
    observed, confidence, iterate, kernel_bank, tap_index, offsets,
    basis_x, basis_y, basis_z, eigen_x, eigen_y, eigen_z,
):
    size_x, size_y = lax.axis_size("gx"), lax.axis_size("gy")
    block_x, block_y, depth = iterate.shape
    bf = jnp.bfloat16
    kernels = kernels_of(kernel_bank, tap_index)
    adjoint = kernels[:, ::-1]
    full_x = lax.all_gather(basis_x, "gx", axis=0, tiled=True)
    full_y = lax.all_gather(basis_y, "gy", axis=0, tiled=True)
    share_x = block_x * size_x // size_y
    rows_x = jnp.broadcast_to(eigen_x.reshape(-1, 1, share_x), (block_x // share_x, 8, share_x))
    rows_y = jnp.broadcast_to(eigen_y[None, :], (8, eigen_y.shape[0]))
    wide_x = block_x + 2 * RIM_ROWS
    x_band = band_matrix(kernels[0], offsets[0], block_x, wide_x, RIM_ROWS).astype(bf)
    x_bands_back = x_bands(adjoint[0], -offsets[0], block_x)
    x_bands_on = x_bands(kernels[0], offsets[0], block_x)
    y_first = y_bands(kernels[1], offsets[1], block_y, SIXES)
    y_band = y_bands(kernels[1], offsets[1], block_y, QUADS)
    y_back = y_bands(adjoint[1], -offsets[1], block_y, QUADS)
    z_band = band_matrix(kernels[2], offsets[2], depth, depth, 0)
    rim_select = rim_selects(block_y, QUADS)
    basis_f = basis_z.astype(jnp.float32)
    blurring = jnp.dot(z_band, basis_f, precision=highest)
    entry = jnp.concatenate([z_band.astype(bf), basis_z.T], axis=0)

    along_z, plain = to_modes(iterate, entry)
    rims = spread(along_z, x_band, rim_selects(block_y, SIXES), size_x, size_y, 1)
    misfit, weighted, *rests = find_misfit(
        *rims, observed, confidence, y_first, blurring.T.astype(bf)
    )
    section_one, section_six, *rims = transform(
        weighted, plain, *rests, x_bands_back, x_bands_on, y_back, rim_select, full_x, full_y,
        rows_x, rows_y, eigen_z, size_x, size_y,
    )
    coarse = blurring.T.astype(bf)
    fine = (blurring.T - coarse.astype(jnp.float32)).astype(bf)
    direction, blurred, sums = find_direction(
        *rims, section_six, section_one, confidence, y_band, basis_z.T,
        jnp.concatenate([coarse, fine], axis=0),
    )
    totals = jnp.sum(total_sums(sums, size_x, size_y, 2), axis=1)
    step_size = totals[0] / (totals[1] + tikhonov * totals[2])
    return (iterate + step_size * direction, misfit - step_size * blurred)


def kernels_fit(block, size_x, size_y):
    block_x, block_y, depth = block
    return (
        block_y == 128
        and depth == 128
        and block_x == 256
        and depth // size_x == 32
        and block_x * size_x // size_y == 128
        and block_y * size_y % 256 == 0
    )


def step_shards(*arrays):
    fits = kernels_fit(arrays[2].shape, lax.axis_size("gx"), lax.axis_size("gy"))
    return (kernel_shards if fits else shards)(*arrays)


def solution(mesh):
    return jax.shard_map(
        step_shards,
        mesh=mesh,
        in_specs=(
            P("gx", "gy", None),
            P("gx", "gy", None),
            P("gx", "gy", None),
            P(),
            P(),
            P(),
            P("gx", None),
            P("gy", None),
            P(),
            P("gx"),
            P(),
            P(),
        ),
        out_specs=(P("gx", "gy", None), P("gx", "gy", None)),
        check_vma=False,
    )
```

```python
import functools

import jax
import jax.numpy as jnp
from jax import lax
from jax.experimental import pallas as pl
from jax.experimental.pallas import tpu as pltpu
from jax.sharding import PartitionSpec as P

HALF = 16
SHIFT = 4
CHUNKS = 2


highest = lax.Precision.HIGHEST
tikhonov = 0.002


def exchange(block, axis, dim, width):
    count = lax.axis_size(axis)
    forward = [(i, i + 1) for i in range(count - 1)]
    backward = [(target, source) for source, target in forward]
    low = lax.ppermute(
        lax.slice_in_dim(block, block.shape[dim] - width, None, axis=dim), axis, forward
    )
    high = lax.ppermute(lax.slice_in_dim(block, 0, width, axis=dim), axis, backward)
    return low, high


def kernels_of(kernel_bank, tap_index):
    entries = jnp.arange(kernel_bank.shape[1], dtype=jnp.int32)
    chosen = tap_index[:, :, None] == entries[None, None, :]
    raw_taps = jnp.sum(jnp.where(chosen, kernel_bank[:, None, :], 0.0), axis=2)
    return raw_taps / jnp.sum(raw_taps, axis=1, keepdims=True)


def band_matrix(kernel, offset, out_count, in_count, margin):
    center = (kernel.shape[0] - 1) // 2
    row_pos = lax.broadcasted_iota(jnp.int32, (out_count, in_count), 0)
    col_pos = lax.broadcasted_iota(jnp.int32, (out_count, in_count), 1)
    position = col_pos - row_pos - margin + center - offset
    tap_ids = jnp.arange(kernel.shape[0], dtype=jnp.int32)
    chosen = position[None, :, :] == tap_ids[:, None, None]
    return jnp.sum(jnp.where(chosen, kernel[:, None, None], 0.0), axis=0)


def split_dot(spec, matrix, block):
    return jnp.einsum(spec, matrix, block.astype(jnp.float32), precision=lax.Precision.HIGH)


def turned(array, axis_name, dim, sign):
    count = lax.axis_size(axis_name)
    size = array.shape[dim] // count
    mine = lax.axis_index(axis_name)
    pieces = [
        lax.dynamic_slice_in_dim(array, lax.rem(mine + sign * step + count, count) * size, size, dim)
        for step in range(count)
    ]
    return jnp.concatenate(pieces, axis=dim)


def swap(block, axis_name, split, concat, sign):
    count = lax.axis_size(axis_name)
    pieces = jnp.split(block, count, axis=split)
    arrived = [pieces[0]]
    for step in range(1, count):
        pairs = [(i, (i + sign * step) % count) for i in range(count)]
        arrived.append(lax.ppermute(pieces[step], axis_name, pairs))
    return jnp.concatenate(arrived, axis=concat)


def blur_xy(along_z, kernels, offsets):
    rim = HALF + SHIFT
    block_x, block_y, _ = along_z.shape
    x_matrix = band_matrix(kernels[0], offsets[0], block_x, block_x + 2 * rim, rim)
    y_matrix = band_matrix(kernels[1], offsets[1], block_y, block_y + 2 * rim, rim)
    low, high = exchange(along_z, "gx", 0, rim)
    extended = jnp.concatenate([low, along_z, high], axis=0)
    along_x = split_dot("ic,cyz->iyz", x_matrix, extended).astype(jnp.bfloat16)
    low, high = exchange(along_x, "gy", 1, rim)
    inner = split_dot("jc,xcz->xjz", y_matrix[:, rim:-rim], along_x)
    rims = jnp.concatenate([low, high], axis=1)
    rim_matrix = jnp.concatenate([y_matrix[:, :rim], y_matrix[:, -rim:]], axis=1)
    return inner + split_dot("jc,xcz->xjz", rim_matrix, rims)


def apply_blur(source, kernels, offsets):
    depth = source.shape[2]
    z_matrix = band_matrix(kernels[2], offsets[2], depth, depth, 0)
    along_z = jnp.einsum("xyc,zc->xyz", source, z_matrix, precision=lax.Precision.HIGH)
    return blur_xy(along_z.astype(jnp.bfloat16), kernels, offsets)


def shards(
    observed,
    confidence,
    iterate,
    kernel_bank,
    tap_index,
    offsets,
    basis_x,
    basis_y,
    basis_z,
    eigen_x,
    eigen_y,
    eigen_z,
):
    kernels = kernels_of(kernel_bank, tap_index)
    adjoint_kernels = kernels[:, ::-1]
    weights = confidence.astype(jnp.float32)
    misfit = observed.astype(jnp.float32) - apply_blur(iterate, kernels, offsets)
    gradient = apply_blur(weights * misfit, adjoint_kernels, -offsets) - tikhonov * iterate
    full_x = lax.all_gather(basis_x, "gx", axis=0, tiled=True)
    full_y = lax.all_gather(basis_y, "gy", axis=0, tiled=True)

    gradient_b = gradient.astype(jnp.bfloat16)
    gx_size = lax.axis_size("gx")
    depth = basis_z.shape[0]
    share_z = depth // gx_size
    chunks = min(CHUNKS, share_z)
    part = share_z // chunks
    z_ahead = turned(basis_z, "gx", 1, 1).reshape(depth, gx_size, chunks, part)
    eigen_part = lax.dynamic_slice_in_dim(eigen_z, lax.axis_index("gx") * share_z, share_z)
    all_x = lax.all_gather(eigen_x, "gx", axis=0, tiled=True)
    share_x = all_x.shape[0] // lax.axis_size("gy")
    part_x = lax.dynamic_slice_in_dim(all_x, lax.axis_index("gy") * share_x, share_x)
    x_rows_behind = turned(full_x, "gx", 0, -1)
    x_ahead = turned(x_rows_behind, "gy", 1, 1)
    x_return = turned(turned(full_x, "gx", 0, 1), "gy", 1, -1)
    y_behind = turned(full_y, "gy", 0, -1)
    y_ahead = turned(full_y, "gy", 0, 1)
    found = []
    for chunk in range(chunks):
        modes = z_ahead[:, :, chunk].reshape(depth, gx_size * part)
        section_one = jnp.einsum(
            "zk,xyz->kxy", modes, gradient_b, preferred_element_type=jnp.float32
        ).astype(jnp.bfloat16)
        lines = swap(section_one, "gx", 0, 1, 1)
        section_two = jnp.einsum(
            "xj,kxy->kjy", x_ahead, lines, preferred_element_type=jnp.float32
        ).astype(jnp.bfloat16)
        lines = swap(section_two, "gy", 1, 2, 1)
        part_z = eigen_part[chunk * part : (chunk + 1) * part]
        inverse = 1.0 / (
            part_x[None, :, None] * eigen_y[None, None, :] * part_z[:, None, None] + tikhonov
        )
        section_four = (
            jnp.einsum("axy,yk->axk", lines, y_behind, preferred_element_type=jnp.float32)
            * inverse
        ).astype(jnp.bfloat16)
        section_five = jnp.einsum(
            "axk,jk->axj", section_four, y_ahead, preferred_element_type=jnp.float32
        ).astype(jnp.bfloat16)
        lines = swap(section_five, "gy", 2, 1, 1)
        section_six = jnp.einsum(
            "jx,kxy->kjy", x_return, lines, preferred_element_type=jnp.float32
        ).astype(jnp.bfloat16)
        found.append(swap(section_six, "gx", 1, 0, 1))
    section_six = jnp.concatenate(found, axis=0)
    basis_z = (
        turned(basis_z, "gx", 1, -1)
        .reshape(depth, gx_size, chunks, part)
        .transpose(0, 2, 1, 3)
        .reshape(depth, depth)
    )
    direction = jnp.einsum("kxy,zk->xyz", section_six, basis_z, preferred_element_type=jnp.float32)
    z_matrix = band_matrix(kernels[2], offsets[2], depth, depth, 0)
    z_modes = jnp.dot(z_matrix, basis_z.astype(jnp.float32), precision=highest)
    along_z = jnp.einsum(
        "kxy,zk->xyz", section_six.astype(jnp.float32), z_modes, precision=lax.Precision.HIGH
    ).astype(jnp.bfloat16)
    local_descent = jnp.sum(gradient * direction)
    descent = lax.psum(local_descent, ("gx", "gy"))
    blurred = blur_xy(along_z, kernels, offsets)
    data_sum, norm_sum = lax.psum(
        (jnp.sum(weights * blurred * blurred), jnp.sum(direction * direction)), ("gx", "gy")
    )
    energy = data_sum + tikhonov * norm_sum
    step_size = descent / energy
    return (iterate + step_size * direction, misfit - step_size * blurred)


MESH_ID = pl.DeviceIdType.MESH
PARTS = 8


def transform_kernel(
    parts, size_x, size_y,
    weighted, plain, first_rest, last_rest,
    x_back, x_band, y_band, rim_select, x_inv, y_fwd, rows_x, rows_y, eigen_z,
    section_one, section_six, spread_out, left_out, right_out,
    lines_x, lines_y, lines_back, send_a, send_b, send_c, modes, along, low, high, low_rest, high_rest,
    found_rest, rims,
    from_left, from_right, x_fwd, eigen_xy, all_x,
    fs, fr, gs, gr, hs, hr, bs, br, fl, gl, hl, bl, xs, xr, ys, yr, us, ur, vs, vr, loads, es, er,
):
    me_x = lax.axis_index("gx")
    me_y = lax.axis_index("gy")
    depth, full = lines_x.shape[0], lines_x.shape[1]
    block_y = lines_x.shape[2]
    block_x = section_one.shape[2]
    share, full_y = lines_y.shape[1], lines_y.shape[2]
    part = depth // parts
    slots = send_a.shape[0]
    halves = block_x // share
    bf = jnp.bfloat16

    barrier = pltpu.get_barrier_semaphore()
    for step in range(1, size_x):
        pl.semaphore_signal(
            barrier, inc=1, device_id=(lax.rem(me_x + step, size_x), me_y), device_id_type=MESH_ID
        )
    for step in range(1, size_y):
        pl.semaphore_signal(
            barrier, inc=1, device_id=(me_x, lax.rem(me_y + step, size_y)), device_id_type=MESH_ID
        )
    pl.semaphore_wait(barrier, size_x + size_y - 2)

    has = (me_x > 0, me_x < size_x - 1, me_y > 0, me_y < size_y - 1)
    peers = ((me_x - 1, me_y), (me_x + 1, me_y), (me_x, me_y - 1), (me_x, me_y + 1))

    def remote(src, dst, send, receive, peer):
        return pltpu.make_async_remote_copy(
            src, dst, send, receive, device_id=peer, device_id_type=MESH_ID
        )

    def x_halo(source, rests, sends, receives):
        def copies_of(c, way):
            here = pl.ds(c * part, part)
            if way == 0:
                near = source.at[here, :, pl.ds(0, NEAR)], high.at[here]
                rest = rests[0].at[here], high_rest.at[here]
            else:
                near = source.at[here, :, pl.ds(block_x - NEAR, NEAR)], low.at[here]
                rest = rests[1].at[here], low_rest.at[here]
            return [
                remote(*pair, sends.at[c, 2 * way + n], receives.at[c, 2 * way + n], peers[way])
                for n, pair in enumerate((near, rest))
            ]

        return copies_of, 0

    def y_halo(landing, sends, receives):
        def copies_of(c, way):
            src = rims.at[c % slots, 1 - way]
            dst = landing[1 - way].at[pl.ds(c * part, part)]
            return [remote(src, dst, sends.at[c, way], receives.at[c, way], peers[2 + way])]

        return copies_of, 2

    def halo_start(kind, c):
        copies_of, base = kind
        for way in range(2):

            @pl.when(has[base + way])
            def _():
                for copy in copies_of(c, way):
                    copy.start()

    def halo_landed(kind, c):
        copies_of, base = kind
        for way in range(2):

            @pl.when(has[base + 1 - way])
            def _():
                for copy in copies_of(c, way):
                    copy.wait_recv()

    def halo_sent(kind, c):
        copies_of, base = kind
        for way in range(2):

            @pl.when(has[base + way])
            def _():
                for copy in copies_of(c, way):
                    copy.wait_send()

    def local(source, target, kind, c):
        return pltpu.make_async_copy(source, target, loads.at[kind, c])

    def whole(ref, c):
        return ref.at[pl.ds(c * part, part)]

    def copies(kind, c):
        out = []
        here = pl.ds(c * part, part)
        slot = c % slots
        count = size_x if kind in "fb" else size_y
        for step in range(count):
            if kind in "fb":
                peer = lax.rem(me_x + step, size_x)
                target = (peer, me_y)
            else:
                peer = lax.rem(me_y + step, size_y)
                target = (me_x, peer)
            if kind == "f":
                src = section_one.at[here, peer]
                dst = lines_x.at[here, pl.ds(me_x * block_x, block_x)]
                sems = fs, fr, fl
            elif kind == "g":
                src = send_a.at[
                    slot, :, peer // halves, pl.ds(lax.rem(peer, halves) * share, share)
                ]
                dst = lines_y.at[here, :, pl.ds(me_y * block_y, block_y)]
                sems = gs, gr, gl
            elif kind == "h":
                src = send_b.at[slot, :, :, pl.ds(peer * block_y, block_y)]
                dst = lines_back.at[here, pl.ds(me_y * share, share)]
                sems = hs, hr, hl
            else:
                src = send_c.at[slot, :, peer]
                dst = section_six.at[here, me_x]
                sems = bs, br, bl
            if step == 0:
                out.append(pltpu.make_async_copy(src, dst, sems[2].at[c]))
            else:
                out.append(remote(src, dst, sems[0].at[c, step], sems[1].at[c, step], target))
        return out

    every = {kind: [copies(kind, c) for c in range(parts)] for kind in "fghb"}

    def start(kind, c):
        group = every[kind][c]
        for copy in group[1:] + group[:1]:
            copy.start()

    def landed(kind, c):
        group = every[kind][c]
        if kind != "b":
            group[0].wait()
        for copy in group[1:]:
            copy.wait_recv()

    def sent(kind, c):
        group = every[kind][c]
        if kind == "b":
            group[0].wait()
        for copy in group[1:]:
            copy.wait_send()

    def along_x(matrix, lines, out, c):
        def pair(i, carry):
            k = c * part + 2 * i
            both = jnp.concatenate([lines[k], lines[k + 1]], axis=1)
            for b in range(full // block_x):
                found = jnp.dot(
                    matrix[pl.ds(b * block_x, block_x), :], both,
                    preferred_element_type=jnp.float32,
                ).astype(bf)
                out[c % slots, 2 * i, b] = found[:, :block_y]
                out[c % slots, 2 * i + 1, b] = found[:, block_y:]
            return carry

        lax.fori_loop(0, part // 2, pair, 0)

    def along_y(c):
        def pair(i, carry):
            k = c * part + 2 * i
            rows = jnp.concatenate([lines_y[k], lines_y[k + 1]], axis=0)
            for b in range(0, full_y, 256):
                found = jnp.dot(rows, y_fwd[:, pl.ds(b, 256)], preferred_element_type=jnp.float32)
                weight = eigen_xy[:, pl.ds(b, 256)]
                modes[pl.ds(0, share), pl.ds(b, 256)] = (
                    found[:share] / (weight * eigen_z[me_x * depth + k] + tikhonov)
                ).astype(bf)
                modes[pl.ds(share, share), pl.ds(b, 256)] = (
                    found[share:] / (weight * eigen_z[me_x * depth + k + 1] + tikhonov)
                ).astype(bf)
            for b in range(0, full_y, 256):
                found = lax.dot_general(
                    modes[...], y_fwd[pl.ds(b, 256), :], (((1,), (1,)), ((), ())),
                    preferred_element_type=jnp.float32,
                ).astype(bf)
                send_b[c % slots, 2 * i, :, pl.ds(b, 256)] = found[:share]
                send_b[c % slots, 2 * i + 1, :, pl.ds(b, 256)] = found[share:]
            return carry

        lax.fori_loop(0, part // 2, pair, 0)

    def blur_x(source, band, c):
        slot = c % slots

        def step(i, carry):
            for q in range(QUADS):
                both = jnp.concatenate(
                    [
                        jnp.concatenate(
                            [
                                low[c * part + p, q], low_rest[c * part + p], source[slot, p, q],
                                high[c * part + p, q], high_rest[c * part + p],
                            ],
                            axis=0,
                        )
                        for p in (2 * i, 2 * i + 1)
                    ],
                    axis=1,
                )
                found = jnp.dot(band[q], both, preferred_element_type=jnp.float32).astype(bf)
                along[slot, 2 * i, q] = found[:, :block_y]
                along[slot, 2 * i + 1, q] = found[:, block_y:]
            for p in (2 * i, 2 * i + 1):
                pack_rims(
                    [along[slot, p, q] for q in range(QUADS)],
                    rims.at[slot, 0, p], rims.at[slot, 1, p], rim_select,
                )
            return carry

        lax.fori_loop(0, part // 2, step, 0)

    def pack_rest(source, c):
        def step(i, carry):
            for n, row, skip in ((0, NEAR, 0), (1, block_x - 2 * NEAR, NEAR - REST)):
                lines = [
                    source[c % slots, i, q, pl.ds(row, NEAR)].astype(jnp.float32)[
                        skip : skip + REST
                    ]
                    for q in range(QUADS)
                ]
                found_rest[n, c * part + i] = jnp.concatenate(lines, axis=0).astype(bf)
            return carry

        lax.fori_loop(0, part, step, 0)

    def blur_y(c):
        some = part // 2

        def step(i, carry):
            here = pl.ds(i * some, some)
            there = pl.ds(c * part + i * some, some)
            rows = some * block_x
            sides = [r[there].reshape(rows, block_y) for r in (from_left, from_right)]
            for q in range(QUADS):
                wide = jnp.concatenate(
                    [along[c % slots, here, q].reshape(rows, block_y)] + sides, axis=1
                )
                found = jnp.dot(wide, y_band[q], preferred_element_type=jnp.float32)
                term = send_c[c % slots, here, q].reshape(rows, block_y).astype(jnp.float32)
                send_c[c % slots, here, q] = (
                    (found - tikhonov * term).astype(bf).reshape(some, block_x, block_y)
                )
            return carry

        lax.fori_loop(0, 2, step, 0)

    x_first = x_halo(weighted, (first_rest, last_rest), xs, xr)
    y_first = y_halo((from_left, from_right), ys, yr)
    load_u = [local(whole(weighted, c), send_a.at[c % slots], 0, c) for c in range(parts)]
    load_p = [local(whole(plain, c), send_c.at[c % slots], 1, c) for c in range(parts)]
    store_one = [local(send_c.at[c % slots], whole(section_one, c), 2, c) for c in range(parts)]
    for c in range(parts):
        halo_start(x_first, c)
    for c in range(slots):
        load_u[c].start()
        load_p[c].start()
    for there, ref in zip(
        has + has[:2], (low, high, from_left, from_right, low_rest, high_rest)
    ):

        @pl.when(jnp.logical_not(there))
        def _():
            ref[...] = jnp.zeros_like(ref)

    eigen_copies = [
        remote(rows_x, all_x.at[me_x], es.at[step], er.at[step],
               (lax.rem(me_x + step, size_x), me_y))
        for step in range(1, size_x)
    ]
    for copy in eigen_copies:
        copy.start()
    all_x[me_x] = rows_x[...]
    for b in range(0, full, block_y):
        x_fwd[pl.ds(b, block_y), :] = x_inv[:, pl.ds(b, block_y)].astype(jnp.float32).T.astype(bf)

    ahead = 3
    for c in range(parts + 1):
        if c < parts:
            load_u[c].wait()
            halo_landed(x_first, c)
            if c >= slots:
                halo_sent(y_first, c - slots)
            blur_x(send_a, x_back, c)
            halo_start(y_first, c)
            if c + slots < parts:
                load_u[c + slots].start()
        if c > 0:
            halo_landed(y_first, c - 1)
            load_p[c - 1].wait()
            blur_y(c - 1)
            store_one[c - 1].start()
            store_one[c - 1].wait()
            if c - 1 < ahead:
                start("f", c - 1)
            if c - 1 + slots < parts:
                load_p[c - 1 + slots].start()
    for c in range(parts):
        halo_sent(x_first, c)
        if c >= parts - slots:
            halo_sent(y_first, c)

    for copy in eigen_copies:
        copy.wait()
    row = all_x[me_y // halves, lax.rem(me_y, halves)][:1]
    column = jnp.broadcast_to(row, (share, share)).T
    for b in range(0, full_y, share):
        eigen_xy[:, pl.ds(b, share)] = column * rows_y[:1, pl.ds(b, share)]
    for step in range(parts + 2):
        c = step
        if c < parts:
            landed("f", c)
            if c + ahead < parts:
                start("f", c + ahead)
            if c >= slots:
                sent("g", c - slots)
            along_x(x_fwd, lines_x, send_a, c)
            start("g", c)
        c = step - 1
        if 0 <= c < parts:
            landed("g", c)
            if c >= slots:
                sent("h", c - slots)
            along_y(c)
            start("h", c)
        c = step - 2
        if 0 <= c < parts:
            landed("h", c)
            if c >= slots:
                sent("b", c - slots)
            along_x(x_inv, lines_back, send_c, c)
            start("b", c)
    for c in range(parts):
        sent("f", c)
        if c >= parts - slots:
            sent("g", c)
            sent("h", c)

    x_last = x_halo(section_six, (found_rest.at[0], found_rest.at[1]), us, ur)
    y_last = y_halo((left_out, right_out), vs, vr)
    load_s = [local(whole(section_six, c), send_a.at[c % slots], 3, c) for c in range(parts)]
    store_a = [local(along.at[c % slots], whole(spread_out, c), 4, c) for c in range(parts)]
    empty = [
        pltpu.make_async_copy(ref, out, loads.at[5, n])
        for n, (ref, out) in enumerate(((from_left, left_out), (from_right, right_out)))
    ]
    for there, copy in zip(has[2:], empty):

        @pl.when(jnp.logical_not(there))
        def _():
            copy.start()

    for c in range(parts + 1):
        if c < parts:
            if c >= parts - slots:
                sent("b", c)
            landed("b", c)
            load_s[c].start()
            load_s[c].wait()
            pack_rest(send_a, c)
            halo_start(x_last, c)
        if c > 0:
            d = c - 1
            halo_landed(x_last, d)
            if d >= slots:
                halo_sent(y_last, d - slots)
                store_a[d - slots].wait()
            blur_x(send_a, x_band, d)
            halo_start(y_last, d)
            store_a[d].start()
    for c in range(parts):
        halo_landed(y_last, c)
        halo_sent(x_last, c)
        if c >= parts - slots:
            halo_sent(y_last, c)
            store_a[c].wait()
    for there, copy in zip(has[2:], empty):

        @pl.when(jnp.logical_not(there))
        def _():
            copy.wait()


def transform(
    weighted, plain, first_rest, last_rest,
    x_back, x_band, y_back, rim_select, x_inv, y_fwd, rows_x, rows_y, eigen_z,
    size_x, size_y,
):
    depth, quads, block_x, block_y = weighted.shape
    full_x, full_y = x_inv.shape[0], y_fwd.shape[0]
    share = full_x // size_y
    parts = PARTS
    part = depth // parts
    slots = 2
    vmem = pl.BlockSpec(memory_space=pltpu.VMEM)
    hbm = pl.BlockSpec(memory_space=pl.ANY)
    sem = lambda n: pltpu.SemaphoreType.DMA((parts, n))
    one = pltpu.SemaphoreType.DMA((parts,))
    bf = jnp.bfloat16
    modes = jax.ShapeDtypeStruct(weighted.shape, bf)
    side = jax.ShapeDtypeStruct((depth, block_x, block_y), bf)
    chunk = pltpu.VMEM((slots, part, quads, block_x, block_y), bf)
    edge = pltpu.VMEM((depth, quads, NEAR, block_y), bf)
    rest = pltpu.VMEM((depth, quads * REST, block_y), bf)
    return pl.pallas_call(
        functools.partial(transform_kernel, parts, size_x, size_y),
        out_shape=[modes, modes, modes, side, side],
        in_specs=[hbm] * 4 + [vmem] * 8 + [pl.BlockSpec(memory_space=pltpu.SMEM)],
        out_specs=[hbm] * 5,
        scratch_shapes=[
            pltpu.VMEM((depth, full_x, block_y), bf),
            pltpu.VMEM((depth, share, full_y), bf),
            pltpu.VMEM((depth, full_x, block_y), bf),
            chunk,
            pltpu.VMEM((slots, part, share, full_y), bf),
            chunk,
            pltpu.VMEM((2 * share, full_y), bf),
            chunk,
            edge, edge, rest, rest,
            pltpu.VMEM((2, depth, quads * REST, block_y), bf),
            pltpu.VMEM((slots, 2, part, block_x, block_y), bf),
            pltpu.VMEM(side.shape, bf), pltpu.VMEM(side.shape, bf),
            pltpu.VMEM((full_x, full_x), bf),
            pltpu.VMEM((share, full_y), jnp.float32),
            pltpu.VMEM((size_x,) + rows_x.shape, jnp.float32),
            sem(size_x), sem(size_x), sem(size_y), sem(size_y),
            sem(size_y), sem(size_y), sem(size_x), sem(size_x),
            one, one, one, one,
            sem(4), sem(4), sem(2), sem(2), sem(4), sem(4), sem(2), sem(2),
            pltpu.SemaphoreType.DMA((6, parts)),
            pltpu.SemaphoreType.DMA((size_x,)), pltpu.SemaphoreType.DMA((size_x,)),
        ],
        compiler_params=pltpu.CompilerParams(
            collective_id=0, has_side_effects=True, vmem_limit_bytes=62 * 2**20
        ),
    )(
        weighted, plain, first_rest, last_rest,
        x_back, x_band, y_back, rim_select, x_inv, y_fwd, rows_x, rows_y, eigen_z,
    )


def blur_x_lines(lines, low, high, band, along, to_right, to_left, rim_select):
    half = lines[0].shape[1]
    for q in range(0, len(lines), 2):
        both = jnp.concatenate(
            [jnp.concatenate([low[p], lines[p], high[p]], axis=0) for p in (q, q + 1)], axis=1
        )
        found = jnp.dot(band[...], both, preferred_element_type=jnp.float32).astype(jnp.bfloat16)
        along[q] = found[:, :half]
        along[q + 1] = found[:, half:]
    pack_rims([along[q] for q in range(len(lines))], to_right, to_left, rim_select)


def pack_rims(lines, to_right, to_left, rim_select):
    half = lines[0].shape[1]
    found = jnp.dot(
        jnp.concatenate(lines, axis=1), rim_select[...], preferred_element_type=jnp.float32
    ).astype(jnp.bfloat16)
    to_left[...] = found[:, half:]
    to_right[...] = found[:, :half]


BAND_ROWS = 16
QUADS = 4
RIM_ROWS = 32
NEAR = 16
REST = HALF + SHIFT - NEAR
SIXES = 6


def to_modes_kernel(matrix, source, first, second, held):
    rows, depth = source.shape[0], source.shape[2]
    for x in range(0, rows, 2):
        lines = source[pl.ds(x, 2)].reshape(2 * source.shape[1], depth).astype(jnp.bfloat16)
        found = lax.dot_general(
            matrix[...], lines, (((1,), (1,)), ((), ())), preferred_element_type=jnp.float32
        )
        held[:, x, :] = found[:, : source.shape[1]]
        held[:, x + 1, :] = found[:, source.shape[1] :]
    full = depth // SIXES
    first[:full] = held[: full * SIXES].reshape((full,) + first.shape[1:]).astype(first.dtype)
    left = depth - full * SIXES
    first[full, :left] = held[full * SIXES : depth].astype(first.dtype)
    first[full, left:] = jnp.zeros((SIXES - left,) + first.shape[2:], first.dtype)
    groups = second.shape[0]
    for q in range(QUADS):
        second[:, q] = held[pl.ds(depth + q * groups, groups)].astype(second.dtype)


def modes_block(rows, shape):
    return pl.BlockSpec((shape[0], shape[1], rows, shape[3]), lambda i: (0, 0, i, 0))


def space_block(rows, shape):
    return pl.BlockSpec((rows, shape[1], shape[2]), lambda i: (i, 0, 0))


def whole_block(shape):
    return pl.BlockSpec(shape, lambda i: (0,) * len(shape))


def to_modes(source, matrix):
    block_x, block_y, depth = source.shape
    shapes = [
        (depth // SIXES + 1, SIXES, block_x, block_y), (depth // QUADS, QUADS, block_x, block_y)
    ]
    return pl.pallas_call(
        to_modes_kernel,
        grid=(block_x // BAND_ROWS,),
        out_shape=[jax.ShapeDtypeStruct(shape, jnp.bfloat16) for shape in shapes],
        in_specs=[whole_block(matrix.shape), space_block(BAND_ROWS, source.shape)],
        out_specs=[modes_block(BAND_ROWS, shape) for shape in shapes],
        scratch_shapes=[pltpu.VMEM((2 * depth, BAND_ROWS, block_y), jnp.float32)],
        compiler_params=pltpu.CompilerParams(vmem_limit_bytes=60 * 2**20),
    )(matrix, source)


def spread_kernel(
    size_x, size_y, parts, source, x_band, rim_select, along, from_left, from_right,
    low, high, right, left, xs, xr, ys, yr,
):
    me_x = lax.axis_index("gx")
    me_y = lax.axis_index("gy")
    block_x = source.shape[2]
    groups = source.shape[0]
    part = groups // parts
    has = (me_x > 0, me_x < size_x - 1, me_y > 0, me_y < size_y - 1)
    peers = ((me_x - 1, me_y), (me_x + 1, me_y), (me_x, me_y - 1), (me_x, me_y + 1))

    barrier = pltpu.get_barrier_semaphore()
    for peer in (
        (lax.rem(me_x + 1, size_x), me_y), (lax.rem(me_x + size_x - 1, size_x), me_y),
        (me_x, lax.rem(me_y + 1, size_y)), (me_x, lax.rem(me_y + size_y - 1, size_y)),
    ):
        pl.semaphore_signal(barrier, inc=1, device_id=peer, device_id_type=MESH_ID)
    pl.semaphore_wait(barrier, 4)

    def x_copy(c, way):
        here = pl.ds(c * part, part)
        if way == 0:
            src, dst = source.at[here, :, pl.ds(0, RIM_ROWS)], high.at[here]
        else:
            src = source.at[here, :, pl.ds(block_x - RIM_ROWS, RIM_ROWS)]
            dst = low.at[here]
        return pltpu.make_async_remote_copy(
            src, dst, xs.at[c, way], xr.at[c, way], device_id=peers[way], device_id_type=MESH_ID
        )

    def y_copy(c, way):
        here = pl.ds(c * part, part)
        if way == 0:
            src, dst = left.at[here], from_right.at[here]
        else:
            src, dst = right.at[here], from_left.at[here]
        return pltpu.make_async_remote_copy(
            src, dst, ys.at[c, way], yr.at[c, way], device_id=peers[2 + way],
            device_id_type=MESH_ID,
        )

    for c in range(parts):
        for way in range(2):

            @pl.when(has[way])
            def _():
                x_copy(c, way).start()

    for there, ref in zip(has, (low, high, from_left, from_right)):

        @pl.when(jnp.logical_not(there))
        def _():
            ref[...] = jnp.zeros_like(ref)

    def blur_x(c):
        def step(i, carry):
            g = c * part + i
            blur_x_lines(
                [source[g, q] for q in range(source.shape[1])], low.at[g], high.at[g], x_band,
                along.at[g], right.at[g], left.at[g], rim_select,
            )
            return carry

        lax.fori_loop(0, part, step, 0)

    for c in range(parts):
        for way in range(2):

            @pl.when(has[1 - way])
            def _():
                x_copy(c, way).wait_recv()

        blur_x(c)
        for way in range(2):

            @pl.when(has[2 + way])
            def _():
                y_copy(c, way).start()

    for c in range(parts):
        for way in range(2):

            @pl.when(has[3 - way])
            def _():
                y_copy(c, way).wait_recv()

            @pl.when(has[way])
            def _():
                x_copy(c, way).wait_send()

            @pl.when(has[2 + way])
            def _():
                y_copy(c, way).wait_send()


def spread(source, x_band, rim_select, size_x, size_y, number):
    groups, quads, block_x, block_y = source.shape
    bf = jnp.bfloat16
    whole = jax.ShapeDtypeStruct(source.shape, bf)
    rims = jax.ShapeDtypeStruct((groups, block_x, block_y), bf)
    vmem = pl.BlockSpec(memory_space=pltpu.VMEM)
    edge = pltpu.VMEM((groups, quads, RIM_ROWS, block_y), bf)
    packed = pltpu.VMEM(rims.shape, bf)
    sem = pltpu.SemaphoreType.DMA((groups // 2, 2))
    return pl.pallas_call(
        functools.partial(spread_kernel, size_x, size_y, groups // 2),
        out_shape=[whole, rims, rims],
        in_specs=[vmem] * 3,
        out_specs=[vmem] * 3,
        scratch_shapes=[edge, edge, packed, packed, sem, sem, sem, sem],
        compiler_params=pltpu.CompilerParams(
            collective_id=number, has_side_effects=True, vmem_limit_bytes=56 * 2**20
        ),
    )(source, x_band, rim_select)


def blur_y_rows(along, from_left, from_right, y_band, put):
    groups, quads, rows, block_y = along.shape
    count = groups * rows
    sides = [from_left[...].reshape(count, block_y), from_right[...].reshape(count, block_y)]
    for q in range(quads):
        wide = jnp.concatenate([along[:, q].reshape(count, block_y)] + sides, axis=1)
        found = jnp.dot(wide, y_band[q], preferred_element_type=jnp.float32)
        put(q, found.reshape(groups, rows, block_y))


def misfit_kernel(
    along, from_left, from_right, observed, confidence, y_band, matrix,
    misfit, weighted, first_rest, last_rest, held, turned_back,
):
    def put(s, found):
        for r in range(found.shape[0]):
            held[r * SIXES + s] = found[r]

    blur_y_rows(along, from_left, from_right, y_band, put)
    depth = observed.shape[2]
    for x in range(observed.shape[0]):
        found = observed[x].astype(jnp.float32) - held[:depth, x, :].T
        misfit[x] = found
        lines = (confidence[x].astype(jnp.float32) * found).astype(jnp.bfloat16)
        turned_back[:, x, :] = lax.dot_general(
            matrix[...], lines, (((1,), (1,)), ((), ())), preferred_element_type=jnp.float32
        )
    groups = weighted.shape[0]
    for q in range(QUADS):
        weighted[:, q] = turned_back[pl.ds(q * groups, groups)].astype(weighted.dtype)

    def rest(row):
        return jnp.concatenate(
            [turned_back[pl.ds(q * groups, groups), pl.ds(row, REST)] for q in range(QUADS)],
            axis=1,
        ).astype(weighted.dtype)

    @pl.when(pl.program_id(0) == 1)
    def _():
        first_rest[...] = rest(0)

    @pl.when(pl.program_id(0) == pl.num_programs(0) - 2)
    def _():
        last_rest[...] = rest(BAND_ROWS - REST)


def find_misfit(along, from_left, from_right, observed, confidence, y_band, matrix):
    shape, space = along.shape, observed.shape
    modes = (space[2] // QUADS, QUADS, shape[2], shape[3])
    rest = (modes[0], QUADS * REST, shape[3])
    rims = pl.BlockSpec((shape[0], BAND_ROWS, shape[3]), lambda i: (0, i, 0))
    held = pltpu.VMEM((shape[0] * SIXES, BAND_ROWS, shape[3]), jnp.float32)
    turned = pltpu.VMEM((space[2], BAND_ROWS, shape[3]), jnp.float32)
    return pl.pallas_call(
        misfit_kernel,
        grid=(shape[2] // BAND_ROWS,),
        out_shape=[
            jax.ShapeDtypeStruct(space, jnp.float32),
            jax.ShapeDtypeStruct(modes, jnp.bfloat16),
            jax.ShapeDtypeStruct(rest, jnp.bfloat16),
            jax.ShapeDtypeStruct(rest, jnp.bfloat16),
        ],
        in_specs=[
            modes_block(BAND_ROWS, shape), rims, rims,
            space_block(BAND_ROWS, space), space_block(BAND_ROWS, space),
            whole_block(y_band.shape), whole_block(matrix.shape),
        ],
        out_specs=[
            space_block(BAND_ROWS, space), modes_block(BAND_ROWS, modes),
            whole_block(rest), whole_block(rest),
        ],
        scratch_shapes=[held, turned],
        compiler_params=pltpu.CompilerParams(vmem_limit_bytes=60 * 2**20),
    )(along, from_left, from_right, observed, confidence, y_band, matrix)


def folded(values):
    return jnp.sum(values.reshape(-1, 8, values.shape[-1]), axis=0)


def direction_kernel(
    along, from_left, from_right, section_six, section_one, confidence, y_band, basis, blurring,
    direction, blurred, sums, held, held_six,
):
    @pl.when(pl.program_id(0) == 0)
    def _():
        sums[...] = jnp.zeros_like(sums)

    def put(q, found):
        held[pl.ds(q * found.shape[0], found.shape[0])] = found

    blur_y_rows(along, from_left, from_right, y_band, put)
    six = section_six[...].astype(jnp.float32)
    sums[0] += folded((six * section_one[...].astype(jnp.float32)).reshape(-1, six.shape[-1]))
    groups = six.shape[0]
    for q in range(QUADS):
        held_six[pl.ds(q * groups, groups)] = six[:, q]
    for x in range(confidence.shape[0]):
        lines = held_six[:, x, :].T.astype(jnp.bfloat16)
        found = jnp.dot(lines, basis[...], preferred_element_type=jnp.float32)
        direction[x] = found
        sums[2] += folded(found * found)
        lines = held[:, x, :].T.astype(jnp.bfloat16)
        found = jnp.dot(
            jnp.concatenate([lines, lines], axis=1), blurring[...],
            preferred_element_type=jnp.float32,
        )
        blurred[x] = found
        sums[1] += folded(confidence[x].astype(jnp.float32) * found * found)


def find_direction(
    along, from_left, from_right, section_six, section_one, confidence, y_band, basis, blurring
):
    shape, space = along.shape, confidence.shape
    rims = pl.BlockSpec((shape[0], BAND_ROWS, shape[3]), lambda i: (0, i, 0))
    held = pltpu.VMEM((space[2], BAND_ROWS, shape[3]), jnp.float32)
    sums = (8, 8, space[2])
    return pl.pallas_call(
        direction_kernel,
        grid=(shape[2] // BAND_ROWS,),
        out_shape=[
            jax.ShapeDtypeStruct(space, jnp.float32),
            jax.ShapeDtypeStruct(space, jnp.float32),
            jax.ShapeDtypeStruct(sums, jnp.float32),
        ],
        in_specs=[
            modes_block(BAND_ROWS, shape), rims, rims,
            modes_block(BAND_ROWS, shape), modes_block(BAND_ROWS, shape),
            space_block(BAND_ROWS, space),
            whole_block(y_band.shape), whole_block(basis.shape), whole_block(blurring.shape),
        ],
        out_specs=[
            space_block(BAND_ROWS, space), space_block(BAND_ROWS, space), whole_block(sums),
        ],
        scratch_shapes=[held, held],
        compiler_params=pltpu.CompilerParams(vmem_limit_bytes=60 * 2**20),
    )(
        along, from_left, from_right, section_six, section_one, confidence, y_band, basis, blurring
    )


def total_kernel(size_x, size_y, values, total, from_x, from_y, held, sx, rx, sy, ry):
    me_x = lax.axis_index("gx")
    me_y = lax.axis_index("gy")
    x_peers = [(lax.rem(me_x + s, size_x), me_y) for s in range(1, size_x)]
    y_peers = [(me_x, lax.rem(me_y + s, size_y)) for s in range(1, size_y)]
    barrier = pltpu.get_barrier_semaphore()
    for peer in x_peers + y_peers:
        pl.semaphore_signal(barrier, inc=1, device_id=peer, device_id_type=MESH_ID)
    pl.semaphore_wait(barrier, size_x + size_y - 2)

    def gather(source, landing, peers, sends, receives):
        copies = [
            pltpu.make_async_remote_copy(
                source, landing.at[s], sends.at[s], receives.at[s],
                device_id=peer, device_id_type=MESH_ID,
            )
            for s, peer in enumerate(peers)
        ]
        for copy in copies:
            copy.start()
        for copy in copies:
            copy.wait()
        return source[...] + jnp.sum(landing[...], axis=0)

    held[...] = jnp.sum(values[...], axis=1)
    held[...] = gather(held, from_x, x_peers, sx, rx)
    total[...] = gather(held, from_y, y_peers, sy, ry)


def total_sums(sums, size_x, size_y, number):
    lanes = sums.shape[2]
    vmem = pl.BlockSpec(memory_space=pltpu.VMEM)
    sem = lambda n: pltpu.SemaphoreType.DMA((n - 1,))
    f32 = jnp.float32
    return pl.pallas_call(
        functools.partial(total_kernel, size_x, size_y),
        out_shape=jax.ShapeDtypeStruct((8, lanes), f32),
        in_specs=[vmem],
        out_specs=vmem,
        scratch_shapes=[
            pltpu.VMEM((size_x - 1, 8, lanes), f32),
            pltpu.VMEM((size_y - 1, 8, lanes), f32),
            pltpu.VMEM((8, lanes), f32),
            sem(size_x), sem(size_x), sem(size_y), sem(size_y),
        ],
        compiler_params=pltpu.CompilerParams(collective_id=number, has_side_effects=True),
    )(sums)


def x_bands(kernel, offset, block_x):
    rim = HALF + SHIFT
    band = band_matrix(kernel, offset, block_x, block_x + 2 * rim, rim)
    stacks = []
    for q in range(QUADS):
        pads = ((0, 0), (q * REST, (QUADS - 1 - q) * REST))
        stacks.append(
            jnp.concatenate(
                [
                    band[:, REST:rim], jnp.pad(band[:, :REST], pads), band[:, rim:-rim],
                    band[:, -rim:-REST], jnp.pad(band[:, -REST:], pads),
                ],
                axis=1,
            )
        )
    return jnp.stack(stacks).astype(jnp.bfloat16)


def y_bands(kernel, offset, block_y, count):
    rim = HALF + SHIFT
    band = band_matrix(kernel, offset, block_y, block_y + 2 * rim, rim).T
    stacks = []
    for q in range(count):
        before = q * (block_y // count)
        pads = ((before, block_y - before - rim), (0, 0))
        stacks.append(
            jnp.concatenate(
                [band[rim:-rim], jnp.pad(band[:rim], pads), jnp.pad(band[-rim:], pads)], axis=0
            )
        )
    return jnp.stack(stacks).astype(jnp.bfloat16)


def rim_selects(block_y, count):
    rim = HALF + SHIFT
    row = lax.broadcasted_iota(jnp.int32, (count * block_y, block_y), 0)
    lane = lax.broadcasted_iota(jnp.int32, (count * block_y, block_y), 1)
    width = block_y // count
    same = row // block_y == lane // width
    place = lane % width
    within = jnp.logical_and(same, place < rim)
    spot = row % block_y
    right = jnp.logical_and(within, spot == block_y - rim + place)
    left = jnp.logical_and(within, spot == place)
    return jnp.concatenate([right, left], axis=1).astype(jnp.bfloat16)


def kernel_shards(
    observed, confidence, iterate, kernel_bank, tap_index, offsets,
    basis_x, basis_y, basis_z, eigen_x, eigen_y, eigen_z,
):
    size_x, size_y = lax.axis_size("gx"), lax.axis_size("gy")
    block_x, block_y, depth = iterate.shape
    bf = jnp.bfloat16
    kernels = kernels_of(kernel_bank, tap_index)
    adjoint = kernels[:, ::-1]
    full_x = lax.all_gather(basis_x, "gx", axis=0, tiled=True)
    full_y = lax.all_gather(basis_y, "gy", axis=0, tiled=True)
    share_x = block_x * size_x // size_y
    rows_x = jnp.broadcast_to(eigen_x.reshape(-1, 1, share_x), (block_x // share_x, 8, share_x))
    rows_y = jnp.broadcast_to(eigen_y[None, :], (8, eigen_y.shape[0]))
    wide_x = block_x + 2 * RIM_ROWS
    x_band = band_matrix(kernels[0], offsets[0], block_x, wide_x, RIM_ROWS).astype(bf)
    x_bands_back = x_bands(adjoint[0], -offsets[0], block_x)
    x_bands_on = x_bands(kernels[0], offsets[0], block_x)
    y_first = y_bands(kernels[1], offsets[1], block_y, SIXES)
    y_band = y_bands(kernels[1], offsets[1], block_y, QUADS)
    y_back = y_bands(adjoint[1], -offsets[1], block_y, QUADS)
    z_band = band_matrix(kernels[2], offsets[2], depth, depth, 0)
    rim_select = rim_selects(block_y, QUADS)
    basis_f = basis_z.astype(jnp.float32)
    blurring = jnp.dot(z_band, basis_f, precision=highest)
    entry = jnp.concatenate([z_band.astype(bf), basis_z.T], axis=0)

    along_z, plain = to_modes(iterate, entry)
    rims = spread(along_z, x_band, rim_selects(block_y, SIXES), size_x, size_y, 1)
    misfit, weighted, *rests = find_misfit(
        *rims, observed, confidence, y_first, blurring.T.astype(bf)
    )
    section_one, section_six, *rims = transform(
        weighted, plain, *rests, x_bands_back, x_bands_on, y_back, rim_select, full_x, full_y,
        rows_x, rows_y, eigen_z, size_x, size_y,
    )
    coarse = blurring.T.astype(bf)
    fine = (blurring.T - coarse.astype(jnp.float32)).astype(bf)
    direction, blurred, sums = find_direction(
        *rims, section_six, section_one, confidence, y_band, basis_z.T,
        jnp.concatenate([coarse, fine], axis=0),
    )
    totals = jnp.sum(total_sums(sums, size_x, size_y, 2), axis=1)
    step_size = totals[0] / (totals[1] + tikhonov * totals[2])
    return (iterate + step_size * direction, misfit - step_size * blurred)


def kernels_fit(block, size_x, size_y):
    block_x, block_y, depth = block
    return (
        block_y == 128
        and depth == 128
        and block_x == 256
        and depth // size_x == 32
        and block_x * size_x // size_y == 128
        and block_y * size_y % 256 == 0
    )


def step_shards(*arrays):
    fits = kernels_fit(arrays[2].shape, lax.axis_size("gx"), lax.axis_size("gy"))
    return (kernel_shards if fits else shards)(*arrays)


def solution(mesh):
    return jax.shard_map(
        step_shards,
        mesh=mesh,
        in_specs=(
            P("gx", "gy", None),
            P("gx", "gy", None),
            P("gx", "gy", None),
            P(),
            P(),
            P(),
            P("gx", None),
            P("gy", None),
            P(),
            P("gx"),
            P(),
            P(),
        ),
        out_specs=(P("gx", "gy", None), P("gx", "gy", None)),
        check_vma=False,
    )
```
